256 devices in a mesh: seq: 32 (over z_hi, x, core), fsdp: 8 (over z_lo, y).
Axes of the slice: x: 4, y: 4, z: 8 (z_hi: 4, z_lo: 2; z = z_hi * 2 + z_lo), core: 2. Of those that a mesh axis runs over, the one named last changes fastest.
Arguments:
- prompt: bfloat16 [8, 256, 4096], P('fsdp'), may hold values from -6 to 6
- lengths: int32 [8], P('fsdp'), may hold values from 1 to 256, 1152 in all
- timesteps: int32 [8], P('fsdp'), may hold values from 0 to 999
- ref_errors: float32 [8, 2], P('fsdp'), may hold values from 4.2 to 4.45
- gain_ffn: float32 [4096], replicated, may hold values from 0.5 to 1.5
- w_in_gate: bfloat16 [4096, 8192], P('fsdp', 'seq'), may hold values from -0.09375 to 0.09375
- w_in_up: bfloat16 [4096, 8192], P('fsdp', 'seq'), may hold values from -0.09375 to 0.09375
- w_in_down: bfloat16 [8192, 4096], P('seq', 'fsdp'), may hold values from -0.0625 to 0.0625
- gain_final: float32 [4096], replicated, may hold values from 0.5 to 1.5
- w_context: bfloat16 [4096, 4096], P('fsdp', 'seq'), may hold values from -0.09375 to 0.09375
- image_q: bfloat16 [8, 2, 2048, 2048], P('fsdp', None, 'seq'), may hold values from -128 to 128
- image_k: bfloat16 [8, 2, 2048, 2048], P('fsdp', None, 'seq'), may hold values from -4 to 4
- image_v: bfloat16 [8, 2, 2048, 2048], P('fsdp', None, 'seq'), may hold values from -6 to 6
- w_out: bfloat16 [2048, 1280], P('fsdp'), may hold values from -0.125 to 0.125
- target: bfloat16 [8, 2, 2048, 1280], P('fsdp', None, 'seq'), may hold values from -12 to 12
Outputs:
- pair_loss: float32 [8], P('fsdp')
- grad_q: bfloat16 [8, 2, 2048, 2048], P('fsdp', None, None, 'seq')
- grad_k: bfloat16 [8, 2, 2048, 2048], P('fsdp', None, None, 'seq')
- grad_v: bfloat16 [8, 2, 2048, 2048], P('fsdp', None, None, 'seq')
The draws below stay inside these ranges and needn't reach their ends.
All inputs are finite; a program needn't handle non-finite values. No bound on the sum of `lengths` on one device may be relied on, other than what follows from the above.
Results may differ from the reference program's by a relative error of at most 0.029.
Values may be sent and summed in bfloat16 or wider, within the bound.
A program may use at most 128 MiB of HBM per device.

```python
import math
import jax
import jax.numpy as jnp
import numpy as np
from jax import lax

D_ENC = 4096
FF = 8192
PROMPT = 256
HEAD = 64
CH = 1280
SEQ = 2048
HEADS = 32
INNER = 2048
PAIRS = 8


def attention_draw(key):
    base_key = jax.random.fold_in(key, 7)
    key_query, key_keys = jax.random.split(base_key, 2)
    full_shape = (PAIRS, 2, SEQ, INNER)
    key_vals = jnp.clip(jax.random.normal(key_keys, full_shape, jnp.float32), -4.0, 4.0)
    query_vals = 1.5 * jnp.clip(jax.random.normal(key_query, full_shape, jnp.float32), -4.0, 4.0)
    return (query_vals, key_vals)


def draw_image_q(key, part):
    return attention_draw(key)[0].astype(jnp.bfloat16)


def draw_image_k(key, part):
    return attention_draw(key)[1].astype(jnp.bfloat16)


def draw_target(key, part):
    base_key = jax.random.fold_in(key, 11)
    key_noise = jax.random.fold_in(base_key, 0)
    position_ramp = 1.0 + 2.0 * jnp.arange(SEQ, dtype=jnp.float32) / (SEQ - 1)
    noise_vals = jnp.clip(jax.random.normal(key_noise, (PAIRS, 2, SEQ, CH), jnp.float32), -4.0, 4.0)
    return (noise_vals * position_ramp[None, None, :, None]).astype(jnp.bfloat16)


def place_ends(values, own_key, least, largest):
    dims = values.shape
    place = [jax.random.randint(jax.random.fold_in(own_key, axis), (), 0, dims[axis]) for axis in range(len(dims))]
    values = values.at[tuple(place)].set(least)
    longest = dims.index(max(dims))
    place[longest] = (place[longest] + 1) % dims[longest]
    return values.at[tuple(place)].set(largest)


def level_of(rng, extent, cuts, smallest, largest):
    def one(position, blocks):
        heights = jax.random.uniform(jax.random.fold_in(jax.random.fold_in(rng, 6), position), (blocks,), jnp.float32, smallest / len(cuts), largest / len(cuts))
        return jnp.repeat(jnp.exp(heights), extent[position] // blocks).reshape((-1,) + (1,) * (len(extent) - position - 1))

    level = one(*cuts[0])
    for cut in cuts[1:]:
        level = level * one(*cut)
    return level


def split_up(count, total, most, skew):
    weights = [(1 << 20) // math.isqrt(standing ** skew) + 1 for standing in range(2, count + 1)]
    rest, counts = total - most - (count - 1), [1] * (count - 1)
    while rest > 0:
        movable = [i for i in range(count - 1) if counts[i] < most]
        pool, left = sum([weights[i] for i in movable]), rest
        for i in movable:
            more = min(most - counts[i], max(1, left * weights[i] // pool), rest)
            counts[i] = counts[i] + more
            rest = rest - more
    return np.array([most] + counts)


def uneven(key, count, total, limit, slope):
    if count == 2:
        one = jax.random.randint(key, (), max(1, total - limit), min(limit, total - 1) + 1)
        return jnp.stack([one, total - one])
    sizes = jnp.asarray(split_up(count, total, limit, slope), jnp.int32)
    twos = (count - 1) // 2
    donor, taker = sizes[1:1 + 2 * twos:2], sizes[2:2 + 2 * twos:2]
    slack = jnp.minimum(donor - 1, limit - taker)
    moved = jax.random.randint(jax.random.fold_in(key, 1), (twos,), 0, 1 << 20) % (slack + 1)
    sizes = sizes.at[1:1 + 2 * twos:2].set(donor - moved).at[2:2 + 2 * twos:2].set(taker + moved)
    return sizes[jax.random.permutation(jax.random.fold_in(key, 2), count)]


def scatter_about(own_key, shape, width, most, cuts=(), kind=jnp.bfloat16):
    drawn = width * jax.random.normal(own_key, shape, jnp.float32)
    if cuts:
        drawn = drawn * level_of(own_key, shape, cuts, -0.22, 0.18)
    return jnp.clip(drawn, -most, most).astype(kind)


def setup_inputs(seed: int = 0) -> dict:
    key_of = jax.random.split(jax.random.key(seed), 16)
    prompt = scatter_about(key_of[0], (PAIRS, PROMPT, D_ENC), 1.0, 6.0, ((0, 8),))
    lengths = uneven(key_of[1], PAIRS, PROMPT * (PAIRS + 1) // 2, PROMPT, 0).astype(jnp.int32)
    timesteps = place_ends(jax.random.randint(key_of[2], (PAIRS,), 0, 1000), jax.random.fold_in(key_of[2], 1), 0, 999).astype(jnp.int32)
    ref_errors = jnp.clip(4.2 + 0.25 * jax.random.uniform(key_of[3], (PAIRS, 2), jnp.float32) ** level_of(key_of[3], (PAIRS, 2), ((0, 8),), -0.2, 0.2), 4.2, 4.45)
    gain_ffn = jnp.clip(1.0 + 0.1 * jax.random.normal(key_of[4], (D_ENC,), jnp.float32), 0.5, 1.5)
    w_in_gate = scatter_about(key_of[5], (D_ENC, FF), D_ENC ** -0.5, 0.09375, ((0, 8), (1, 32)))
    w_in_up = scatter_about(key_of[6], (D_ENC, FF), D_ENC ** -0.5, 0.09375, ((0, 8), (1, 32)))
    w_in_down = scatter_about(key_of[7], (FF, D_ENC), FF ** -0.5, 0.0625, ((0, 32), (1, 8)))
    gain_final = jnp.clip(1.0 + 0.1 * jax.random.normal(key_of[8], (D_ENC,), jnp.float32), 0.5, 1.5)
    w_context = scatter_about(key_of[9], (D_ENC, 2 * INNER), D_ENC ** -0.5, 0.09375, ((0, 8), (1, 32)))
    image_q = draw_image_q(jax.random.fold_in(key_of[15], 71), 0)
    image_k = draw_image_k(jax.random.fold_in(key_of[15], 71), 0)
    image_v = scatter_about(key_of[12], (PAIRS, 2, SEQ, INNER), 1.0, 6.0, ((0, 8), (2, 32)))
    w_out = scatter_about(key_of[13], (INNER, CH), INNER ** -0.5, 0.125, ((0, 8),))
    target = draw_target(jax.random.fold_in(key_of[15], 71), 0)
    return dict(prompt=prompt, lengths=lengths, timesteps=timesteps, ref_errors=ref_errors, gain_ffn=gain_ffn, w_in_gate=w_in_gate, w_in_up=w_in_up, w_in_down=w_in_down, gain_final=gain_final, w_context=w_context, image_q=image_q, image_k=image_k, image_v=image_v, w_out=w_out, target=target)


dpo_beta = 20.0
norm_eps = 1e-06

def rms_gain(values, gain):
    mean_sq = lax.optimization_barrier(jnp.mean(values * values, axis=-1, keepdims=True))
    return values * lax.rsqrt(mean_sq + norm_eps) * gain

def noise_level(step_index):
    fraction = (step_index.astype(jnp.float32) + 1.0) / 1000.0
    return 3.0 * fraction / (1.0 + 2.0 * fraction)

def softmax_rows(queries, key_rows, key_mask):
    scores = jnp.dot(queries, key_rows.T, preferred_element_type=jnp.float32) * (1.0 / math.sqrt(HEAD))
    scores = jnp.where(key_mask[None, :], scores, -jnp.inf)
    top_score = lax.optimization_barrier(jnp.max(scores, axis=-1, keepdims=True))
    weights = jnp.exp(scores - top_score)
    return (weights / lax.optimization_barrier(jnp.sum(weights, axis=-1, keepdims=True))).astype(jnp.bfloat16)

def head_forward(queries, key_rows, value_rows, key_mask):
    probs_bf = softmax_rows(queries, key_rows, key_mask)
    return jnp.dot(probs_bf, value_rows, preferred_element_type=jnp.float32).astype(jnp.bfloat16)

def head_backward(queries, key_rows, value_rows, key_mask, attended, grad_out):
    seq_len = queries.shape[0]
    probs_bf = softmax_rows(queries, key_rows, key_mask)
    grad_prob = jnp.dot(grad_out, value_rows.T, preferred_element_type=jnp.float32)
    row_delta = lax.optimization_barrier(jnp.sum(grad_out.astype(jnp.float32) * attended.astype(jnp.float32), axis=-1, keepdims=True))
    grad_score = (probs_bf.astype(jnp.float32) * (grad_prob - row_delta) * (1.0 / math.sqrt(HEAD))).astype(jnp.bfloat16)
    grad_query = jnp.dot(grad_score, key_rows, preferred_element_type=jnp.float32).astype(jnp.bfloat16)
    grad_key = jnp.dot(grad_score[:, :seq_len].T, queries, preferred_element_type=jnp.float32).astype(jnp.bfloat16)
    grad_value = jnp.dot(probs_bf[:, :seq_len].T, grad_out, preferred_element_type=jnp.float32).astype(jnp.bfloat16)
    return (grad_query, grad_key, grad_value)

def encode(prompt_rows, gain_ffn, w_in_gate, w_in_up, w_in_down, gain_final, w_context):
    prompt_f32 = prompt_rows.astype(jnp.float32)
    normed = rms_gain(prompt_f32, gain_ffn).astype(jnp.bfloat16)
    gate_act = jnp.dot(normed, w_in_gate, preferred_element_type=jnp.float32)
    up_act = jnp.dot(normed, w_in_up, preferred_element_type=jnp.float32)
    hidden = (jax.nn.gelu(gate_act, approximate=True) * up_act).astype(jnp.bfloat16)
    state = prompt_f32 + jnp.dot(hidden, w_in_down, preferred_element_type=jnp.float32)
    encoded = rms_gain(state, gain_final).astype(jnp.bfloat16)
    return jnp.dot(encoded, w_context, preferred_element_type=jnp.float32).astype(jnp.bfloat16)

def split_heads(rows):
    return jnp.transpose(rows.reshape(SEQ, HEADS, HEAD), (1, 0, 2))

def join_heads(rows):
    return jnp.transpose(rows, (1, 0, 2)).reshape(SEQ, INNER)

def reference(prompt, lengths, timesteps, ref_errors, gain_ffn, w_in_gate, w_in_up, w_in_down, gain_final, w_context, image_q, image_k, image_v, w_out, target):

    def one_pair(inputs):
        prompt_rows, length, step_index, ref_pair, pair_q, pair_k, pair_v, pair_target = inputs
        context = encode(prompt_rows, gain_ffn, w_in_gate, w_in_up, w_in_down, gain_final, w_context)
        context = context.reshape(PROMPT, HEADS, 2, HEAD)
        text_keys = jnp.transpose(context[:, :, 0, :], (1, 0, 2))
        text_values = jnp.transpose(context[:, :, 1, :], (1, 0, 2))
        key_mask = jnp.arange(SEQ + PROMPT) < SEQ + length
        head_sets = []
        attended_all = []
        residuals = []
        errors = []
        for stream in range(2):
            q_heads = split_heads(pair_q[stream])
            k_heads = jnp.concatenate([split_heads(pair_k[stream]), text_keys], axis=1)
            v_heads = jnp.concatenate([split_heads(pair_v[stream]), text_values], axis=1)

            def forward_head(head_items):
                q_one, k_one, v_one = head_items
                return head_forward(q_one, k_one, v_one, key_mask)
            head_outs = lax.map(forward_head, (q_heads, k_heads, v_heads))
            predicted = jnp.dot(join_heads(head_outs), w_out, preferred_element_type=jnp.float32)
            residual = predicted - pair_target[stream].astype(jnp.float32)
            head_sets.append((q_heads, k_heads, v_heads))
            attended_all.append(head_outs)
            residuals.append(residual)
            errors.append(jnp.mean(residual * residual))
        error_gap = errors[0] - ref_pair[0] - (errors[1] - ref_pair[1])
        sigma_t = noise_level(step_index)
        logit_value = dpo_beta * sigma_t * error_gap
        pair_loss = jax.nn.softplus(logit_value)
        coefficient = sigma_t * jax.nn.sigmoid(logit_value)
        grad_sets = []
        for stream in range(2):
            signed = coefficient if stream == 0 else -coefficient
            grad_pred = (signed * residuals[stream]).astype(jnp.bfloat16)
            grad_tok = jnp.dot(grad_pred, w_out.T, preferred_element_type=jnp.float32).astype(jnp.bfloat16)
            q_heads, k_heads, v_heads = head_sets[stream]

            def backward_head(head_items):
                q_one, k_one, v_one, out_one, grad_one = head_items
                return head_backward(q_one, k_one, v_one, key_mask, out_one, grad_one)
            grad_query, grad_key, grad_value = lax.map(backward_head, (q_heads, k_heads, v_heads, attended_all[stream], split_heads(grad_tok)))
            grad_sets.append((join_heads(grad_query), join_heads(grad_key), join_heads(grad_value)))
        grad_query = jnp.stack([grad_sets[0][0], grad_sets[1][0]])
        grad_key = jnp.stack([grad_sets[0][1], grad_sets[1][1]])
        grad_value = jnp.stack([grad_sets[0][2], grad_sets[1][2]])
        return (pair_loss, grad_query, grad_key, grad_value)
    results = lax.map(one_pair, (prompt, lengths, timesteps, ref_errors, image_q, image_k, image_v, target))
    return (results[0], results[1], results[2], results[3])
```

```python
import functools
import math

import jax
import jax.numpy as jnp
from jax import lax
from jax.experimental import pallas as pl
from jax.experimental.pallas import tpu as pltpu
from jax.sharding import PartitionSpec as P

PROMPT = 256
HEAD = 64
CH = 1280
SEQ = 2048
LANES = 128
ROWS = 256

dpo_beta = 20.0
norm_eps = 1e-06

NT = (((1,), (1,)), ((), ()))
NN = (((1,), (0,)), ((), ()))


def dot(a, b, dims=NN):
    return lax.dot_general(a, b, dims, preferred_element_type=jnp.float32)


def rms_gain(values, gain):
    mean_sq = jnp.mean(values * values, axis=-1, keepdims=True)
    return values * lax.rsqrt(mean_sq + norm_eps) * gain


def noise_level(step_index):
    fraction = (step_index.astype(jnp.float32) + 1.0) / 1000.0
    return 3.0 * fraction / (1.0 + 2.0 * fraction)


def head_lanes(j):
    lane = lax.broadcasted_iota(jnp.int32, (1, LANES), 1)
    return (lane >= j * HEAD) & (lane < (j + 1) * HEAD)


def with_ones(values):
    return jnp.concatenate([values, jnp.ones_like(values)], axis=1)


def by_head(first, second):
    return jnp.where(head_lanes(0), first, second)


def image_forward(q_ref, k_ref, v_ref, e_ref, o_ref, z_ref, m_ref):
    q = q_ref[...] * jnp.asarray(1.0 / math.sqrt(HEAD), jnp.bfloat16)
    v_aug = with_ones(v_ref[...])
    outs, tops = [], []
    for j in range(2):
        qj = jnp.where(head_lanes(j), q, jnp.zeros_like(q))
        s = dot(qj, k_ref[...], NT)
        top = jnp.max(s, axis=-1, keepdims=True)
        e = jnp.exp(s - top).astype(jnp.bfloat16)
        e_ref[j] = e
        outs.append(dot(e, v_aug))
        tops.append(top)
    o_ref[...] = by_head(outs[0][:, :LANES], outs[1][:, :LANES])
    z_ref[...] = by_head(outs[0][:, LANES:], outs[1][:, LANES:])
    m_ref[...] = by_head(tops[0], tops[1])


def text_forward(len_ref, q_ref, k_ref, v_ref, o_ref, z_ref, m_ref, att_ref, e_ref, si_ref, st_ref):
    q = q_ref[...] * jnp.asarray(1.0 / math.sqrt(HEAD), jnp.bfloat16)
    v_aug = with_ones(v_ref[...])
    kept = lax.broadcasted_iota(jnp.int32, (1, PROMPT), 1) < len_ref[0]
    outs, tops = [], []
    for j in range(2):
        qj = jnp.where(head_lanes(j), q, jnp.zeros_like(q))
        s = jnp.where(kept, dot(qj, k_ref[...], NT), -jnp.inf)
        old = m_ref[:, j * HEAD:j * HEAD + 1]
        top = jnp.maximum(old, jnp.max(s, axis=-1, keepdims=True))
        e = jnp.exp(s - top).astype(jnp.bfloat16)
        e_ref[j] = e
        outs.append(dot(e, v_aug))
        tops.append(top)
    top = by_head(tops[0], tops[1])
    alpha = jnp.exp(m_ref[...] - top)
    z = alpha * z_ref[...] + by_head(outs[0][:, LANES:], outs[1][:, LANES:])
    o = alpha * o_ref[...] + by_head(outs[0][:, :LANES], outs[1][:, :LANES])
    inv = 1.0 / z
    att_ref[...] = (o * inv).astype(jnp.bfloat16)
    si_ref[...] = alpha * inv
    st_ref[...] = inv


def backward(coef_ref, q_ref, g_ref, att_ref, ei_ref, et_ref, si_ref, st_ref, k_ref, v_ref, kt_ref, vt_ref,
             gq_ref, gk_ref, gv_ref, k_acc, v_acc):
    step = pl.program_id(0)

    @pl.when(step == 0)
    def _():
        k_acc[...] = jnp.zeros_like(k_acc)
        v_acc[...] = jnp.zeros_like(v_acc)

    coef = coef_ref[0]
    g = g_ref[...].astype(jnp.float32)
    prod = g * att_ref[...].astype(jnp.float32)
    v_aug, vt_aug = with_ones(v_ref[...]), with_ones(vt_ref[...])
    q_t = q_ref[...].T
    lane = lax.broadcasted_iota(jnp.int32, (1, LANES), 1)
    grads = []
    for j in range(2):
        mine = head_lanes(j)
        gj = jnp.where(mine, g, 0.0)
        delta = jnp.sum(jnp.where(mine, prod, 0.0), axis=-1, keepdims=True)

        def scaled(scale):
            gs = (gj * scale).astype(jnp.bfloat16)
            d = -delta * scale
            hi = d.astype(jnp.bfloat16)
            lo = (d - hi.astype(jnp.float32)).astype(jnp.bfloat16)
            extra = jnp.where(lane == 0, hi, jnp.where(lane == 1, lo, jnp.zeros_like(hi)))
            return gs, jnp.concatenate([gs, extra], axis=1)

        gi, lhs_i = scaled(si_ref[:, j * HEAD:j * HEAD + 1])
        _, lhs_t = scaled(st_ref[:, j * HEAD:j * HEAD + 1])
        ei = ei_ref[j]
        ds = (ei.astype(jnp.float32) * dot(lhs_i, v_aug, NT)).astype(jnp.bfloat16)
        ds_t = (et_ref[j].astype(jnp.float32) * dot(lhs_t, vt_aug, NT)).astype(jnp.bfloat16)
        grads.append(dot(ds, k_ref[...]) + dot(ds_t, kt_ref[...]))
        rows = slice(j * HEAD, (j + 1) * HEAD)
        k_acc[rows, :] += dot(q_t[rows, :], ds)
        v_acc[rows, :] += dot(gi.T[rows, :], ei)
    factor = coef * (1.0 / math.sqrt(HEAD))
    gq_ref[...] = (by_head(grads[0], grads[1]) * factor).T.astype(jnp.bfloat16)

    @pl.when(step == pl.num_programs(0) - 1)
    def _():
        gk_ref[...] = (k_acc[...] * factor).astype(jnp.bfloat16)
        gv_ref[...] = (v_acc[...] * coef).astype(jnp.bfloat16)


def block(shape, index_map):
    return pl.BlockSpec(shape, index_map)


def whole(*shape):
    return pl.BlockSpec(shape, lambda i: (0,) * len(shape))


def rows_of(width):
    return pl.BlockSpec((ROWS, width), lambda i: (i, 0))


def params():
    return pltpu.CompilerParams(vmem_limit_bytes=48 * 1024 * 1024)


def call_image_forward(q, k, v):
    f32 = lambda: jax.ShapeDtypeStruct((SEQ, LANES), jnp.float32)
    return pl.pallas_call(
        image_forward,
        grid=(SEQ // ROWS,),
        in_specs=[rows_of(LANES), whole(SEQ, LANES), whole(SEQ, LANES)],
        out_specs=[pl.BlockSpec((2, ROWS, SEQ), lambda i: (0, i, 0)), rows_of(LANES), rows_of(LANES), rows_of(LANES)],
        out_shape=[jax.ShapeDtypeStruct((2, SEQ, SEQ), jnp.bfloat16), f32(), f32(), f32()],
        compiler_params=params(),
        cost_estimate=pl.CostEstimate(flops=4 * 2 * SEQ * SEQ * 256, bytes_accessed=20_000_000, transcendentals=2 * SEQ * SEQ),
        name="image_forward",
    )(q, k, v)


def call_text_forward(lengths, q, k, v, o, z, m):
    f32 = lambda: jax.ShapeDtypeStruct((SEQ, LANES), jnp.float32)
    return pl.pallas_call(
        text_forward,
        grid=(SEQ // ROWS,),
        in_specs=[pl.BlockSpec(memory_space=pltpu.SMEM), rows_of(LANES), whole(PROMPT, LANES), whole(PROMPT, LANES),
                  rows_of(LANES), rows_of(LANES), rows_of(LANES)],
        out_specs=[rows_of(LANES), pl.BlockSpec((2, ROWS, PROMPT), lambda i: (0, i, 0)), rows_of(LANES), rows_of(LANES)],
        out_shape=[jax.ShapeDtypeStruct((SEQ, LANES), jnp.bfloat16), jax.ShapeDtypeStruct((2, SEQ, PROMPT), jnp.bfloat16),
                   f32(), f32()],
        compiler_params=params(),
        name="text_forward",
    )(lengths, q, k, v, o, z, m)


def call_backward(coef, q, g, att, ei, et, si, st, k, v, kt, vt):
    out = lambda: jax.ShapeDtypeStruct((LANES, SEQ), jnp.bfloat16)
    return pl.pallas_call(
        backward,
        grid=(SEQ // ROWS,),
        in_specs=[pl.BlockSpec(memory_space=pltpu.SMEM), rows_of(LANES), rows_of(LANES), rows_of(LANES),
                  pl.BlockSpec((2, ROWS, SEQ), lambda i: (0, i, 0)), pl.BlockSpec((2, ROWS, PROMPT), lambda i: (0, i, 0)),
                  rows_of(LANES), rows_of(LANES), whole(SEQ, LANES), whole(SEQ, LANES),
                  whole(PROMPT, LANES), whole(PROMPT, LANES)],
        out_specs=[pl.BlockSpec((LANES, ROWS), lambda i: (0, i)), whole(LANES, SEQ), whole(LANES, SEQ)],
        out_shape=[out(), out(), out()],
        scratch_shapes=[pltpu.VMEM((LANES, SEQ), jnp.float32), pltpu.VMEM((LANES, SEQ), jnp.float32)],
        compiler_params=params(),
        name="backward",
    )(coef, q, g, att, ei, et, si, st, k, v, kt, vt)


def to_heads(values):
    return jnp.transpose(values.reshape(2, 64, 16, LANES), (2, 0, 1, 3)).reshape(32, 64, LANES)


def exchange(values):
    return lax.all_to_all(values, "seq", split_axis=0, concat_axis=0, tiled=True)


def swap(values, pairs):
    return lax.ppermute(values, "seq", pairs)


def on_device(prompt, lengths, timesteps, ref_errors, gain_ffn, w_in_gate, w_in_up, w_in_down, gain_final, w_context,
              image_q, image_k, image_v, w_out, target):
    seat = lax.axis_index("seq")
    core = seat % 2
    pairs = [(i, i ^ 1) for i in range(32)]
    gate_full = lax.all_gather(w_in_gate, "fsdp", axis=0, tiled=True)
    up_full = lax.all_gather(w_in_up, "fsdp", axis=0, tiled=True)
    down_full = lax.all_gather(w_in_down, "fsdp", axis=1, tiled=True)
    context_full = lax.all_gather(w_context, "fsdp", axis=0, tiled=True)
    out_full = lax.all_gather(w_out, "fsdp", axis=0, tiled=True)

    sent = jnp.concatenate([to_heads(image_q[0]), to_heads(image_k[0]), to_heads(image_v[0])], axis=1)
    got = exchange(sent)
    q, k, v = (got[:, 64 * i:64 * (i + 1)].reshape(SEQ, LANES) for i in range(3))
    ei, o, z, m = call_image_forward(q, k, v)

    prompt_f32 = prompt[0].astype(jnp.float32)
    normed = rms_gain(prompt_f32, gain_ffn).astype(jnp.bfloat16)
    gate_act = dot(normed, gate_full)
    up_act = dot(normed, up_full)
    hidden = (jax.nn.gelu(gate_act, approximate=True) * up_act).astype(jnp.bfloat16)
    partial_value = dot(hidden, down_full).astype(jnp.bfloat16)
    parts = exchange(partial_value.reshape(32, 8, 4096))
    mine = lax.dynamic_slice_in_dim(prompt[0], seat * 8, 8, 0).astype(jnp.float32)
    state = mine + jnp.sum(parts.astype(jnp.float32), axis=0)
    encoded_rows = rms_gain(state, gain_final).astype(jnp.bfloat16)
    encoded = lax.all_gather(encoded_rows, "seq", axis=0, tiled=True)
    context = dot(encoded, context_full).astype(jnp.bfloat16)
    other = swap(context, pairs)
    first = jnp.where(core == 0, context, other)
    second = jnp.where(core == 0, other, context)
    kt = jnp.concatenate([first[:, :HEAD], second[:, :HEAD]], axis=1)
    vt = jnp.concatenate([first[:, HEAD:], second[:, HEAD:]], axis=1)

    att, et, si, st = call_text_forward(lengths, q, kt, vt, o, z, m)
    back = exchange(att.reshape(32, 64, LANES))
    tok = jnp.transpose(back.reshape(16, 2, 64, LANES), (1, 2, 0, 3)).reshape(LANES, SEQ)
    residual = dot(tok, out_full) - target[0].reshape(LANES, CH).astype(jnp.float32)
    err = jnp.sum((residual * residual).reshape(2, 64 * CH), axis=1)
    hi = lax.reduce_precision(err, 8, 7)
    mid = lax.reduce_precision(err - hi, 8, 7)
    low = err - hi - mid
    pieces = jnp.concatenate([hi, mid, low]).astype(jnp.bfloat16)
    grad_tok = dot(residual.astype(jnp.bfloat16), out_full, NT).astype(jnp.bfloat16)
    extra = jnp.broadcast_to(jnp.pad(pieces, (0, LANES - 6))[None, None, :], (32, 16, LANES))
    arrived = exchange(jnp.concatenate([to_heads(grad_tok), extra], axis=1))
    g = arrived[:, :64].reshape(SEQ, LANES)
    sums = jnp.sum(arrived[:, 64, :6].astype(jnp.float32).reshape(32, 3, 2), axis=(0, 1))
    mean_errors = sums / (SEQ * CH)
    error_gap = mean_errors[0] - ref_errors[0, 0] - (mean_errors[1] - ref_errors[0, 1])
    sigma_t = noise_level(timesteps[0])
    logit_value = dpo_beta * sigma_t * error_gap
    pair_loss = jax.nn.softplus(logit_value)[None]
    coefficient = sigma_t * jax.nn.sigmoid(logit_value)
    coef = jnp.where(core == 0, coefficient, -coefficient)[None]

    grads = jnp.stack(call_backward(coef, q, g, att, ei, et, si, st, k, v, kt, vt))
    halves = grads.reshape(3, 2, HEAD, SEQ)
    own = lax.dynamic_index_in_dim(halves, core, 1, keepdims=False)
    theirs = swap(lax.dynamic_index_in_dim(halves, 1 - core, 1, keepdims=False), pairs)
    outs = jnp.where(core == 0, jnp.stack([own, theirs], axis=1), jnp.stack([theirs, own], axis=1))
    outs = jnp.transpose(outs, (0, 1, 3, 2))
    return pair_loss, outs[0][None], outs[1][None], outs[2][None]


def solution(mesh):
    return jax.shard_map(
        on_device,
        mesh=mesh,
        in_specs=(
            P("fsdp", None, None),
            P("fsdp"),
            P("fsdp"),
            P("fsdp", None),
            P(),
            P("fsdp", "seq"),
            P("fsdp", "seq"),
            P("seq", "fsdp"),
            P(),
            P("fsdp", "seq"),
            P("fsdp", None, "seq", None),
            P("fsdp", None, "seq", None),
            P("fsdp", None, "seq", None),
            P("fsdp", None),
            P("fsdp", None, "seq", None),
        ),
        out_specs=(
            P("fsdp"),
            P("fsdp", None, None, "seq"),
            P("fsdp", None, None, "seq"),
            P("fsdp", None, None, "seq"),
        ),
        check_vma=False,
    )
```

```python
import functools
import math

import jax
import jax.numpy as jnp
from jax import lax
from jax.experimental import pallas as pl
from jax.experimental.pallas import tpu as pltpu
from jax.sharding import PartitionSpec as P

PROMPT = 256
HEAD = 64
CH = 1280
SEQ = 2048
LANES = 128
ROWS = 256

dpo_beta = 20.0
norm_eps = 1e-06

NT = (((1,), (1,)), ((), ()))
NN = (((1,), (0,)), ((), ()))


def dot(a, b, dims=NN):
    return lax.dot_general(a, b, dims, preferred_element_type=jnp.float32)


def noise_level(step_index):
    fraction = (step_index.astype(jnp.float32) + 1.0) / 1000.0
    return 3.0 * fraction / (1.0 + 2.0 * fraction)


def head_lanes(j):
    lane = lax.broadcasted_iota(jnp.int32, (1, LANES), 1)
    return (lane >= j * HEAD) & (lane < (j + 1) * HEAD)


def with_ones(values):
    return jnp.concatenate([values, jnp.ones_like(values)], axis=1)


def by_head(first, second):
    return jnp.where(head_lanes(0), first, second)


def image_rows(q, k, v_aug, e_ref):
    q = q * jnp.asarray(1.0 / math.sqrt(HEAD), jnp.bfloat16)
    outs, tops = [], []
    for j in range(2):
        qj = jnp.where(head_lanes(j), q, jnp.zeros_like(q))
        s = dot(qj, k, NT)
        top = jnp.max(s, axis=-1, keepdims=True)
        e = jnp.exp(s - top).astype(jnp.bfloat16)
        e_ref[j] = e
        outs.append(dot(e, v_aug))
        tops.append(top)
    return (
        by_head(outs[0][:, :LANES], outs[1][:, :LANES]),
        by_head(outs[0][:, LANES:], outs[1][:, LANES:]),
        by_head(tops[0], tops[1]),
    )


def place():
    seat, pair = lax.axis_index("seq"), lax.axis_index("fsdp")
    chip = seat // 2
    return seat, lax.rem(seat, 2), lax.rem(chip, 4), chip // 4, pair, lax.rem(pair, 4), pair // 4


def remote(src, dst, send_sem, recv_sem, seat, pair):
    return pltpu.make_async_remote_copy(
        src_ref=src, dst_ref=dst, send_sem=send_sem, recv_sem=recv_sem,
        device_id=(seat, pair), device_id_type=pl.DeviceIdType.MESH,
    )


def arrived(ref, sem):
    pltpu.make_async_copy(ref, ref, sem).wait()


def greet_seats(barrier, seat, pair):
    @pl.loop(1, 32)
    def _(d):
        pl.semaphore_signal(barrier, inc=1, device_id=(lax.rem(seat + d, 32), pair), device_id_type=pl.DeviceIdType.MESH)


def encode_and_exchange(
    prompt_ref, gain_in_ref, gain_out_ref, gate_in, up_in, down_in, ctx_in, q_in, k_in, v_in,
    q_ref, k_ref, v_ref, e_ref, o_ref, z_ref, m_ref, kt_ref, vt_ref,
    gate_buf, up_buf, down_buf, ctx_buf, normed, gate_acc, up_acc, part, sib, half, from_x, sum_x, from_z, state, ctx_pair,
    e_tile, w_local, w_send, w_recv, qkv_local, qkv_send, qkv_recv, e_sem, stage_send, stage_recv,
):
    seat, core, x, zh, pair, y, zl = place()
    other = seat + 1 - 2 * core
    up_y, down_y = lax.rem(y + 1, 4), lax.rem(y + 3, 4)
    far = lax.rem(y + 2, 4)
    base, base_p = zl * 4, (1 - zl) * 4
    partner = base_p + y

    barrier = pltpu.get_barrier_semaphore()
    greet_seats(barrier, seat, pair)
    for peer in (partner, base + up_y, base + down_y):
        pl.semaphore_signal(barrier, inc=1, device_id=(seat, peer), device_id_type=pl.DeviceIdType.MESH)
    pl.semaphore_wait(barrier, 34)

    weights = ((gate_in, gate_buf), (up_in, up_buf), (down_in, down_buf), (ctx_in, ctx_buf))

    def send_weight(w, src, dst, sem, peer):
        remote(src, dst, w_send.at[w], w_recv.at[w, sem], seat, peer).start()

    for w, (src, buf) in enumerate(weights):
        send_weight(w, src, buf.at[pair], 0, partner)
        send_weight(w, src, buf.at[pair], 1, base + up_y)
        send_weight(w, src, buf.at[pair], 2, base + down_y)
        pltpu.make_async_copy(src, buf.at[pair], w_local.at[w]).start()

    images = ((q_in, q_ref), (k_in, k_ref), (v_in, v_ref))
    here = pl.ds(pl.multiple_of(seat * 64, 64), 64)
    for i, (src, dst) in enumerate(images):

        @pl.loop(1, 32)
        def _(d, i=i, src=src, dst=dst):
            to = lax.rem(seat + d, 32)
            columns = pl.ds(pl.multiple_of((to // 2) * LANES, LANES), LANES)
            remote(src.at[lax.rem(to, 2), :, columns], dst.at[here, :], qkv_send.at[i], qkv_recv.at[i], to, pair).start()

        own = pl.ds(pl.multiple_of((seat // 2) * LANES, LANES), LANES)
        pltpu.make_async_copy(src.at[core, :, own], dst.at[here, :], qkv_local.at[i]).start()

    total = jnp.zeros((PROMPT, 1), jnp.float32)
    for f in range(8):
        rows = prompt_ref[:, 512 * f:512 * (f + 1)].astype(jnp.float32)
        total = total + jnp.sum(rows * rows, axis=-1, keepdims=True)
    inv = lax.rsqrt(total * (1.0 / 4096) + norm_eps)
    for f in range(8):
        cols = slice(512 * f, 512 * (f + 1))
        normed[f] = (prompt_ref[:, cols].astype(jnp.float32) * inv * gain_in_ref[:, cols]).astype(jnp.bfloat16)

    def first_half(buf, slot):
        return buf.at[slot, pl.ds(0, buf.shape[1] // 2)]

    def second_half(buf, slot):
        return buf.at[slot, pl.ds(buf.shape[1] // 2, buf.shape[1] // 2)]

    for w, (_, buf) in enumerate(weights):
        arrived(buf.at[partner], w_recv.at[w, 0])
        send_weight(w, buf.at[partner], buf.at[partner], 3, base + up_y)
        send_weight(w, buf.at[partner], buf.at[partner], 4, base + down_y)
        arrived(buf.at[base + down_y], w_recv.at[w, 1])
        send_weight(w, first_half(buf, base + down_y), first_half(buf, base + down_y), 5, base + up_y)
        arrived(buf.at[base + up_y], w_recv.at[w, 2])
        send_weight(w, second_half(buf, base + up_y), second_half(buf, base + up_y), 6, base + down_y)
    for w, (_, buf) in enumerate(weights):
        arrived(buf.at[base_p + down_y], w_recv.at[w, 3])
        send_weight(w, first_half(buf, base_p + down_y), first_half(buf, base_p + down_y), 7, base + up_y)
        arrived(buf.at[base_p + up_y], w_recv.at[w, 4])
        send_weight(w, second_half(buf, base_p + up_y), second_half(buf, base_p + up_y), 8, base + down_y)

    def weight_ready(w):
        buf = weights[w][1]
        arrived(first_half(buf, base + far), w_recv.at[w, 5])
        arrived(second_half(buf, base + far), w_recv.at[w, 6])
        arrived(first_half(buf, base_p + far), w_recv.at[w, 7])
        arrived(second_half(buf, base_p + far), w_recv.at[w, 8])
        pltpu.make_async_copy(weights[w][0], buf.at[pair], w_local.at[w]).wait()

    for i, (src, dst) in enumerate(images):
        arrived(dst.at[pl.ds(0, 31 * 64), :], qkv_recv.at[i])
        arrived(dst.at[pl.ds(0, 64), :], qkv_local.at[i])

    blocks = SEQ // ROWS

    def out_copy(b):
        slot = lax.rem(b, 2)
        return pltpu.make_async_copy(e_tile.at[slot], e_ref.at[:, pl.ds(pl.multiple_of(b * ROWS, ROWS), ROWS), :], e_sem.at[slot])

    @pl.loop(0, blocks)
    def _(b):
        @pl.when(b >= 2)
        def _():
            out_copy(b - 2).wait()

        rows = pl.ds(pl.multiple_of(b * ROWS, ROWS), ROWS)
        o, z, m = image_rows(q_ref[rows, :], k_ref[...], with_ones(v_ref[...]), e_tile.at[lax.rem(b, 2)])
        o_ref[rows, :], z_ref[rows, :], m_ref[rows, :] = o, z, m
        out_copy(b).start()

    weight_ready(0)
    weight_ready(1)
    gate_acc[...] = jnp.zeros_like(gate_acc)
    up_acc[...] = jnp.zeros_like(up_acc)

    @pl.loop(0, 8)
    def _(f):
        gate_acc[...] += dot(normed[f], gate_buf[f])
        up_acc[...] += dot(normed[f], up_buf[f])

    hidden = (jax.nn.gelu(gate_acc[...], approximate=True) * up_acc[...]).astype(jnp.bfloat16)
    weight_ready(2)

    def part_block(f):
        part[f] = dot(hidden, down_buf[f]).astype(jnp.bfloat16)

    @pl.loop(0, 4)
    def _(i):
        part_block((1 - core) * 4 + i)

    to_other = remote(part.at[pl.ds((1 - core) * 4, 4)], sib, stage_send.at[0], stage_recv.at[0], other, pair)
    to_other.start()

    @pl.loop(0, 4)
    def _(i):
        part_block(core * 4 + i)

    to_other.wait()
    for i in range(4):
        half[i] = (part[core * 4 + i].astype(jnp.float32) + sib[i].astype(jnp.float32)).astype(jnp.bfloat16)

    def seat_of(zh_to, x_to):
        return (zh_to * 4 + x_to) * 2 + core

    def rows_x(at):
        return pl.ds(pl.multiple_of(at * 64, 64), 64)

    def rows_z(at):
        return pl.ds(pl.multiple_of(at * 16, 16), 16)

    def round_of(stage, make):
        copies = [make(d, stage_send.at[stage + d], stage_recv.at[stage + d]) for d in (1, 2, 3)]
        for copy in copies:
            copy.start()
        for copy in copies:
            copy.wait()

    round_of(0, lambda d, s, r: remote(
        half.at[:, rows_x(lax.rem(x + d, 4)), :], from_x.at[d], s, r, seat_of(zh, lax.rem(x + d, 4)), pair))
    for i in range(4):
        acc = half[i, rows_x(x), :].astype(jnp.float32)
        for d in (1, 2, 3):
            acc = acc + from_x[d, i].astype(jnp.float32)
        sum_x[i] = acc.astype(jnp.bfloat16)
    round_of(3, lambda d, s, r: remote(
        sum_x.at[:, rows_z(lax.rem(zh + d, 4)), :], from_z.at[d], s, r, seat_of(lax.rem(zh + d, 4), x), pair))
    mine = rows_z(x * 4 + zh)
    for i in range(4):
        columns = pl.ds(pl.multiple_of(core * 2048 + i * 512, 512), 512)
        acc = prompt_ref[mine, columns].astype(jnp.float32) + sum_x[i, rows_z(zh), :].astype(jnp.float32)
        for d in (1, 2, 3):
            acc = acc + from_z[d, i].astype(jnp.float32)
        state[core * 4 + i, mine, :] = acc.astype(jnp.bfloat16)
    ours = pl.ds(core * 4, 4)
    round_of(6, lambda d, s, r: remote(
        state.at[ours, mine, :], state.at[ours, mine, :], s, r, seat_of(lax.rem(zh + d, 4), x), pair))
    round_of(9, lambda d, s, r: remote(
        state.at[ours, rows_x(x), :], state.at[ours, rows_x(x), :], s, r, seat_of(zh, lax.rem(x + d, 4)), pair))
    last = remote(state.at[ours], state.at[ours], stage_send.at[13], stage_recv.at[13], other, pair)
    last.start()
    weight_ready(3)
    last.wait()

    total = jnp.zeros((PROMPT, 1), jnp.float32)
    for f in range(8):
        rows = state[f].astype(jnp.float32)
        total = total + jnp.sum(rows * rows, axis=-1, keepdims=True)
    inv = lax.rsqrt(total * (1.0 / 4096) + norm_eps)
    context = jnp.zeros((PROMPT, LANES), jnp.float32)
    for f in range(8):
        encoded = (state[f].astype(jnp.float32) * inv * gain_out_ref[:, 512 * f:512 * (f + 1)]).astype(jnp.bfloat16)
        context = context + dot(encoded, ctx_buf[f])
    ctx_pair[core] = context.astype(jnp.bfloat16)
    give = remote(ctx_pair.at[core], ctx_pair.at[core], stage_send.at[14], stage_recv.at[14], other, pair)
    give.start()
    give.wait()
    first, second = ctx_pair[0].astype(jnp.float32), ctx_pair[1].astype(jnp.float32)
    kt_ref[...] = by_head(first, pltpu.roll(second, HEAD, 1)).astype(jnp.bfloat16)
    vt_ref[...] = by_head(pltpu.roll(first, HEAD, 1), second).astype(jnp.bfloat16)

    out_copy(blocks - 2).wait()
    out_copy(blocks - 1).wait()
    for w, (_, buf) in enumerate(weights):
        arrived(buf.at[pl.ds(0, 7)], w_send.at[w])
    for i, (_, dst) in enumerate(images):
        arrived(dst.at[pl.ds(0, 31 * 64), :], qkv_send.at[i])


def project_and_exchange(att_ref, w_ref, target_ref, g_ref, err_ref, tok, resid, grad, err_all,
                         tok_local, tok_send, tok_recv, g_local, g_send, g_recv, e_send, e_recv):
    seat, core, _, _, pair, _, _ = place()
    barrier = pltpu.get_barrier_semaphore()
    greet_seats(barrier, seat, pair)
    pl.semaphore_wait(barrier, 31)

    def token_rows(to):
        return pl.ds(pl.multiple_of(to * 64, 64), 64)

    def lanes_of(to):
        return pl.ds(pl.multiple_of((to // 2) * LANES, LANES), LANES)

    def stream_rows(to):
        return pl.ds(pl.multiple_of(lax.rem(to, 2) * 64, 64), 64)

    spot = tok.at[stream_rows(seat), lanes_of(seat)]

    @pl.loop(1, 32)
    def _(d):
        to = lax.rem(seat + d, 32)
        remote(att_ref.at[token_rows(to), :], spot, tok_send, tok_recv, to, pair).start()

    keep = pltpu.make_async_copy(att_ref.at[token_rows(seat), :], spot, tok_local)
    keep.start()
    keep.wait()
    arrived(att_ref.at[pl.ds(0, 31 * 64), :], tok_recv)

    @pl.loop(0, CH // 256)
    def _(n):
        columns = pl.ds(pl.multiple_of(n * 256, 256), 256)
        resid[:, columns] = dot(tok[...], w_ref[:, columns]) - target_ref[:, columns].astype(jnp.float32)

    halves = []
    for stream in range(2):
        rows = resid[64 * stream:64 * (stream + 1), :]
        halves.append(jnp.sum(jnp.sum(rows * rows, axis=1, keepdims=True), axis=0, keepdims=True))
    row = lax.broadcasted_iota(jnp.int32, (8, LANES), 0)
    err_all[seat] = jnp.where(row == 0, halves[0], jnp.where(row == 1, halves[1], 0.0))

    @pl.loop(1, 32)
    def _(d):
        remote(err_all.at[seat], err_all.at[seat], e_send, e_recv, lax.rem(seat + d, 32), pair).start()

    rounded = resid[...].astype(jnp.bfloat16)

    @pl.loop(0, 2048 // 256)
    def _(n):
        columns = pl.ds(pl.multiple_of(n * 256, 256), 256)
        grad[:, columns] = dot(rounded, w_ref[columns, :], NT).astype(jnp.bfloat16)

    @pl.loop(1, 32)
    def _(d):
        to = lax.rem(seat + d, 32)
        remote(grad.at[stream_rows(to), lanes_of(to)], g_ref.at[token_rows(seat), :], g_send, g_recv, to, pair).start()

    keep = pltpu.make_async_copy(grad.at[stream_rows(seat), lanes_of(seat)], g_ref.at[token_rows(seat), :], g_local)
    keep.start()
    keep.wait()
    arrived(err_all.at[pl.ds(0, 31)], e_recv)
    err_ref[...] = jnp.sum(err_all[...], axis=0)
    arrived(g_ref.at[pl.ds(0, 31 * 64), :], g_recv)
    arrived(g_ref.at[pl.ds(0, 31 * 64), :], g_send)
    arrived(att_ref.at[pl.ds(0, 31 * 64), :], tok_send)
    arrived(err_all.at[pl.ds(0, 31)], e_send)


def text_forward(len_ref, q_ref, k_ref, v_ref, o_ref, z_ref, m_ref, att_ref, e_ref, si_ref, st_ref):
    q = q_ref[...] * jnp.asarray(1.0 / math.sqrt(HEAD), jnp.bfloat16)
    v_aug = with_ones(v_ref[...])
    kept = lax.broadcasted_iota(jnp.int32, (1, PROMPT), 1) < len_ref[0]
    outs, tops = [], []
    for j in range(2):
        qj = jnp.where(head_lanes(j), q, jnp.zeros_like(q))
        s = jnp.where(kept, dot(qj, k_ref[...], NT), -jnp.inf)
        old = m_ref[:, j * HEAD:j * HEAD + 1]
        top = jnp.maximum(old, jnp.max(s, axis=-1, keepdims=True))
        e = jnp.exp(s - top).astype(jnp.bfloat16)
        e_ref[j] = e
        outs.append(dot(e, v_aug))
        tops.append(top)
    top = by_head(tops[0], tops[1])
    alpha = jnp.exp(m_ref[...] - top)
    z = alpha * z_ref[...] + by_head(outs[0][:, LANES:], outs[1][:, LANES:])
    o = alpha * o_ref[...] + by_head(outs[0][:, :LANES], outs[1][:, :LANES])
    inv = 1.0 / z
    att_ref[...] = (o * inv).astype(jnp.bfloat16)
    si_ref[...] = alpha * inv
    st_ref[...] = inv


def backward(coef_ref, q_ref, g_ref, att_ref, ei_ref, et_ref, si_ref, st_ref, k_ref, v_ref, kt_ref, vt_ref,
             gq_ref, gk_ref, gv_ref, k_acc, v_acc):
    step = pl.program_id(0)

    @pl.when(step == 0)
    def _():
        k_acc[...] = jnp.zeros_like(k_acc)
        v_acc[...] = jnp.zeros_like(v_acc)

    coef = coef_ref[0]
    g = g_ref[...].astype(jnp.float32)
    prod = g * att_ref[...].astype(jnp.float32)
    v_aug, vt_aug = with_ones(v_ref[...]), with_ones(vt_ref[...])
    q_t = q_ref[...].T
    lane = lax.broadcasted_iota(jnp.int32, (1, LANES), 1)
    grads = []
    for j in range(2):
        mine = head_lanes(j)
        gj = jnp.where(mine, g, 0.0)
        delta = jnp.sum(jnp.where(mine, prod, 0.0), axis=-1, keepdims=True)

        def scaled(scale):
            gs = (gj * scale).astype(jnp.bfloat16)
            d = -delta * scale
            hi = d.astype(jnp.bfloat16)
            lo = (d - hi.astype(jnp.float32)).astype(jnp.bfloat16)
            extra = jnp.where(lane == 0, hi, jnp.where(lane == 1, lo, jnp.zeros_like(hi)))
            return gs, jnp.concatenate([gs, extra], axis=1)

        gi, lhs_i = scaled(si_ref[:, j * HEAD:j * HEAD + 1])
        _, lhs_t = scaled(st_ref[:, j * HEAD:j * HEAD + 1])
        ei = ei_ref[j]
        ds = (ei.astype(jnp.float32) * dot(lhs_i, v_aug, NT)).astype(jnp.bfloat16)
        ds_t = (et_ref[j].astype(jnp.float32) * dot(lhs_t, vt_aug, NT)).astype(jnp.bfloat16)
        grads.append(dot(ds, k_ref[...]) + dot(ds_t, kt_ref[...]))
        rows = slice(j * HEAD, (j + 1) * HEAD)
        k_acc[rows, :] += dot(q_t[rows, :], ds)
        v_acc[rows, :] += dot(gi.T[rows, :], ei)
    factor = coef * (1.0 / math.sqrt(HEAD))
    gq_ref[...] = (by_head(grads[0], grads[1]) * factor).T.astype(jnp.bfloat16)

    @pl.when(step == pl.num_programs(0) - 1)
    def _():
        gk_ref[...] = (k_acc[...] * factor).astype(jnp.bfloat16)
        gv_ref[...] = (v_acc[...] * coef).astype(jnp.bfloat16)


def block(shape, index_map):
    return pl.BlockSpec(shape, index_map)


def whole(*shape):
    return pl.BlockSpec(shape, lambda i: (0,) * len(shape))


def rows_of(width):
    return pl.BlockSpec((ROWS, width), lambda i: (i, 0))


def params():
    return pltpu.CompilerParams(vmem_limit_bytes=48 * 1024 * 1024)


def call_encode(prompt, gain_in, gain_out, gate, up, down, ctx, q, k, v):
    bf16, f32 = jnp.bfloat16, jnp.float32
    anywhere, vmem = pl.BlockSpec(memory_space=pl.ANY), pl.BlockSpec(memory_space=pltpu.VMEM)
    shape = jax.ShapeDtypeStruct
    dma = pltpu.SemaphoreType.DMA
    return pl.pallas_call(
        encode_and_exchange,
        in_specs=[vmem] * 3 + [anywhere] * 7,
        out_specs=[vmem] * 3 + [anywhere] + [vmem] * 5,
        out_shape=[shape((SEQ, LANES), bf16)] * 3 + [shape((2, SEQ, SEQ), bf16)] + [shape((SEQ, LANES), f32)] * 3
        + [shape((PROMPT, LANES), bf16)] * 2,
        scratch_shapes=[
            pltpu.VMEM((8, 512, 256), bf16), pltpu.VMEM((8, 512, 256), bf16), pltpu.VMEM((8, 256, 512), bf16),
            pltpu.VMEM((8, 512, 128), bf16), pltpu.VMEM((8, PROMPT, 512), bf16), pltpu.VMEM((PROMPT, 256), f32),
            pltpu.VMEM((PROMPT, 256), f32), pltpu.VMEM((8, PROMPT, 512), bf16), pltpu.VMEM((4, PROMPT, 512), bf16),
            pltpu.VMEM((4, PROMPT, 512), bf16), pltpu.VMEM((4, 4, 64, 512), bf16), pltpu.VMEM((4, 64, 512), bf16),
            pltpu.VMEM((4, 4, 16, 512), bf16), pltpu.VMEM((8, PROMPT, 512), bf16), pltpu.VMEM((2, PROMPT, LANES), bf16),
            pltpu.VMEM((2, 2, ROWS, SEQ), bf16),
            dma((4,)), dma((4,)), dma((4, 9)), dma((3,)), dma((3,)), dma((3,)), dma((2,)), dma((15,)), dma((15,)),
        ],
        compiler_params=pltpu.CompilerParams(collective_id=0, has_side_effects=True, vmem_limit_bytes=56 * 1024 * 1024),
        cost_estimate=pl.CostEstimate(flops=20_000_000_000, bytes_accessed=40_000_000, transcendentals=2 * SEQ * SEQ),
        name="encode_and_exchange",
    )(prompt, gain_in, gain_out, gate, up, down, ctx, q, k, v)


def call_project(att, w_out, target):
    bf16, f32 = jnp.bfloat16, jnp.float32
    vmem = pl.BlockSpec(memory_space=pltpu.VMEM)
    shape = jax.ShapeDtypeStruct
    dma = pltpu.SemaphoreType.DMA
    return pl.pallas_call(
        project_and_exchange,
        in_specs=[vmem] * 3,
        out_specs=[vmem] * 2,
        out_shape=[shape((SEQ, LANES), bf16), shape((8, LANES), f32)],
        scratch_shapes=[
            pltpu.VMEM((LANES, 2048), bf16), pltpu.VMEM((LANES, CH), f32), pltpu.VMEM((LANES, 2048), bf16),
            pltpu.VMEM((32, 8, LANES), f32),
        ] + [dma] * 8,
        compiler_params=pltpu.CompilerParams(collective_id=1, has_side_effects=True, vmem_limit_bytes=40 * 1024 * 1024),
        name="project_and_exchange",
    )(att, w_out, target)


def call_text_forward(lengths, q, k, v, o, z, m):
    f32 = lambda: jax.ShapeDtypeStruct((SEQ, LANES), jnp.float32)
    return pl.pallas_call(
        text_forward,
        grid=(SEQ // ROWS,),
        in_specs=[pl.BlockSpec(memory_space=pltpu.SMEM), rows_of(LANES), whole(PROMPT, LANES), whole(PROMPT, LANES),
                  rows_of(LANES), rows_of(LANES), rows_of(LANES)],
        out_specs=[rows_of(LANES), pl.BlockSpec((2, ROWS, PROMPT), lambda i: (0, i, 0)), rows_of(LANES), rows_of(LANES)],
        out_shape=[jax.ShapeDtypeStruct((SEQ, LANES), jnp.bfloat16), jax.ShapeDtypeStruct((2, SEQ, PROMPT), jnp.bfloat16),
                   f32(), f32()],
        compiler_params=params(),
        name="text_forward",
    )(lengths, q, k, v, o, z, m)


def call_backward(coef, q, g, att, ei, et, si, st, k, v, kt, vt):
    out = lambda: jax.ShapeDtypeStruct((LANES, SEQ), jnp.bfloat16)
    return pl.pallas_call(
        backward,
        grid=(SEQ // ROWS,),
        in_specs=[pl.BlockSpec(memory_space=pltpu.SMEM), rows_of(LANES), rows_of(LANES), rows_of(LANES),
                  pl.BlockSpec((2, ROWS, SEQ), lambda i: (0, i, 0)), pl.BlockSpec((2, ROWS, PROMPT), lambda i: (0, i, 0)),
                  rows_of(LANES), rows_of(LANES), whole(SEQ, LANES), whole(SEQ, LANES),
                  whole(PROMPT, LANES), whole(PROMPT, LANES)],
        out_specs=[pl.BlockSpec((LANES, ROWS), lambda i: (0, i)), whole(LANES, SEQ), whole(LANES, SEQ)],
        out_shape=[out(), out(), out()],
        scratch_shapes=[pltpu.VMEM((LANES, SEQ), jnp.float32), pltpu.VMEM((LANES, SEQ), jnp.float32)],
        compiler_params=params(),
        name="backward",
    )(coef, q, g, att, ei, et, si, st, k, v, kt, vt)


def swap(values, pairs):
    return lax.ppermute(values, "seq", pairs)


def on_device(prompt, lengths, timesteps, ref_errors, gain_ffn, w_in_gate, w_in_up, w_in_down, gain_final, w_context,
              image_q, image_k, image_v, w_out, target):
    core = lax.axis_index("seq") % 2
    pairs = [(i, i ^ 1) for i in range(32)]
    out_full = lax.all_gather(w_out, "fsdp", axis=0, tiled=True)
    q, k, v, ei, o, z, m, kt, vt = call_encode(
        prompt[0], gain_ffn[None], gain_final[None], w_in_gate, w_in_up, w_in_down, w_context, image_q[0], image_k[0], image_v[0])
    att, et, si, st = call_text_forward(lengths, q, kt, vt, o, z, m)
    g, err = call_project(att, out_full, target[0].reshape(LANES, CH))
    sums = err[:2, 0]
    mean_errors = sums / (SEQ * CH)
    error_gap = mean_errors[0] - ref_errors[0, 0] - (mean_errors[1] - ref_errors[0, 1])
    sigma_t = noise_level(timesteps[0])
    logit_value = dpo_beta * sigma_t * error_gap
    pair_loss = jax.nn.softplus(logit_value)[None]
    coefficient = sigma_t * jax.nn.sigmoid(logit_value)
    coef = jnp.where(core == 0, coefficient, -coefficient)[None]

    grads = jnp.stack(call_backward(coef, q, g, att, ei, et, si, st, k, v, kt, vt))
    halves = grads.reshape(3, 2, HEAD, SEQ)
    own = lax.dynamic_index_in_dim(halves, core, 1, keepdims=False)
    theirs = swap(lax.dynamic_index_in_dim(halves, 1 - core, 1, keepdims=False), pairs)
    outs = jnp.where(core == 0, jnp.stack([own, theirs], axis=1), jnp.stack([theirs, own], axis=1))
    outs = jnp.transpose(outs, (0, 1, 3, 2))
    return pair_loss, outs[0][None], outs[1][None], outs[2][None]


def solution(mesh):
    return jax.shard_map(
        on_device,
        mesh=mesh,
        in_specs=(
            P("fsdp", None, None),
            P("fsdp"),
            P("fsdp"),
            P("fsdp", None),
            P(),
            P("fsdp", "seq"),
            P("fsdp", "seq"),
            P("seq", "fsdp"),
            P(),
            P("fsdp", "seq"),
            P("fsdp", None, "seq", None),
            P("fsdp", None, "seq", None),
            P("fsdp", None, "seq", None),
            P("fsdp", None),
            P("fsdp", None, "seq", None),
        ),
        out_specs=(
            P("fsdp"),
            P("fsdp", None, None, "seq"),
            P("fsdp", None, None, "seq"),
            P("fsdp", None, None, "seq"),
        ),
        check_vma=False,
    )
```

```python
import math

import jax
import jax.numpy as jnp
from jax import lax
from jax.experimental import pallas as pl
from jax.experimental.pallas import tpu as pltpu
from jax.sharding import PartitionSpec as P

PROMPT = 256
HEAD = 64
CH = 1280
SEQ = 2048
LANES = 128
ROWS = 256

dpo_beta = 20.0
norm_eps = 1e-06

NT = (((1,), (1,)), ((), ()))
NN = (((1,), (0,)), ((), ()))


def dot(a, b, dims=NN):
    return lax.dot_general(a, b, dims, preferred_element_type=jnp.float32)


def noise_level(step_index):
    fraction = (step_index.astype(jnp.float32) + 1.0) / 1000.0
    return 3.0 * fraction / (1.0 + 2.0 * fraction)


def head_lanes(j):
    lane = lax.broadcasted_iota(jnp.int32, (1, LANES), 1)
    return (lane >= j * HEAD) & (lane < (j + 1) * HEAD)


def with_ones(values):
    return jnp.concatenate([values, jnp.ones_like(values)], axis=1)


def by_head(first, second):
    return jnp.where(head_lanes(0), first, second)


def image_rows(q, k, v_aug, e_ref):
    q = q * jnp.asarray(1.0 / math.sqrt(HEAD), jnp.bfloat16)
    outs, tops = [], []
    for j in range(2):
        qj = jnp.where(head_lanes(j), q, jnp.zeros_like(q))
        s = dot(qj, k, NT)
        top = jnp.max(s, axis=-1, keepdims=True)
        e = jnp.exp(s - top).astype(jnp.bfloat16)
        e_ref[j] = e
        outs.append(dot(e, v_aug))
        tops.append(top)
    return (
        by_head(outs[0][:, :LANES], outs[1][:, :LANES]),
        by_head(outs[0][:, LANES:], outs[1][:, LANES:]),
        by_head(tops[0], tops[1]),
    )


def place():
    seat, pair = lax.axis_index("seq"), lax.axis_index("fsdp")
    chip = seat // 2
    return seat, lax.rem(seat, 2), lax.rem(chip, 4), chip // 4, pair, lax.rem(pair, 4), pair // 4


def remote(src, dst, send_sem, recv_sem, seat, pair):
    return pltpu.make_async_remote_copy(
        src_ref=src, dst_ref=dst, send_sem=send_sem, recv_sem=recv_sem,
        device_id=(seat, pair), device_id_type=pl.DeviceIdType.MESH,
    )


def arrived(ref, sem):
    pltpu.make_async_copy(ref, ref, sem).wait()


ALTERNATE = (1, 3, 2, 0)


def forward(
    len_ref, prompt_ref, gain_in_ref, gain_out_ref, target_ref, gate_in, up_in, down_in, ctx_in, out_in, q_in, k_in, v_in,
    q_ref, k_ref, v_ref, kt_ref, vt_ref, ei_ref, et_ref, si_ref, st_ref, att_ref, g_ref, err_ref,
    gate_buf, up_buf, down_buf, ctx_buf, out_buf, normed, gate_acc, up_acc, part, sib, half, from_x, sum_x, from_z, state,
    ctx_pair, e_tile, o_all, z_all, m_all, tok, resid, grad, err_all,
    w_local, w_send, w_recv, qkv_local, qkv_send, qkv_recv, e_sem, stage_send, stage_recv,
    tok_local, tok_send, tok_recv, g_local, g_send, g_recv, err_send, err_recv,
):
    seat, core, x, zh, pair, y, zl = place()
    other = seat + 1 - 2 * core
    low = lax.rem(seat, 8)
    up_y, down_y = lax.rem(y + 1, 4), lax.rem(y + 3, 4)
    far = lax.rem(y + 2, 4)
    base, base_p = zl * 4, (1 - zl) * 4
    partner = base_p + y

    barrier = pltpu.get_barrier_semaphore()

    @pl.loop(1, 32)
    def _(d):
        pl.semaphore_signal(barrier, inc=1, device_id=(lax.rem(seat + d, 32), pair), device_id_type=pl.DeviceIdType.MESH)

    for peer in (partner, base + up_y, base + down_y):
        pl.semaphore_signal(barrier, inc=1, device_id=(seat, peer), device_id_type=pl.DeviceIdType.MESH)
    pl.semaphore_wait(barrier, 34)

    def plain(buf):
        return lambda slot, rows=None: buf.at[slot] if rows is None else buf.at[slot, rows]

    def own_half(slot, rows=None):
        return out_buf.at[slot, core] if rows is None else out_buf.at[slot, core, rows]

    weights = (
        (gate_in, plain(gate_buf), 512), (up_in, plain(up_buf), 512), (down_in, plain(down_buf), 256),
        (ctx_in, plain(ctx_buf), 512), (out_in.at[core], own_half, 128),
    )
    early, late = (0, 1, 2), (3, 4)

    def send_weight(w, src, dst, sem, peer):
        remote(src, dst, w_send.at[w], w_recv.at[w, sem], seat, peer).start()

    def upper(w, slot):
        return weights[w][1](slot, pl.ds(0, weights[w][2] // 2))

    def lower(w, slot):
        return weights[w][1](slot, pl.ds(weights[w][2] // 2, weights[w][2] // 2))

    def send_own(w):
        src, at, _ = weights[w]
        send_weight(w, src, at(pair), 0, partner)
        send_weight(w, src, at(pair), 1, base + up_y)
        send_weight(w, src, at(pair), 2, base + down_y)
        pltpu.make_async_copy(src, at(pair), w_local.at[w]).start()

    def forward_near(w):
        at = weights[w][1]
        arrived(at(partner), w_recv.at[w, 0])
        send_weight(w, at(partner), at(partner), 3, base + up_y)
        send_weight(w, at(partner), at(partner), 4, base + down_y)
        arrived(at(base + down_y), w_recv.at[w, 1])
        send_weight(w, upper(w, base + down_y), upper(w, base + down_y), 5, base + up_y)
        arrived(at(base + up_y), w_recv.at[w, 2])
        send_weight(w, lower(w, base + up_y), lower(w, base + up_y), 6, base + down_y)

    def forward_partner(w):
        at = weights[w][1]
        arrived(at(base_p + down_y), w_recv.at[w, 3])
        send_weight(w, upper(w, base_p + down_y), upper(w, base_p + down_y), 7, base + up_y)
        arrived(at(base_p + up_y), w_recv.at[w, 4])
        send_weight(w, lower(w, base_p + up_y), lower(w, base_p + up_y), 8, base + down_y)

    def weight_ready(w):
        arrived(upper(w, base + far), w_recv.at[w, 5])
        arrived(lower(w, base + far), w_recv.at[w, 6])
        arrived(upper(w, base_p + far), w_recv.at[w, 7])
        arrived(lower(w, base_p + far), w_recv.at[w, 8])
        pltpu.make_async_copy(weights[w][0], weights[w][1](pair), w_local.at[w]).wait()

    for w in early:
        send_own(w)

    def token_rows(to):
        return pl.ds(pl.multiple_of(to * 64, 64), 64)

    def lanes_of(to):
        return pl.ds(pl.multiple_of((to // 2) * LANES, LANES), LANES)

    def stream_rows(to):
        return pl.ds(pl.multiple_of(lax.rem(to, 2) * 64, 64), 64)

    images = ((q_in, q_ref), (k_in, k_ref), (v_in, v_ref))
    for i, (src, dst) in enumerate(images):

        @pl.loop(0, 8)
        def _(j, i=i, src=src, dst=dst):
            for dz in ALTERNATE:
                to = lax.rem(zh + dz, 4) * 8 + lax.rem(low + j, 8)

                def start(to=to):
                    remote(src.at[lax.rem(to, 2), :, lanes_of(to)], dst.at[token_rows(seat), :],
                           qkv_send.at[i], qkv_recv.at[i], to, pair).start()

                if dz:
                    start()
                else:
                    pl.when(j > 0)(start)

        pltpu.make_async_copy(src.at[core, :, lanes_of(seat)], dst.at[token_rows(seat), :], qkv_local.at[i]).start()

    total = jnp.zeros((PROMPT, 1), jnp.float32)
    for f in range(8):
        rows = prompt_ref[:, 512 * f:512 * (f + 1)].astype(jnp.float32)
        total = total + jnp.sum(rows * rows, axis=-1, keepdims=True)
    inv = lax.rsqrt(total * (1.0 / 4096) + norm_eps)
    for f in range(8):
        cols = slice(512 * f, 512 * (f + 1))
        normed[f] = (prompt_ref[:, cols].astype(jnp.float32) * inv * gain_in_ref[:, cols]).astype(jnp.bfloat16)

    for w in early:
        forward_near(w)
    forward_partner(0)
    forward_partner(1)

    for i, (src, dst) in enumerate(images):
        arrived(dst.at[pl.ds(0, 31 * 64), :], qkv_recv.at[i])
        arrived(dst.at[pl.ds(0, 64), :], qkv_local.at[i])

    blocks = SEQ // ROWS

    def out_copy(b):
        slot = lax.rem(b, 2)
        return pltpu.make_async_copy(e_tile.at[slot], ei_ref.at[:, pl.ds(pl.multiple_of(b * ROWS, ROWS), ROWS), :], e_sem.at[slot])

    def image_blocks(start, stop):
        @pl.loop(start, stop)
        def _(b):
            @pl.when(b >= 2)
            def _():
                out_copy(b - 2).wait()

            rows = pl.ds(pl.multiple_of(b * ROWS, ROWS), ROWS)
            o, z, m = image_rows(q_ref[rows, :], k_ref[...], with_ones(v_ref[...]), e_tile.at[lax.rem(b, 2)])
            o_all[rows, :], z_all[rows, :], m_all[rows, :] = o, z, m
            out_copy(b).start()

    image_blocks(0, 4)
    forward_partner(2)
    for w in late:
        send_own(w)
    image_blocks(4, 8)

    weight_ready(0)
    weight_ready(1)
    gate_acc[...] = jnp.zeros_like(gate_acc)
    up_acc[...] = jnp.zeros_like(up_acc)

    @pl.loop(0, 8)
    def _(f):
        gate_acc[...] += dot(normed[f], gate_buf[f])
        up_acc[...] += dot(normed[f], up_buf[f])

    hidden = (jax.nn.gelu(gate_acc[...], approximate=True) * up_acc[...]).astype(jnp.bfloat16)
    weight_ready(2)

    def part_block(f):
        part[f] = dot(hidden, down_buf[f]).astype(jnp.bfloat16)

    @pl.loop(0, 4)
    def _(i):
        part_block((1 - core) * 4 + i)

    to_other = remote(part.at[pl.ds((1 - core) * 4, 4)], sib, stage_send.at[0], stage_recv.at[0], other, pair)
    to_other.start()

    @pl.loop(0, 4)
    def _(i):
        part_block(core * 4 + i)

    for w in late:
        forward_near(w)
    to_other.wait()
    for i in range(4):
        half[i] = (part[core * 4 + i].astype(jnp.float32) + sib[i].astype(jnp.float32)).astype(jnp.bfloat16)

    def seat_of(zh_to, x_to):
        return (zh_to * 4 + x_to) * 2 + core

    def rows_x(at):
        return pl.ds(pl.multiple_of(at * 64, 64), 64)

    def rows_z(at):
        return pl.ds(pl.multiple_of(at * 16, 16), 16)

    def round_of(stage, make, between=lambda: None):
        copies = [make(d, stage_send.at[stage + d], stage_recv.at[stage + d]) for d in (1, 3, 2)]
        for copy in copies:
            copy.start()
        between()
        for copy in copies:
            copy.wait()

    round_of(0, lambda d, s, r: remote(
        half.at[:, rows_x(lax.rem(x + d, 4)), :], from_x.at[d], s, r, seat_of(zh, lax.rem(x + d, 4)), pair))
    for i in range(4):
        acc = half[i, rows_x(x), :].astype(jnp.float32)
        for d in (1, 2, 3):
            acc = acc + from_x[d, i].astype(jnp.float32)
        sum_x[i] = acc.astype(jnp.bfloat16)
    round_of(3, lambda d, s, r: remote(
        sum_x.at[:, rows_z(lax.rem(zh + d, 4)), :], from_z.at[d], s, r, seat_of(lax.rem(zh + d, 4), x), pair))
    mine = rows_z(x * 4 + zh)
    for i in range(4):
        columns = pl.ds(pl.multiple_of(core * 2048 + i * 512, 512), 512)
        acc = prompt_ref[mine, columns].astype(jnp.float32) + sum_x[i, rows_z(zh), :].astype(jnp.float32)
        for d in (1, 2, 3):
            acc = acc + from_z[d, i].astype(jnp.float32)
        state[core * 4 + i, mine, :] = acc.astype(jnp.bfloat16)
    ours = pl.ds(core * 4, 4)
    round_of(6, lambda d, s, r: remote(
        state.at[ours, mine, :], state.at[ours, mine, :], s, r, seat_of(lax.rem(zh + d, 4), x), pair))

    def forward_late():
        for w in late:
            forward_partner(w)

    round_of(9, lambda d, s, r: remote(
        state.at[ours, rows_x(x), :], state.at[ours, rows_x(x), :], s, r, seat_of(zh, lax.rem(x + d, 4)), pair), forward_late)
    last = remote(state.at[ours], state.at[ours], stage_send.at[13], stage_recv.at[13], other, pair)
    last.start()
    weight_ready(3)
    last.wait()

    total = jnp.zeros((PROMPT, 1), jnp.float32)
    for f in range(8):
        rows = state[f].astype(jnp.float32)
        total = total + jnp.sum(rows * rows, axis=-1, keepdims=True)
    inv = lax.rsqrt(total * (1.0 / 4096) + norm_eps)
    context = jnp.zeros((PROMPT, LANES), jnp.float32)
    for f in range(8):
        encoded = (state[f].astype(jnp.float32) * inv * gain_out_ref[:, 512 * f:512 * (f + 1)]).astype(jnp.bfloat16)
        context = context + dot(encoded, ctx_buf[f])
    ctx_pair[core] = context.astype(jnp.bfloat16)
    give = remote(ctx_pair.at[core], ctx_pair.at[core], stage_send.at[14], stage_recv.at[14], other, pair)
    give.start()
    weight_ready(4)
    share = remote(out_buf.at[:, core], out_buf.at[:, core], stage_send.at[15], stage_recv.at[15], other, pair)
    share.start()
    give.wait()
    first, second = ctx_pair[0].astype(jnp.float32), ctx_pair[1].astype(jnp.float32)
    kt_ref[...] = by_head(first, pltpu.roll(second, HEAD, 1)).astype(jnp.bfloat16)
    vt_ref[...] = by_head(pltpu.roll(first, HEAD, 1), second).astype(jnp.bfloat16)

    spot = tok.at[stream_rows(seat), lanes_of(seat)]
    kept = lax.broadcasted_iota(jnp.int32, (1, PROMPT), 1) < len_ref[...]

    @pl.loop(0, 2)
    def _(part_of):
        for dz in ALTERNATE:
            b = lax.rem(zh + dz, 4) * 2 + part_of
            rows = pl.ds(pl.multiple_of(b * ROWS, ROWS), ROWS)
            att, scale_i, scale_t = text_rows(
                q_ref[rows, :], kt_ref[...], with_ones(vt_ref[...]), kept, o_all[rows, :], z_all[rows, :], m_all[rows, :],
                et_ref.at[:, rows, :])
            att_ref[rows, :], si_ref[rows, :], st_ref[rows, :] = att, scale_i, scale_t
            for t in range(4):
                to = b * 4 + t

                def start(to=to):
                    remote(att_ref.at[token_rows(to), :], spot, tok_send, tok_recv, to, pair).start()

                def keep(to=to):
                    pltpu.make_async_copy(att_ref.at[token_rows(to), :], spot, tok_local).start()

                if dz:
                    start()
                else:
                    pl.when(to != seat)(start)
                    pl.when(to == seat)(keep)

    share.wait()
    arrived(spot, tok_local)
    arrived(att_ref.at[pl.ds(0, 31 * 64), :], tok_recv)

    acc = -target_ref[...].astype(jnp.float32)
    resid[...] = acc

    @pl.loop(0, 8)
    def _(f):
        columns = pl.ds(pl.multiple_of(f * 256, 256), 256)
        resid[...] += dot(tok[:, columns], out_buf[f].reshape(256, CH))

    halves = []
    for stream in range(2):
        rows = resid[64 * stream:64 * (stream + 1), :]
        halves.append(jnp.sum(jnp.sum(rows * rows, axis=1, keepdims=True), axis=0, keepdims=True))
    row = lax.broadcasted_iota(jnp.int32, (8, LANES), 0)
    err_all[seat] = jnp.where(row == 0, halves[0], jnp.where(row == 1, halves[1], 0.0))
    rounded = resid[...].astype(jnp.bfloat16)

    @pl.loop(0, 2)
    def _(part_of):
        for dz in ALTERNATE:
            n = lax.rem(zh + dz, 4) * 2 + part_of
            columns = pl.ds(pl.multiple_of(n * 256, 256), 256)
            grad[:, columns] = dot(rounded, out_buf[n].reshape(256, CH), NT).astype(jnp.bfloat16)
            for t in range(4):
                to = n * 4 + t

                def start(to=to):
                    remote(grad.at[stream_rows(to), lanes_of(to)], g_ref.at[token_rows(seat), :], g_send, g_recv, to, pair).start()
                    remote(err_all.at[seat], err_all.at[seat], err_send, err_recv, to, pair).start()

                def keep(to=to):
                    pltpu.make_async_copy(grad.at[stream_rows(to), lanes_of(to)], g_ref.at[token_rows(seat), :], g_local).start()

                if dz:
                    start()
                else:
                    pl.when(to != seat)(start)
                    pl.when(to == seat)(keep)

    arrived(err_all.at[pl.ds(0, 31)], err_recv)
    err_ref[...] = jnp.sum(err_all[...], axis=0)
    arrived(g_ref.at[pl.ds(0, 64), :], g_local)
    arrived(g_ref.at[pl.ds(0, 31 * 64), :], g_recv)

    out_copy(blocks - 2).wait()
    out_copy(blocks - 1).wait()
    for w, buf in enumerate((gate_buf, up_buf, down_buf, ctx_buf)):
        arrived(buf.at[pl.ds(0, 7)], w_send.at[w])
    arrived(out_buf.at[pl.ds(0, 7), 0], w_send.at[4])
    for i, (_, dst) in enumerate(images):
        arrived(dst.at[pl.ds(0, 31 * 64), :], qkv_send.at[i])
    arrived(g_ref.at[pl.ds(0, 31 * 64), :], g_send)
    arrived(att_ref.at[pl.ds(0, 31 * 64), :], tok_send)
    arrived(err_all.at[pl.ds(0, 31)], err_send)


def text_rows(q, k, v_aug, kept, o, z, m, e_ref):
    q = q * jnp.asarray(1.0 / math.sqrt(HEAD), jnp.bfloat16)
    outs, tops = [], []
    for j in range(2):
        qj = jnp.where(head_lanes(j), q, jnp.zeros_like(q))
        s = jnp.where(kept, dot(qj, k, NT), -jnp.inf)
        top = jnp.maximum(m[:, j * HEAD:j * HEAD + 1], jnp.max(s, axis=-1, keepdims=True))
        e = jnp.exp(s - top).astype(jnp.bfloat16)
        e_ref[j] = e
        outs.append(dot(e, v_aug))
        tops.append(top)
    alpha = jnp.exp(m - by_head(tops[0], tops[1]))
    inv = 1.0 / (alpha * z + by_head(outs[0][:, LANES:], outs[1][:, LANES:]))
    o = alpha * o + by_head(outs[0][:, :LANES], outs[1][:, :LANES])
    return (o * inv).astype(jnp.bfloat16), alpha * inv, inv


def backward(coef_ref, q_ref, g_ref, att_ref, ei_ref, et_ref, si_ref, st_ref, k_ref, v_ref, kt_ref, vt_ref,
             gq_ref, gk_ref, gv_ref, k_acc, v_acc):
    step = pl.program_id(0)

    @pl.when(step == 0)
    def _():
        k_acc[...] = jnp.zeros_like(k_acc)
        v_acc[...] = jnp.zeros_like(v_acc)

    coef = coef_ref[0]
    g = g_ref[...].astype(jnp.float32)
    prod = g * att_ref[...].astype(jnp.float32)
    v_aug, vt_aug = with_ones(v_ref[...]), with_ones(vt_ref[...])
    q_t = q_ref[...].T
    lane = lax.broadcasted_iota(jnp.int32, (1, LANES), 1)
    grads = []
    for j in range(2):
        mine = head_lanes(j)
        gj = jnp.where(mine, g, 0.0)
        delta = jnp.sum(jnp.where(mine, prod, 0.0), axis=-1, keepdims=True)

        def scaled(scale):
            gs = (gj * scale).astype(jnp.bfloat16)
            d = -delta * scale
            hi = d.astype(jnp.bfloat16)
            lo = (d - hi.astype(jnp.float32)).astype(jnp.bfloat16)
            extra = jnp.where(lane == 0, hi, jnp.where(lane == 1, lo, jnp.zeros_like(hi)))
            return gs, jnp.concatenate([gs, extra], axis=1)

        gi, lhs_i = scaled(si_ref[:, j * HEAD:j * HEAD + 1])
        _, lhs_t = scaled(st_ref[:, j * HEAD:j * HEAD + 1])
        ei = ei_ref[j]
        ds = (ei.astype(jnp.float32) * dot(lhs_i, v_aug, NT)).astype(jnp.bfloat16)
        ds_t = (et_ref[j].astype(jnp.float32) * dot(lhs_t, vt_aug, NT)).astype(jnp.bfloat16)
        grads.append(dot(ds, k_ref[...]) + dot(ds_t, kt_ref[...]))
        rows = slice(j * HEAD, (j + 1) * HEAD)
        k_acc[rows, :] += dot(q_t[rows, :], ds)
        v_acc[rows, :] += dot(gi.T[rows, :], ei)
    factor = coef * (1.0 / math.sqrt(HEAD))
    gq_ref[...] = (by_head(grads[0], grads[1]) * factor).T.astype(jnp.bfloat16)

    @pl.when(step == pl.num_programs(0) - 1)
    def _():
        gk_ref[...] = (k_acc[...] * factor).astype(jnp.bfloat16)
        gv_ref[...] = (v_acc[...] * coef).astype(jnp.bfloat16)


def block(shape, index_map):
    return pl.BlockSpec(shape, index_map)


def whole(*shape):
    return pl.BlockSpec(shape, lambda i: (0,) * len(shape))


def rows_of(width):
    return pl.BlockSpec((ROWS, width), lambda i: (i, 0))


def params():
    return pltpu.CompilerParams(vmem_limit_bytes=48 * 1024 * 1024)


def call_forward(lengths, prompt, gain_in, gain_out, target, gate, up, down, ctx, out, q, k, v):
    bf16, f32 = jnp.bfloat16, jnp.float32
    anywhere, vmem = pl.BlockSpec(memory_space=pl.ANY), pl.BlockSpec(memory_space=pltpu.VMEM)
    shape = jax.ShapeDtypeStruct
    dma, buf = pltpu.SemaphoreType.DMA, pltpu.VMEM
    rows_bf16, rows_f32 = shape((SEQ, LANES), bf16), shape((SEQ, LANES), f32)
    text = shape((PROMPT, LANES), bf16)
    return pl.pallas_call(
        forward,
        in_specs=[vmem] * 5 + [anywhere] * 8,
        out_specs=[vmem] * 5 + [anywhere] + [vmem] * 6,
        out_shape=[rows_bf16] * 3 + [text] * 2 + [shape((2, SEQ, SEQ), bf16), shape((2, SEQ, PROMPT), bf16)]
        + [rows_f32] * 2 + [rows_bf16] * 2 + [shape((8, LANES), f32)],
        scratch_shapes=[
            buf((8, 512, 256), bf16), buf((8, 512, 256), bf16), buf((8, 256, 512), bf16), buf((8, 512, 128), bf16),
            buf((8, 2, 128, CH), bf16),
            buf((8, PROMPT, 512), bf16), buf((PROMPT, 256), f32), buf((PROMPT, 256), f32),
            buf((8, PROMPT, 512), bf16), buf((4, PROMPT, 512), bf16), buf((4, PROMPT, 512), bf16),
            buf((4, 4, 64, 512), bf16), buf((4, 64, 512), bf16), buf((4, 4, 16, 512), bf16),
            buf((8, PROMPT, 512), bf16), buf((2, PROMPT, LANES), bf16), buf((2, 2, ROWS, SEQ), bf16),
            buf((SEQ, LANES), f32), buf((SEQ, LANES), f32), buf((SEQ, LANES), f32),
            buf((LANES, 2048), bf16), buf((LANES, CH), f32), buf((LANES, 2048), bf16), buf((32, 8, LANES), f32),
            dma((5,)), dma((5,)), dma((5, 9)), dma((3,)), dma((3,)), dma((3,)), dma((2,)), dma((16,)), dma((16,)),
        ] + [dma] * 8,
        compiler_params=pltpu.CompilerParams(collective_id=0, has_side_effects=True, vmem_limit_bytes=60 * 1024 * 1024),
        name="forward",
    )(lengths, prompt, gain_in, gain_out, target, gate, up, down, ctx, out, q, k, v)


def call_backward(coef, q, g, att, ei, et, si, st, k, v, kt, vt):
    out = lambda: jax.ShapeDtypeStruct((LANES, SEQ), jnp.bfloat16)
    return pl.pallas_call(
        backward,
        grid=(SEQ // ROWS,),
        in_specs=[pl.BlockSpec(memory_space=pltpu.SMEM), rows_of(LANES), rows_of(LANES), rows_of(LANES),
                  pl.BlockSpec((2, ROWS, SEQ), lambda i: (0, i, 0)), pl.BlockSpec((2, ROWS, PROMPT), lambda i: (0, i, 0)),
                  rows_of(LANES), rows_of(LANES), whole(SEQ, LANES), whole(SEQ, LANES),
                  whole(PROMPT, LANES), whole(PROMPT, LANES)],
        out_specs=[pl.BlockSpec((LANES, ROWS), lambda i: (0, i)), whole(LANES, SEQ), whole(LANES, SEQ)],
        out_shape=[out(), out(), out()],
        scratch_shapes=[pltpu.VMEM((LANES, SEQ), jnp.float32), pltpu.VMEM((LANES, SEQ), jnp.float32)],
        compiler_params=params(),
        name="backward",
    )(coef, q, g, att, ei, et, si, st, k, v, kt, vt)


def swap(values, pairs):
    return lax.ppermute(values, "seq", pairs)


def on_device(prompt, lengths, timesteps, ref_errors, gain_ffn, w_in_gate, w_in_up, w_in_down, gain_final, w_context,
              image_q, image_k, image_v, w_out, target):
    core = lax.axis_index("seq") % 2
    pairs = [(i, i ^ 1) for i in range(32)]
    q, k, v, kt, vt, ei, et, si, st, att, g, err = call_forward(
        jnp.broadcast_to(lengths[:, None], (1, PROMPT)), prompt[0], gain_ffn[None], gain_final[None],
        target[0].reshape(LANES, CH), w_in_gate, w_in_up, w_in_down, w_context, w_out.reshape(2, 128, CH),
        image_q[0], image_k[0], image_v[0])
    sums = err[:2, 0]
    mean_errors = sums / (SEQ * CH)
    error_gap = mean_errors[0] - ref_errors[0, 0] - (mean_errors[1] - ref_errors[0, 1])
    sigma_t = noise_level(timesteps[0])
    logit_value = dpo_beta * sigma_t * error_gap
    pair_loss = jax.nn.softplus(logit_value)[None]
    coefficient = sigma_t * jax.nn.sigmoid(logit_value)
    coef = jnp.where(core == 0, coefficient, -coefficient)[None]

    grads = jnp.stack(call_backward(coef, q, g, att, ei, et, si, st, k, v, kt, vt))
    halves = grads.reshape(3, 2, HEAD, SEQ)
    own = lax.dynamic_index_in_dim(halves, core, 1, keepdims=False)
    theirs = swap(lax.dynamic_index_in_dim(halves, 1 - core, 1, keepdims=False), pairs)
    outs = jnp.where(core == 0, jnp.stack([own, theirs], axis=1), jnp.stack([theirs, own], axis=1))
    outs = jnp.transpose(outs, (0, 1, 3, 2))
    return pair_loss, outs[0][None], outs[1][None], outs[2][None]


def solution(mesh):
    return jax.shard_map(
        on_device,
        mesh=mesh,
        in_specs=(
            P("fsdp", None, None),
            P("fsdp"),
            P("fsdp"),
            P("fsdp", None),
            P(),
            P("fsdp", "seq"),
            P("fsdp", "seq"),
            P("seq", "fsdp"),
            P(),
            P("fsdp", "seq"),
            P("fsdp", None, "seq", None),
            P("fsdp", None, "seq", None),
            P("fsdp", None, "seq", None),
            P("fsdp", None),
            P("fsdp", None, "seq", None),
        ),
        out_specs=(
            P("fsdp"),
            P("fsdp", None, None, "seq"),
            P("fsdp", None, None, "seq"),
            P("fsdp", None, None, "seq"),
        ),
        check_vma=False,
    )
```

```python
import math

import jax
import jax.numpy as jnp
from jax import lax
from jax.experimental import pallas as pl
from jax.experimental.pallas import tpu as pltpu
from jax.sharding import PartitionSpec as P

PROMPT = 256
HEAD = 64
CH = 1280
SEQ = 2048
LANES = 128
ROWS = 256

dpo_beta = 20.0
norm_eps = 1e-06

NT = (((1,), (1,)), ((), ()))
NN = (((1,), (0,)), ((), ()))


def dot(a, b, dims=NN):
    return lax.dot_general(a, b, dims, preferred_element_type=jnp.float32)


def noise_level(step_index):
    fraction = (step_index.astype(jnp.float32) + 1.0) / 1000.0
    return 3.0 * fraction / (1.0 + 2.0 * fraction)


def head_lanes(j):
    lane = lax.broadcasted_iota(jnp.int32, (1, LANES), 1)
    return (lane >= j * HEAD) & (lane < (j + 1) * HEAD)


def with_ones(values):
    return jnp.concatenate([values, jnp.ones_like(values)], axis=1)


def by_head(first, second):
    return jnp.where(head_lanes(0), first, second)


def image_rows(q, k, v_aug, e_ref):
    q = q * jnp.asarray(1.0 / math.sqrt(HEAD), jnp.bfloat16)
    outs, tops = [], []
    for j in range(2):
        qj = jnp.where(head_lanes(j), q, jnp.zeros_like(q))
        s = dot(qj, k, NT)
        top = jnp.max(s, axis=-1, keepdims=True)
        e = jnp.exp(s - top).astype(jnp.bfloat16)
        e_ref[j] = e
        outs.append(dot(e, v_aug))
        tops.append(top)
    return (
        by_head(outs[0][:, :LANES], outs[1][:, :LANES]),
        by_head(outs[0][:, LANES:], outs[1][:, LANES:]),
        by_head(tops[0], tops[1]),
    )


def place():
    seat, pair = lax.axis_index("seq"), lax.axis_index("fsdp")
    chip = seat // 2
    return seat, lax.rem(seat, 2), lax.rem(chip, 4), chip // 4, pair, lax.rem(pair, 4), pair // 4


def remote(src, dst, send_sem, recv_sem, seat, pair):
    return pltpu.make_async_remote_copy(
        src_ref=src, dst_ref=dst, send_sem=send_sem, recv_sem=recv_sem,
        device_id=(seat, pair), device_id_type=pl.DeviceIdType.MESH,
    )


def arrived(ref, sem):
    pltpu.make_async_copy(ref, ref, sem).wait()


ALTERNATE = (1, 3, 2, 0)


def window(
    len_ref, scalar_ref, prompt_ref, gain_in_ref, gain_out_ref, target_ref, gate_in, up_in, down_in, ctx_in, out_in, q_in, k_in, v_in,
    loss_ref, gq_ref, gk_ref, gv_ref, ei_ref,
    gate_buf, up_buf, down_buf, ctx_buf, out_buf, normed, gate_acc, up_acc, part, sib, half, from_x, sum_x, from_z, state,
    ctx_pair, e_tile, o_all, z_all, m_all, tok, resid, grad, err_all,
    q_ref, k_ref, v_ref, kt_ref, vt_ref, et_ref, si_ref, st_ref, att_ref, g_ref, k_acc, v_acc, give_q, give_k, give_v,
    w_local, w_send, w_recv, qkv_local, qkv_send, qkv_recv, e_sem, stage_send, stage_recv, swap_send, swap_recv, g_recv,
    tok_local, tok_send, tok_recv, g_local, g_send, err_send, err_recv,
):
    seat, core, x, zh, pair, y, zl = place()
    other = seat + 1 - 2 * core
    low = lax.rem(seat, 8)
    up_y, down_y = lax.rem(y + 1, 4), lax.rem(y + 3, 4)
    far = lax.rem(y + 2, 4)
    base, base_p = zl * 4, (1 - zl) * 4
    partner = base_p + y

    barrier = pltpu.get_barrier_semaphore()

    @pl.loop(1, 32)
    def _(d):
        pl.semaphore_signal(barrier, inc=1, device_id=(lax.rem(seat + d, 32), pair), device_id_type=pl.DeviceIdType.MESH)

    for peer in (partner, base + up_y, base + down_y):
        pl.semaphore_signal(barrier, inc=1, device_id=(seat, peer), device_id_type=pl.DeviceIdType.MESH)
    pl.semaphore_wait(barrier, 34)

    def plain(buf):
        return lambda slot, rows=None: buf.at[slot] if rows is None else buf.at[slot, rows]

    def own_half(slot, rows=None):
        return out_buf.at[slot, core] if rows is None else out_buf.at[slot, core, rows]

    weights = (
        (gate_in, plain(gate_buf), 512), (up_in, plain(up_buf), 512), (down_in, plain(down_buf), 256),
        (ctx_in, plain(ctx_buf), 512), (out_in.at[core], own_half, 128),
    )
    early, late = (0, 1, 2), (3, 4)

    def send_weight(w, src, dst, sem, peer):
        remote(src, dst, w_send.at[w], w_recv.at[w, sem], seat, peer).start()

    def upper(w, slot):
        return weights[w][1](slot, pl.ds(0, weights[w][2] // 2))

    def lower(w, slot):
        return weights[w][1](slot, pl.ds(weights[w][2] // 2, weights[w][2] // 2))

    def send_own(w):
        src, at, _ = weights[w]
        send_weight(w, src, at(pair), 0, partner)
        send_weight(w, src, at(pair), 1, base + up_y)
        send_weight(w, src, at(pair), 2, base + down_y)
        pltpu.make_async_copy(src, at(pair), w_local.at[w]).start()

    def forward_near(w):
        at = weights[w][1]
        arrived(at(partner), w_recv.at[w, 0])
        send_weight(w, at(partner), at(partner), 3, base + up_y)
        send_weight(w, at(partner), at(partner), 4, base + down_y)
        arrived(at(base + down_y), w_recv.at[w, 1])
        send_weight(w, upper(w, base + down_y), upper(w, base + down_y), 5, base + up_y)
        arrived(at(base + up_y), w_recv.at[w, 2])
        send_weight(w, lower(w, base + up_y), lower(w, base + up_y), 6, base + down_y)

    def forward_partner(w):
        at = weights[w][1]
        arrived(at(base_p + down_y), w_recv.at[w, 3])
        send_weight(w, upper(w, base_p + down_y), upper(w, base_p + down_y), 7, base + up_y)
        arrived(at(base_p + up_y), w_recv.at[w, 4])
        send_weight(w, lower(w, base_p + up_y), lower(w, base_p + up_y), 8, base + down_y)

    def weight_ready(w):
        arrived(upper(w, base + far), w_recv.at[w, 5])
        arrived(lower(w, base + far), w_recv.at[w, 6])
        arrived(upper(w, base_p + far), w_recv.at[w, 7])
        arrived(lower(w, base_p + far), w_recv.at[w, 8])
        pltpu.make_async_copy(weights[w][0], weights[w][1](pair), w_local.at[w]).wait()

    for w in early:
        send_own(w)

    def token_rows(to):
        return pl.ds(pl.multiple_of(to * 64, 64), 64)

    def lanes_of(to):
        return pl.ds(pl.multiple_of((to // 2) * LANES, LANES), LANES)

    def stream_rows(to):
        return pl.ds(pl.multiple_of(lax.rem(to, 2) * 64, 64), 64)

    images = ((q_in, q_ref), (k_in, k_ref), (v_in, v_ref))
    for i, (src, dst) in enumerate(images):

        @pl.loop(0, 8)
        def _(j, i=i, src=src, dst=dst):
            for dz in ALTERNATE:
                to = lax.rem(zh + dz, 4) * 8 + lax.rem(low + j, 8)

                def start(to=to):
                    remote(src.at[lax.rem(to, 2), :, lanes_of(to)], dst.at[token_rows(seat), :],
                           qkv_send.at[i], qkv_recv.at[i], to, pair).start()

                if dz:
                    start()
                else:
                    pl.when(j > 0)(start)

        pltpu.make_async_copy(src.at[core, :, lanes_of(seat)], dst.at[token_rows(seat), :], qkv_local.at[i]).start()

    total = jnp.zeros((PROMPT, 1), jnp.float32)
    for f in range(8):
        rows = prompt_ref[:, 512 * f:512 * (f + 1)].astype(jnp.float32)
        total = total + jnp.sum(rows * rows, axis=-1, keepdims=True)
    inv = lax.rsqrt(total * (1.0 / 4096) + norm_eps)
    for f in range(8):
        cols = slice(512 * f, 512 * (f + 1))
        normed[f] = (prompt_ref[:, cols].astype(jnp.float32) * inv * gain_in_ref[:, cols]).astype(jnp.bfloat16)

    for w in early:
        forward_near(w)
    forward_partner(0)
    forward_partner(1)

    for i, (src, dst) in enumerate(images):
        arrived(dst.at[pl.ds(0, 31 * 64), :], qkv_recv.at[i])
        arrived(dst.at[pl.ds(0, 64), :], qkv_local.at[i])

    blocks = SEQ // ROWS

    def out_copy(b):
        slot = lax.rem(b, 2)
        return pltpu.make_async_copy(e_tile.at[slot], ei_ref.at[:, pl.ds(pl.multiple_of(b * ROWS, ROWS), ROWS), :], e_sem.at[slot])

    def image_blocks(start, stop):
        @pl.loop(start, stop)
        def _(b):
            @pl.when(b >= 2)
            def _():
                out_copy(b - 2).wait()

            rows = pl.ds(pl.multiple_of(b * ROWS, ROWS), ROWS)
            o, z, m = image_rows(q_ref[rows, :], k_ref[...], with_ones(v_ref[...]), e_tile.at[lax.rem(b, 2)])
            o_all[rows, :], z_all[rows, :], m_all[rows, :] = o, z, m
            out_copy(b).start()

    image_blocks(0, 4)
    forward_partner(2)
    for w in late:
        send_own(w)
    image_blocks(4, 8)

    weight_ready(0)
    weight_ready(1)
    gate_acc[...] = jnp.zeros_like(gate_acc)
    up_acc[...] = jnp.zeros_like(up_acc)

    @pl.loop(0, 8)
    def _(f):
        gate_acc[...] += dot(normed[f], gate_buf[f])
        up_acc[...] += dot(normed[f], up_buf[f])

    hidden = (jax.nn.gelu(gate_acc[...], approximate=True) * up_acc[...]).astype(jnp.bfloat16)
    weight_ready(2)

    def part_block(f):
        part[f] = dot(hidden, down_buf[f]).astype(jnp.bfloat16)

    @pl.loop(0, 4)
    def _(i):
        part_block((1 - core) * 4 + i)

    to_other = remote(part.at[pl.ds((1 - core) * 4, 4)], sib, stage_send.at[0], stage_recv.at[0], other, pair)
    to_other.start()

    @pl.loop(0, 4)
    def _(i):
        part_block(core * 4 + i)

    for w in late:
        forward_near(w)
    to_other.wait()
    for i in range(4):
        half[i] = (part[core * 4 + i].astype(jnp.float32) + sib[i].astype(jnp.float32)).astype(jnp.bfloat16)

    def seat_of(zh_to, x_to):
        return (zh_to * 4 + x_to) * 2 + core

    def rows_x(at):
        return pl.ds(pl.multiple_of(at * 64, 64), 64)

    def rows_z(at):
        return pl.ds(pl.multiple_of(at * 16, 16), 16)

    def round_of(stage, make, between=lambda: None):
        copies = [make(d, stage_send.at[stage + d], stage_recv.at[stage + d]) for d in (1, 3, 2)]
        for copy in copies:
            copy.start()
        between()
        for copy in copies:
            copy.wait()

    round_of(0, lambda d, s, r: remote(
        half.at[:, rows_x(lax.rem(x + d, 4)), :], from_x.at[d], s, r, seat_of(zh, lax.rem(x + d, 4)), pair))
    for i in range(4):
        acc = half[i, rows_x(x), :].astype(jnp.float32)
        for d in (1, 2, 3):
            acc = acc + from_x[d, i].astype(jnp.float32)
        sum_x[i] = acc.astype(jnp.bfloat16)
    round_of(3, lambda d, s, r: remote(
        sum_x.at[:, rows_z(lax.rem(zh + d, 4)), :], from_z.at[d], s, r, seat_of(lax.rem(zh + d, 4), x), pair))
    mine = rows_z(x * 4 + zh)
    for i in range(4):
        columns = pl.ds(pl.multiple_of(core * 2048 + i * 512, 512), 512)
        acc = prompt_ref[mine, columns].astype(jnp.float32) + sum_x[i, rows_z(zh), :].astype(jnp.float32)
        for d in (1, 2, 3):
            acc = acc + from_z[d, i].astype(jnp.float32)
        state[core * 4 + i, mine, :] = acc.astype(jnp.bfloat16)
    ours = pl.ds(core * 4, 4)
    round_of(6, lambda d, s, r: remote(
        state.at[ours, mine, :], state.at[ours, mine, :], s, r, seat_of(lax.rem(zh + d, 4), x), pair))

    def forward_late():
        for w in late:
            forward_partner(w)

    round_of(9, lambda d, s, r: remote(
        state.at[ours, rows_x(x), :], state.at[ours, rows_x(x), :], s, r, seat_of(zh, lax.rem(x + d, 4)), pair), forward_late)
    last = remote(state.at[ours], state.at[ours], stage_send.at[13], stage_recv.at[13], other, pair)
    last.start()
    weight_ready(3)
    last.wait()

    total = jnp.zeros((PROMPT, 1), jnp.float32)
    for f in range(8):
        rows = state[f].astype(jnp.float32)
        total = total + jnp.sum(rows * rows, axis=-1, keepdims=True)
    inv = lax.rsqrt(total * (1.0 / 4096) + norm_eps)
    context = jnp.zeros((PROMPT, LANES), jnp.float32)
    for f in range(8):
        encoded = (state[f].astype(jnp.float32) * inv * gain_out_ref[:, 512 * f:512 * (f + 1)]).astype(jnp.bfloat16)
        context = context + dot(encoded, ctx_buf[f])
    ctx_pair[core] = context.astype(jnp.bfloat16)
    text_swap = remote(ctx_pair.at[core], ctx_pair.at[core], stage_send.at[14], stage_recv.at[14], other, pair)
    text_swap.start()
    weight_ready(4)
    share = remote(out_buf.at[:, core], out_buf.at[:, core], stage_send.at[15], stage_recv.at[15], other, pair)
    share.start()
    text_swap.wait()
    first, second = ctx_pair[0].astype(jnp.float32), ctx_pair[1].astype(jnp.float32)
    kt_ref[...] = by_head(first, pltpu.roll(second, HEAD, 1)).astype(jnp.bfloat16)
    vt_ref[...] = by_head(pltpu.roll(first, HEAD, 1), second).astype(jnp.bfloat16)

    spot = tok.at[stream_rows(seat), lanes_of(seat)]
    kept = lax.broadcasted_iota(jnp.int32, (1, PROMPT), 1) < len_ref[...]

    @pl.loop(0, 2)
    def _(part_of):
        for dz in ALTERNATE:
            b = lax.rem(zh + dz, 4) * 2 + part_of
            rows = pl.ds(pl.multiple_of(b * ROWS, ROWS), ROWS)
            att, scale_i, scale_t = text_rows(
                q_ref[rows, :], kt_ref[...], with_ones(vt_ref[...]), kept, o_all[rows, :], z_all[rows, :], m_all[rows, :],
                et_ref.at[:, rows, :])
            att_ref[rows, :], si_ref[rows, :], st_ref[rows, :] = att, scale_i, scale_t
            for t in range(4):
                to = b * 4 + t

                def start(to=to):
                    remote(att_ref.at[token_rows(to), :], spot, tok_send, tok_recv, to, pair).start()

                def keep(to=to):
                    pltpu.make_async_copy(att_ref.at[token_rows(to), :], spot, tok_local).start()

                if dz:
                    start()
                else:
                    pl.when(to != seat)(start)
                    pl.when(to == seat)(keep)

    share.wait()
    arrived(spot, tok_local)
    arrived(att_ref.at[pl.ds(0, 31 * 64), :], tok_recv)

    acc = -target_ref[...].astype(jnp.float32)
    resid[...] = acc

    @pl.loop(0, 8)
    def _(f):
        columns = pl.ds(pl.multiple_of(f * 256, 256), 256)
        resid[...] += dot(tok[:, columns], out_buf[f].reshape(256, CH))

    halves = []
    for stream in range(2):
        rows = resid[64 * stream:64 * (stream + 1), :]
        halves.append(jnp.sum(jnp.sum(rows * rows, axis=1, keepdims=True), axis=0, keepdims=True))
    row = lax.broadcasted_iota(jnp.int32, (8, LANES), 0)
    err_all[seat] = jnp.where(row == 0, halves[0], jnp.where(row == 1, halves[1], 0.0))
    rounded = resid[...].astype(jnp.bfloat16)

    @pl.loop(0, 2)
    def _(part_of):
        for dz in ALTERNATE:
            n = lax.rem(zh + dz, 4) * 2 + lax.rem(low // 4 + part_of, 2)
            columns = pl.ds(pl.multiple_of(n * 256, 256), 256)
            grad[:, columns] = dot(rounded, out_buf[n].reshape(256, CH), NT).astype(jnp.bfloat16)
            for t in range(4):
                to = n * 4 + t

                def start(to=to):
                    remote(grad.at[stream_rows(to), lanes_of(to)], g_ref.at[token_rows(seat), :], g_send, g_recv.at[seat // 4], to, pair).start()
                    remote(err_all.at[seat], err_all.at[seat], err_send, err_recv, to, pair).start()

                def keep(to=to):
                    pltpu.make_async_copy(grad.at[stream_rows(to), lanes_of(to)], g_ref.at[token_rows(seat), :], g_local).start()

                if dz:
                    start()
                else:
                    pl.when(to != seat)(start)
                    pl.when(to == seat)(keep)

    def order(i):
        r = lax.rem(i, 4)
        return lax.rem(zh + lax.rem(1 + 2 * r + r // 2, 4), 4) * 2 + lax.rem(low // 4 + i // 4, 2)

    def in_copy(i):
        slot = lax.rem(i, 2)
        rows = pl.ds(pl.multiple_of(order(i) * ROWS, ROWS), ROWS)
        return pltpu.make_async_copy(ei_ref.at[:, rows, :], e_tile.at[slot], e_sem.at[slot])

    out_copy(blocks - 2).wait()
    out_copy(blocks - 1).wait()
    in_copy(0).start()
    in_copy(1).start()
    k_acc[...] = jnp.zeros_like(k_acc)
    v_acc[...] = jnp.zeros_like(v_acc)

    arrived(err_all.at[pl.ds(0, 31)], err_recv)
    mean_errors = jnp.sum(err_all[...], axis=0) * (1.0 / (SEQ * CH))
    error_gap = (mean_errors[0:1] - scalar_ref[1:2]) - (mean_errors[1:2] - scalar_ref[2:3])
    logit = dpo_beta * scalar_ref[0:1] * error_gap
    loss_ref[...] = jnp.maximum(logit, 0.0) + jnp.log1p(jnp.exp(-jnp.abs(logit)))
    coef = scalar_ref[0:1] / (1.0 + jnp.exp(-logit)) * (1 - 2 * core).astype(jnp.float32)
    factor = coef * (1.0 / math.sqrt(HEAD))
    head_rows = pl.ds(pl.multiple_of(core * HEAD, HEAD), HEAD)
    other_rows = pl.ds(pl.multiple_of((1 - core) * HEAD, HEAD), HEAD)
    arrived(g_ref.at[pl.ds(0, 64), :], g_local)

    def give(i, staged, out, cols):
        return remote(staged.at[other_rows, cols], out.at[core, :, cols], swap_send.at[i], swap_recv.at[i], other, pair)

    every = pl.ds(0, SEQ)

    @pl.loop(0, blocks)
    def _(i):
        b = order(i)
        rows = pl.ds(pl.multiple_of(b * ROWS, ROWS), ROWS)

        @pl.when(b == seat // 4)
        def _():
            arrived(g_ref.at[pl.ds(0, 192), :], g_recv.at[b])

        @pl.when(b != seat // 4)
        def _():
            arrived(g_ref.at[pl.ds(0, 256), :], g_recv.at[b])

        in_copy(i).wait()
        grad_q = backward_rows(
            q_ref[rows, :], g_ref[rows, :], att_ref[rows, :], e_tile.at[lax.rem(i, 2)], et_ref.at[:, rows, :],
            si_ref[rows, :], st_ref[rows, :], k_ref[...], with_ones(v_ref[...]), kt_ref[...], with_ones(vt_ref[...]), k_acc, v_acc)

        @pl.when(i + 2 < blocks)
        def _():
            in_copy(i + 2).start()

        give_q[:, rows] = (grad_q * factor).T.astype(jnp.bfloat16)
        gq_ref[core, :, rows] = give_q[head_rows, rows]
        give(0, give_q, gq_ref, rows).start()

    give_k[...] = (k_acc[...] * factor[:, :1]).astype(jnp.bfloat16)
    give(1, give_k, gk_ref, every).start()
    give_v[...] = (v_acc[...] * coef[:, :1]).astype(jnp.bfloat16)
    give(2, give_v, gv_ref, every).start()
    gk_ref[core] = give_k[head_rows, :]
    gv_ref[core] = give_v[head_rows, :]
    for w, buf in enumerate((gate_buf, up_buf, down_buf, ctx_buf)):
        arrived(buf.at[pl.ds(0, 7)], w_send.at[w])
    arrived(out_buf.at[pl.ds(0, 7), 0], w_send.at[4])
    for i, (_, dst) in enumerate(images):
        arrived(dst.at[pl.ds(0, 31 * 64), :], qkv_send.at[i])
    arrived(g_ref.at[pl.ds(0, 31 * 64), :], g_send)
    arrived(att_ref.at[pl.ds(0, 31 * 64), :], tok_send)
    arrived(err_all.at[pl.ds(0, 31)], err_send)
    for i, (staged, out) in enumerate(((give_q, gq_ref), (give_k, gk_ref), (give_v, gv_ref))):
        give(i, staged, out, every).wait()


def text_rows(q, k, v_aug, kept, o, z, m, e_ref):
    q = q * jnp.asarray(1.0 / math.sqrt(HEAD), jnp.bfloat16)
    outs, tops = [], []
    for j in range(2):
        qj = jnp.where(head_lanes(j), q, jnp.zeros_like(q))
        s = jnp.where(kept, dot(qj, k, NT), -jnp.inf)
        top = jnp.maximum(m[:, j * HEAD:j * HEAD + 1], jnp.max(s, axis=-1, keepdims=True))
        e = jnp.exp(s - top).astype(jnp.bfloat16)
        e_ref[j] = e
        outs.append(dot(e, v_aug))
        tops.append(top)
    alpha = jnp.exp(m - by_head(tops[0], tops[1]))
    inv = 1.0 / (alpha * z + by_head(outs[0][:, LANES:], outs[1][:, LANES:]))
    o = alpha * o + by_head(outs[0][:, :LANES], outs[1][:, :LANES])
    return (o * inv).astype(jnp.bfloat16), alpha * inv, inv


def backward_rows(q, g, att, ei_ref, et_ref, si, st, k, v_aug, kt, vt_aug, k_acc, v_acc):
    g = g.astype(jnp.float32)
    prod = g * att.astype(jnp.float32)
    q_t = q.T
    lane = lax.broadcasted_iota(jnp.int32, (1, LANES), 1)
    grads = []
    for j in range(2):
        mine = head_lanes(j)
        gj = jnp.where(mine, g, 0.0)
        delta = jnp.sum(jnp.where(mine, prod, 0.0), axis=-1, keepdims=True)

        def scaled(scale):
            gs = (gj * scale).astype(jnp.bfloat16)
            d = -delta * scale
            hi = d.astype(jnp.bfloat16)
            low = (d - hi.astype(jnp.float32)).astype(jnp.bfloat16)
            extra = jnp.where(lane == 0, hi, jnp.where(lane == 1, low, jnp.zeros_like(hi)))
            return gs, jnp.concatenate([gs, extra], axis=1)

        gi, lhs_i = scaled(si[:, j * HEAD:j * HEAD + 1])
        _, lhs_t = scaled(st[:, j * HEAD:j * HEAD + 1])
        ei = ei_ref[j]
        ds = (ei.astype(jnp.float32) * dot(lhs_i, v_aug, NT)).astype(jnp.bfloat16)
        ds_t = (et_ref[j].astype(jnp.float32) * dot(lhs_t, vt_aug, NT)).astype(jnp.bfloat16)
        grads.append(dot(ds, k) + dot(ds_t, kt))
        rows = slice(j * HEAD, (j + 1) * HEAD)
        k_acc[rows, :] += dot(q_t[rows, :], ds)
        v_acc[rows, :] += dot(gi.T[rows, :], ei)
    return by_head(grads[0], grads[1])


def call_window(lengths, scalars, prompt, gain_in, gain_out, target, gate, up, down, ctx, out, q, k, v):
    bf16, f32 = jnp.bfloat16, jnp.float32
    anywhere, vmem = pl.BlockSpec(memory_space=pl.ANY), pl.BlockSpec(memory_space=pltpu.VMEM)
    shape = jax.ShapeDtypeStruct
    dma, buf = pltpu.SemaphoreType.DMA, pltpu.VMEM
    grads = shape((2, HEAD, SEQ), bf16)
    return pl.pallas_call(
        window,
        in_specs=[vmem] * 6 + [anywhere] * 8,
        out_specs=[vmem] * 4 + [anywhere],
        out_shape=[shape((1, LANES), f32)] + [grads] * 3 + [shape((2, SEQ, SEQ), bf16)],
        scratch_shapes=[
            buf((8, 512, 256), bf16), buf((8, 512, 256), bf16), buf((8, 256, 512), bf16), buf((8, 512, 128), bf16),
            buf((8, 2, 128, CH), bf16),
            buf((8, PROMPT, 512), bf16), buf((PROMPT, 256), f32), buf((PROMPT, 256), f32),
            buf((8, PROMPT, 512), bf16), buf((4, PROMPT, 512), bf16), buf((4, PROMPT, 512), bf16),
            buf((4, 4, 64, 512), bf16), buf((4, 64, 512), bf16), buf((4, 4, 16, 512), bf16),
            buf((8, PROMPT, 512), bf16), buf((2, PROMPT, LANES), bf16), buf((2, 2, ROWS, SEQ), bf16),
            buf((SEQ, LANES), f32), buf((SEQ, LANES), f32), buf((SEQ, LANES), f32),
            buf((LANES, 2048), bf16), buf((LANES, CH), f32), buf((LANES, 2048), bf16), buf((32, 8, LANES), f32),
            buf((SEQ, LANES), bf16), buf((SEQ, LANES), bf16), buf((SEQ, LANES), bf16), buf((PROMPT, LANES), bf16),
            buf((PROMPT, LANES), bf16), buf((2, SEQ, PROMPT), bf16), buf((SEQ, LANES), f32), buf((SEQ, LANES), f32),
            buf((SEQ, LANES), bf16), buf((SEQ, LANES), bf16), buf((LANES, SEQ), f32), buf((LANES, SEQ), f32),
            buf((LANES, SEQ), bf16), buf((LANES, SEQ), bf16), buf((LANES, SEQ), bf16),
            dma((5,)), dma((5,)), dma((5, 9)), dma((3,)), dma((3,)), dma((3,)), dma((2,)), dma((16,)), dma((16,)),
            dma((3,)), dma((3,)), dma((8,)),
        ] + [dma] * 7,
        compiler_params=pltpu.CompilerParams(collective_id=0, has_side_effects=True, vmem_limit_bytes=60 * 1024 * 1024),
        name="window",
    )(lengths, scalars, prompt, gain_in, gain_out, target, gate, up, down, ctx, out, q, k, v)


def on_device(prompt, lengths, timesteps, ref_errors, gain_ffn, w_in_gate, w_in_up, w_in_down, gain_final, w_context,
              image_q, image_k, image_v, w_out, target):
    scalars = jnp.stack([noise_level(timesteps[0]), ref_errors[0, 0], ref_errors[0, 1]])
    loss, grad_q, grad_k, grad_v, _ = call_window(
        jnp.broadcast_to(lengths[:, None], (1, PROMPT)), jnp.broadcast_to(scalars[:, None], (3, LANES)),
        prompt[0], gain_ffn[None], gain_final[None], target[0].reshape(LANES, CH),
        w_in_gate, w_in_up, w_in_down, w_context, w_out.reshape(2, 128, CH), image_q[0], image_k[0], image_v[0])
    return (loss[0, :1],) + tuple(jnp.transpose(grads, (0, 2, 1))[None] for grads in (grad_q, grad_k, grad_v))


def solution(mesh):
    return jax.shard_map(
        on_device,
        mesh=mesh,
        in_specs=(
            P("fsdp", None, None),
            P("fsdp"),
            P("fsdp"),
            P("fsdp", None),
            P(),
            P("fsdp", "seq"),
            P("fsdp", "seq"),
            P("seq", "fsdp"),
            P(),
            P("fsdp", "seq"),
            P("fsdp", None, "seq", None),
            P("fsdp", None, "seq", None),
            P("fsdp", None, "seq", None),
            P("fsdp", None),
            P("fsdp", None, "seq", None),
        ),
        out_specs=(
            P("fsdp"),
            P("fsdp", None, None, "seq"),
            P("fsdp", None, None, "seq"),
            P("fsdp", None, None, "seq"),
        ),
        check_vma=False,
    )
```

```python
import math

import jax
import jax.numpy as jnp
from jax import lax
from jax.experimental import pallas as pl
from jax.experimental.pallas import tpu as pltpu
from jax.sharding import PartitionSpec as P

PROMPT = 256
HEAD = 64
CH = 1280
SEQ = 2048
LANES = 128
ROWS = 256

dpo_beta = 20.0
norm_eps = 1e-06

NT = (((1,), (1,)), ((), ()))
NN = (((1,), (0,)), ((), ()))


def dot(a, b, dims=NN):
    return lax.dot_general(a, b, dims, preferred_element_type=jnp.float32)


def noise_level(step_index):
    fraction = (step_index.astype(jnp.float32) + 1.0) / 1000.0
    return 3.0 * fraction / (1.0 + 2.0 * fraction)


def head_lanes(j):
    lane = lax.broadcasted_iota(jnp.int32, (1, LANES), 1)
    return (lane >= j * HEAD) & (lane < (j + 1) * HEAD)


def with_ones(values):
    return jnp.concatenate([values, jnp.ones_like(values)], axis=1)


def by_head(first, second):
    return jnp.where(head_lanes(0), first, second)


def image_rows(q, k, v_aug, e_ref):
    q = q * jnp.asarray(1.0 / math.sqrt(HEAD), jnp.bfloat16)
    outs, tops = [], []
    for j in range(2):
        qj = jnp.where(head_lanes(j), q, jnp.zeros_like(q))
        s = dot(qj, k, NT)
        top = jnp.max(s, axis=-1, keepdims=True)
        e = jnp.exp(s - top).astype(jnp.bfloat16)
        e_ref[j] = e
        outs.append(dot(e, v_aug))
        tops.append(top)
    return (
        by_head(outs[0][:, :LANES], outs[1][:, :LANES]),
        by_head(outs[0][:, LANES:], outs[1][:, LANES:]),
        by_head(tops[0], tops[1]),
    )


def place():
    seat, pair = lax.axis_index("seq"), lax.axis_index("fsdp")
    chip = seat // 2
    return seat, lax.rem(seat, 2), lax.rem(chip, 4), chip // 4, pair, lax.rem(pair, 4), pair // 4


def remote(src, dst, send_sem, recv_sem, seat, pair):
    return pltpu.make_async_remote_copy(
        src_ref=src, dst_ref=dst, send_sem=send_sem, recv_sem=recv_sem,
        device_id=(seat, pair), device_id_type=pl.DeviceIdType.MESH,
    )


def arrived(ref, sem):
    pltpu.make_async_copy(ref, ref, sem).wait()


ALTERNATE = (1, 3, 2, 0)


def window(
    len_ref, step_ref, error_ref, prompt_ref, gain_in_ref, gain_out_ref, target_ref, gate_in, up_in, down_in, ctx_in, out_in, q_in, k_in, v_in,
    loss_ref, gq_ref, gk_ref, gv_ref, ei_ref,
    gate_buf, up_buf, down_buf, ctx_buf, out_buf, normed, gate_acc, up_acc, part, sib, half, from_x, sum_x, from_z, state,
    ctx_pair, e_tile, o_all, z_all, m_all, tok, resid, grad, err_all,
    q_ref, k_ref, v_ref, kt_ref, vt_ref, et_ref, si_ref, st_ref, att_ref, g_ref, k_acc, v_acc, give_q, give_k, give_v,
    w_local, w_send, w_recv, qkv_local, qkv_send, qkv_recv, e_sem, stage_send, stage_recv, swap_send, swap_recv, g_recv,
    tok_local, tok_send, tok_recv, g_local, g_send, err_send, err_recv,
):
    seat, core, x, zh, pair, y, zl = place()
    other = seat + 1 - 2 * core
    low = lax.rem(seat, 8)
    up_y, down_y = lax.rem(y + 1, 4), lax.rem(y + 3, 4)
    far = lax.rem(y + 2, 4)
    base, base_p = zl * 4, (1 - zl) * 4
    partner = base_p + y

    barrier = pltpu.get_barrier_semaphore()

    @pl.loop(1, 32)
    def _(d):
        pl.semaphore_signal(barrier, inc=1, device_id=(lax.rem(seat + d, 32), pair), device_id_type=pl.DeviceIdType.MESH)

    for peer in (partner, base + up_y, base + down_y):
        pl.semaphore_signal(barrier, inc=1, device_id=(seat, peer), device_id_type=pl.DeviceIdType.MESH)
    pl.semaphore_wait(barrier, 34)

    def plain(buf):
        return lambda slot, rows=None: buf.at[slot] if rows is None else buf.at[slot, rows]

    def own_half(slot, rows=None):
        return out_buf.at[slot, core] if rows is None else out_buf.at[slot, core, rows]

    weights = (
        (gate_in, plain(gate_buf), 512), (up_in, plain(up_buf), 512), (down_in, plain(down_buf), 256),
        (ctx_in, plain(ctx_buf), 512), (out_in.at[core], own_half, 128),
    )
    early, late = (0, 1, 2), (3, 4)

    def send_weight(w, src, dst, sem, peer):
        remote(src, dst, w_send.at[w], w_recv.at[w, sem], seat, peer).start()

    def upper(w, slot):
        return weights[w][1](slot, pl.ds(0, weights[w][2] // 2))

    def lower(w, slot):
        return weights[w][1](slot, pl.ds(weights[w][2] // 2, weights[w][2] // 2))

    def send_own(w):
        src, at, _ = weights[w]
        send_weight(w, src, at(pair), 0, partner)
        send_weight(w, src, at(pair), 1, base + up_y)
        send_weight(w, src, at(pair), 2, base + down_y)
        pltpu.make_async_copy(src, at(pair), w_local.at[w]).start()

    def forward_near(w):
        at = weights[w][1]
        arrived(at(partner), w_recv.at[w, 0])
        send_weight(w, at(partner), at(partner), 3, base + up_y)
        send_weight(w, at(partner), at(partner), 4, base + down_y)
        arrived(at(base + down_y), w_recv.at[w, 1])
        send_weight(w, upper(w, base + down_y), upper(w, base + down_y), 5, base + up_y)
        arrived(at(base + up_y), w_recv.at[w, 2])
        send_weight(w, lower(w, base + up_y), lower(w, base + up_y), 6, base + down_y)

    def forward_partner(w):
        at = weights[w][1]
        arrived(at(base_p + down_y), w_recv.at[w, 3])
        send_weight(w, upper(w, base_p + down_y), upper(w, base_p + down_y), 7, base + up_y)
        arrived(at(base_p + up_y), w_recv.at[w, 4])
        send_weight(w, lower(w, base_p + up_y), lower(w, base_p + up_y), 8, base + down_y)

    def weight_ready(w):
        arrived(upper(w, base + far), w_recv.at[w, 5])
        arrived(lower(w, base + far), w_recv.at[w, 6])
        arrived(upper(w, base_p + far), w_recv.at[w, 7])
        arrived(lower(w, base_p + far), w_recv.at[w, 8])
        pltpu.make_async_copy(weights[w][0], weights[w][1](pair), w_local.at[w]).wait()

    for w in early:
        send_own(w)

    def token_rows(to):
        return pl.ds(pl.multiple_of(to * 64, 64), 64)

    def lanes_of(to):
        return pl.ds(pl.multiple_of((to // 2) * LANES, LANES), LANES)

    def stream_rows(to):
        return pl.ds(pl.multiple_of(lax.rem(to, 2) * 64, 64), 64)

    images = ((q_in, q_ref), (k_in, k_ref), (v_in, v_ref))

    def send_image(i):
        src, dst = images[i]

        @pl.loop(0, 8)
        def _(j):
            for dz in ALTERNATE:
                to = lax.rem(zh + dz, 4) * 8 + lax.rem(low + j, 8)

                def start(to=to):
                    remote(src.at[lax.rem(to, 2), :, lanes_of(to)], dst.at[token_rows(seat), :],
                           qkv_send.at[i], qkv_recv.at[i], to, pair).start()

                if dz:
                    start()
                else:
                    pl.when(j > 0)(start)

        pltpu.make_async_copy(src.at[core, :, lanes_of(seat)], dst.at[token_rows(seat), :], qkv_local.at[i]).start()

    total = jnp.zeros((PROMPT, 1), jnp.float32)
    for f in range(8):
        rows = prompt_ref[:, 512 * f:512 * (f + 1)].astype(jnp.float32)
        total = total + jnp.sum(rows * rows, axis=-1, keepdims=True)
    inv = lax.rsqrt(total * (1.0 / 4096) + norm_eps)
    for f in range(8):
        cols = slice(512 * f, 512 * (f + 1))
        normed[f] = (prompt_ref[:, cols].astype(jnp.float32) * inv * gain_in_ref[:, cols]).astype(jnp.bfloat16)

    for w in early:
        forward_near(w)
    for i in range(3):
        send_image(i)
        forward_partner(i)

    def images_ready():
        for i, (_, dst) in enumerate(images):
            arrived(dst.at[pl.ds(0, 31 * 64), :], qkv_recv.at[i])
            arrived(dst.at[pl.ds(0, 64), :], qkv_local.at[i])

    blocks = SEQ // ROWS

    def out_copy(b):
        slot = lax.rem(b, 2)
        return pltpu.make_async_copy(e_tile.at[slot], ei_ref.at[:, pl.ds(pl.multiple_of(b * ROWS, ROWS), ROWS), :], e_sem.at[slot])

    def image_blocks(start, stop):
        @pl.loop(start, stop)
        def _(b):
            @pl.when(b >= 2)
            def _():
                out_copy(b - 2).wait()

            rows = pl.ds(pl.multiple_of(b * ROWS, ROWS), ROWS)
            o, z, m = image_rows(q_ref[rows, :], k_ref[...], with_ones(v_ref[...]), e_tile.at[lax.rem(b, 2)])
            o_all[rows, :], z_all[rows, :], m_all[rows, :] = o, z, m
            out_copy(b).start()

    weight_ready(0)
    weight_ready(1)
    gate_acc[...] = jnp.zeros_like(gate_acc)
    up_acc[...] = jnp.zeros_like(up_acc)

    @pl.loop(0, 8)
    def _(f):
        gate_acc[...] += dot(normed[f], gate_buf[f])
        up_acc[...] += dot(normed[f], up_buf[f])

    hidden = (jax.nn.gelu(gate_acc[...], approximate=True) * up_acc[...]).astype(jnp.bfloat16)
    weight_ready(2)

    def part_block(f):
        part[f] = dot(hidden, down_buf[f]).astype(jnp.bfloat16)

    @pl.loop(0, 4)
    def _(i):
        part_block((1 - core) * 4 + i)

    to_other = remote(part.at[pl.ds((1 - core) * 4, 4)], sib, stage_send.at[0], stage_recv.at[0], other, pair)
    to_other.start()
    for w in late:
        send_own(w)

    @pl.loop(0, 4)
    def _(i):
        part_block(core * 4 + i)

    to_other.wait()
    for i in range(4):
        half[i] = (part[core * 4 + i].astype(jnp.float32) + sib[i].astype(jnp.float32)).astype(jnp.bfloat16)

    def seat_of(zh_to, x_to):
        return (zh_to * 4 + x_to) * 2 + core

    def rows_x(at):
        return pl.ds(pl.multiple_of(at * 64, 64), 64)

    def rows_z(at):
        return pl.ds(pl.multiple_of(at * 16, 16), 16)

    def round_of(stage, make, between=lambda: None):
        copies = [make(d, stage_send.at[stage + d], stage_recv.at[stage + d]) for d in (1, 3, 2)]
        for copy in copies:
            copy.start()
        between()
        for copy in copies:
            copy.wait()

    def during_x():
        images_ready()
        image_blocks(0, 2)
        for w in late:
            forward_near(w)
        image_blocks(2, 4)

    round_of(0, lambda d, s, r: remote(
        half.at[:, rows_x(lax.rem(x + d, 4)), :], from_x.at[d], s, r, seat_of(zh, lax.rem(x + d, 4)), pair), during_x)
    for i in range(4):
        acc = half[i, rows_x(x), :].astype(jnp.float32)
        for d in (1, 2, 3):
            acc = acc + from_x[d, i].astype(jnp.float32)
        sum_x[i] = acc.astype(jnp.bfloat16)
    round_of(3, lambda d, s, r: remote(
        sum_x.at[:, rows_z(lax.rem(zh + d, 4)), :], from_z.at[d], s, r, seat_of(lax.rem(zh + d, 4), x), pair),
        lambda: image_blocks(4, 5))
    mine = rows_z(x * 4 + zh)
    for i in range(4):
        columns = pl.ds(pl.multiple_of(core * 2048 + i * 512, 512), 512)
        acc = prompt_ref[mine, columns].astype(jnp.float32) + sum_x[i, rows_z(zh), :].astype(jnp.float32)
        for d in (1, 2, 3):
            acc = acc + from_z[d, i].astype(jnp.float32)
        state[core * 4 + i, mine, :] = acc.astype(jnp.bfloat16)
    ours = pl.ds(core * 4, 4)
    round_of(6, lambda d, s, r: remote(
        state.at[ours, mine, :], state.at[ours, mine, :], s, r, seat_of(lax.rem(zh + d, 4), x), pair),
        lambda: image_blocks(5, 6))

    def forward_late():
        for w in late:
            forward_partner(w)
        image_blocks(6, 8)

    round_of(9, lambda d, s, r: remote(
        state.at[ours, rows_x(x), :], state.at[ours, rows_x(x), :], s, r, seat_of(zh, lax.rem(x + d, 4)), pair), forward_late)
    last = remote(state.at[ours], state.at[ours], stage_send.at[13], stage_recv.at[13], other, pair)
    last.start()
    weight_ready(3)
    last.wait()

    total = jnp.zeros((PROMPT, 1), jnp.float32)
    for f in range(8):
        rows = state[f].astype(jnp.float32)
        total = total + jnp.sum(rows * rows, axis=-1, keepdims=True)
    inv = lax.rsqrt(total * (1.0 / 4096) + norm_eps)
    context = jnp.zeros((PROMPT, LANES), jnp.float32)
    for f in range(8):
        encoded = (state[f].astype(jnp.float32) * inv * gain_out_ref[:, 512 * f:512 * (f + 1)]).astype(jnp.bfloat16)
        context = context + dot(encoded, ctx_buf[f])
    ctx_pair[core] = context.astype(jnp.bfloat16)
    text_swap = remote(ctx_pair.at[core], ctx_pair.at[core], stage_send.at[14], stage_recv.at[14], other, pair)
    text_swap.start()
    weight_ready(4)
    share = remote(out_buf.at[:, core], out_buf.at[:, core], stage_send.at[15], stage_recv.at[15], other, pair)
    share.start()
    text_swap.wait()
    first, second = ctx_pair[0].astype(jnp.float32), ctx_pair[1].astype(jnp.float32)
    kt_ref[...] = by_head(first, pltpu.roll(second, HEAD, 1)).astype(jnp.bfloat16)
    vt_ref[...] = by_head(pltpu.roll(first, HEAD, 1), second).astype(jnp.bfloat16)

    spot = tok.at[stream_rows(seat), lanes_of(seat)]
    kept = lax.broadcasted_iota(jnp.int32, (1, PROMPT), 1) < len_ref[0]

    @pl.loop(0, 2)
    def _(part_of):
        for dz in ALTERNATE:
            b = lax.rem(zh + dz, 4) * 2 + part_of
            rows = pl.ds(pl.multiple_of(b * ROWS, ROWS), ROWS)
            att, scale_i, scale_t = text_rows(
                q_ref[rows, :], kt_ref[...], with_ones(vt_ref[...]), kept, o_all[rows, :], z_all[rows, :], m_all[rows, :],
                et_ref.at[:, rows, :])
            att_ref[rows, :], si_ref[rows, :], st_ref[rows, :] = att, scale_i, scale_t
            for t in range(4):
                to = b * 4 + t

                def start(to=to):
                    remote(att_ref.at[token_rows(to), :], spot, tok_send, tok_recv, to, pair).start()

                def keep(to=to):
                    pltpu.make_async_copy(att_ref.at[token_rows(to), :], spot, tok_local).start()

                if dz:
                    start()
                else:
                    pl.when(to != seat)(start)
                    pl.when(to == seat)(keep)

    share.wait()
    arrived(spot, tok_local)
    arrived(att_ref.at[pl.ds(0, 31 * 64), :], tok_recv)

    acc = -target_ref[...].astype(jnp.float32)
    resid[...] = acc

    @pl.loop(0, 8)
    def _(f):
        columns = pl.ds(pl.multiple_of(f * 256, 256), 256)
        resid[...] += dot(tok[:, columns], out_buf[f].reshape(256, CH))

    halves = []
    for stream in range(2):
        rows = resid[64 * stream:64 * (stream + 1), :]
        halves.append(jnp.sum(jnp.sum(rows * rows, axis=1, keepdims=True), axis=0, keepdims=True))
    row = lax.broadcasted_iota(jnp.int32, (8, LANES), 0)
    err_all[seat] = jnp.where(row == 0, halves[0], jnp.where(row == 1, halves[1], 0.0))
    rounded = resid[...].astype(jnp.bfloat16)

    @pl.loop(0, 2)
    def _(part_of):
        for dz in ALTERNATE:
            n = lax.rem(zh + dz, 4) * 2 + lax.rem(low // 4 + part_of, 2)
            columns = pl.ds(pl.multiple_of(n * 256, 256), 256)
            grad[:, columns] = dot(rounded, out_buf[n].reshape(256, CH), NT).astype(jnp.bfloat16)
            for t in range(4):
                to = n * 4 + t

                def start(to=to):
                    remote(grad.at[stream_rows(to), lanes_of(to)], g_ref.at[token_rows(seat), :], g_send, g_recv.at[seat // 4], to, pair).start()
                    remote(err_all.at[seat], err_all.at[seat], err_send, err_recv, to, pair).start()

                def keep(to=to):
                    pltpu.make_async_copy(grad.at[stream_rows(to), lanes_of(to)], g_ref.at[token_rows(seat), :], g_local).start()

                if dz:
                    start()
                else:
                    pl.when(to != seat)(start)
                    pl.when(to == seat)(keep)

    def order(i):
        r = lax.rem(i, 4)
        return lax.rem(zh + lax.rem(1 + 2 * r + r // 2, 4), 4) * 2 + lax.rem(low // 4 + i // 4, 2)

    def in_copy(i):
        slot = lax.rem(i, 2)
        rows = pl.ds(pl.multiple_of(order(i) * ROWS, ROWS), ROWS)
        return pltpu.make_async_copy(ei_ref.at[:, rows, :], e_tile.at[slot], e_sem.at[slot])

    out_copy(blocks - 2).wait()
    out_copy(blocks - 1).wait()
    in_copy(0).start()
    in_copy(1).start()
    k_acc[...] = jnp.zeros_like(k_acc)
    v_acc[...] = jnp.zeros_like(v_acc)

    arrived(err_all.at[pl.ds(0, 31)], err_recv)
    mean_errors = jnp.sum(err_all[...], axis=0) * (1.0 / (SEQ * CH))
    error_gap = (mean_errors[0:1] - error_ref[:, 0:1]) - (mean_errors[1:2] - error_ref[:, 1:2])
    sigma = noise_level(jnp.full((1, LANES), step_ref[0], jnp.int32))
    logit = dpo_beta * sigma * error_gap
    loss_ref[...] = jnp.maximum(logit, 0.0) + jnp.log1p(jnp.exp(-jnp.abs(logit)))
    coef = sigma / (1.0 + jnp.exp(-logit)) * (1 - 2 * core).astype(jnp.float32)
    factor = coef * (1.0 / math.sqrt(HEAD))
    head_rows = pl.ds(pl.multiple_of(core * HEAD, HEAD), HEAD)
    other_rows = pl.ds(pl.multiple_of((1 - core) * HEAD, HEAD), HEAD)
    arrived(g_ref.at[pl.ds(0, 64), :], g_local)

    def give(i, staged, out, cols):
        return remote(staged.at[other_rows, cols], out.at[core, :, cols], swap_send.at[i], swap_recv.at[i], other, pair)

    every = pl.ds(0, SEQ)

    @pl.loop(0, blocks)
    def _(i):
        b = order(i)
        rows = pl.ds(pl.multiple_of(b * ROWS, ROWS), ROWS)

        @pl.when(b == seat // 4)
        def _():
            arrived(g_ref.at[pl.ds(0, 192), :], g_recv.at[b])

        @pl.when(b != seat // 4)
        def _():
            arrived(g_ref.at[pl.ds(0, 256), :], g_recv.at[b])

        in_copy(i).wait()
        grad_q = backward_rows(
            q_ref[rows, :], g_ref[rows, :], att_ref[rows, :], e_tile.at[lax.rem(i, 2)], et_ref.at[:, rows, :],
            si_ref[rows, :], st_ref[rows, :], k_ref[...], with_ones(v_ref[...]), kt_ref[...], with_ones(vt_ref[...]), k_acc, v_acc)

        @pl.when(i + 2 < blocks)
        def _():
            in_copy(i + 2).start()

        give_q[:, rows] = (grad_q * factor).T.astype(jnp.bfloat16)
        gq_ref[core, :, rows] = give_q[head_rows, rows]
        give(0, give_q, gq_ref, rows).start()

    give_k[...] = (k_acc[...] * factor[:, :1]).astype(jnp.bfloat16)
    give(1, give_k, gk_ref, every).start()
    give_v[...] = (v_acc[...] * coef[:, :1]).astype(jnp.bfloat16)
    give(2, give_v, gv_ref, every).start()
    gk_ref[core] = give_k[head_rows, :]
    gv_ref[core] = give_v[head_rows, :]
    for w, buf in enumerate((gate_buf, up_buf, down_buf, ctx_buf)):
        arrived(buf.at[pl.ds(0, 7)], w_send.at[w])
    arrived(out_buf.at[pl.ds(0, 7), 0], w_send.at[4])
    for i, (_, dst) in enumerate(images):
        arrived(dst.at[pl.ds(0, 31 * 64), :], qkv_send.at[i])
    arrived(g_ref.at[pl.ds(0, 31 * 64), :], g_send)
    arrived(att_ref.at[pl.ds(0, 31 * 64), :], tok_send)
    arrived(err_all.at[pl.ds(0, 31)], err_send)
    for i, (staged, out) in enumerate(((give_q, gq_ref), (give_k, gk_ref), (give_v, gv_ref))):
        give(i, staged, out, every).wait()


def text_rows(q, k, v_aug, kept, o, z, m, e_ref):
    q = q * jnp.asarray(1.0 / math.sqrt(HEAD), jnp.bfloat16)
    outs, tops = [], []
    for j in range(2):
        qj = jnp.where(head_lanes(j), q, jnp.zeros_like(q))
        s = jnp.where(kept, dot(qj, k, NT), -jnp.inf)
        top = jnp.maximum(m[:, j * HEAD:j * HEAD + 1], jnp.max(s, axis=-1, keepdims=True))
        e = jnp.exp(s - top).astype(jnp.bfloat16)
        e_ref[j] = e
        outs.append(dot(e, v_aug))
        tops.append(top)
    alpha = jnp.exp(m - by_head(tops[0], tops[1]))
    inv = 1.0 / (alpha * z + by_head(outs[0][:, LANES:], outs[1][:, LANES:]))
    o = alpha * o + by_head(outs[0][:, :LANES], outs[1][:, :LANES])
    return (o * inv).astype(jnp.bfloat16), alpha * inv, inv


def backward_rows(q, g, att, ei_ref, et_ref, si, st, k, v_aug, kt, vt_aug, k_acc, v_acc):
    g = g.astype(jnp.float32)
    prod = g * att.astype(jnp.float32)
    q_t = q.T
    lane = lax.broadcasted_iota(jnp.int32, (1, LANES), 1)
    grads = []
    for j in range(2):
        mine = head_lanes(j)
        gj = jnp.where(mine, g, 0.0)
        delta = jnp.sum(jnp.where(mine, prod, 0.0), axis=-1, keepdims=True)

        def scaled(scale):
            gs = (gj * scale).astype(jnp.bfloat16)
            d = -delta * scale
            hi = d.astype(jnp.bfloat16)
            low = (d - hi.astype(jnp.float32)).astype(jnp.bfloat16)
            extra = jnp.where(lane == 0, hi, jnp.where(lane == 1, low, jnp.zeros_like(hi)))
            return gs, jnp.concatenate([gs, extra], axis=1)

        gi, lhs_i = scaled(si[:, j * HEAD:j * HEAD + 1])
        _, lhs_t = scaled(st[:, j * HEAD:j * HEAD + 1])
        ei = ei_ref[j]
        ds = (ei.astype(jnp.float32) * dot(lhs_i, v_aug, NT)).astype(jnp.bfloat16)
        ds_t = (et_ref[j].astype(jnp.float32) * dot(lhs_t, vt_aug, NT)).astype(jnp.bfloat16)
        grads.append(dot(ds, k) + dot(ds_t, kt))
        rows = slice(j * HEAD, (j + 1) * HEAD)
        k_acc[rows, :] += dot(q_t[rows, :], ds)
        v_acc[rows, :] += dot(gi.T[rows, :], ei)
    return by_head(grads[0], grads[1])


def call_window(lengths, timesteps, ref_errors, prompt, gain_in, gain_out, target, gate, up, down, ctx, out, q, k, v):
    bf16, f32 = jnp.bfloat16, jnp.float32
    anywhere, vmem = pl.BlockSpec(memory_space=pl.ANY), pl.BlockSpec(memory_space=pltpu.VMEM)
    shape = jax.ShapeDtypeStruct
    dma, buf = pltpu.SemaphoreType.DMA, pltpu.VMEM
    grads = shape((2, HEAD, SEQ), bf16)
    return pl.pallas_call(
        window,
        in_specs=[pl.BlockSpec(memory_space=pltpu.SMEM)] * 2 + [vmem] * 5 + [anywhere] * 8,
        out_specs=[vmem] * 4 + [anywhere],
        out_shape=[shape((1, LANES), f32)] + [grads] * 3 + [shape((2, SEQ, SEQ), bf16)],
        scratch_shapes=[
            buf((8, 512, 256), bf16), buf((8, 512, 256), bf16), buf((8, 256, 512), bf16), buf((8, 512, 128), bf16),
            buf((8, 2, 128, CH), bf16),
            buf((8, PROMPT, 512), bf16), buf((PROMPT, 256), f32), buf((PROMPT, 256), f32),
            buf((8, PROMPT, 512), bf16), buf((4, PROMPT, 512), bf16), buf((4, PROMPT, 512), bf16),
            buf((4, 4, 64, 512), bf16), buf((4, 64, 512), bf16), buf((4, 4, 16, 512), bf16),
            buf((8, PROMPT, 512), bf16), buf((2, PROMPT, LANES), bf16), buf((2, 2, ROWS, SEQ), bf16),
            buf((SEQ, LANES), f32), buf((SEQ, LANES), f32), buf((SEQ, LANES), f32),
            buf((LANES, 2048), bf16), buf((LANES, CH), f32), buf((LANES, 2048), bf16), buf((32, 8, LANES), f32),
            buf((SEQ, LANES), bf16), buf((SEQ, LANES), bf16), buf((SEQ, LANES), bf16), buf((PROMPT, LANES), bf16),
            buf((PROMPT, LANES), bf16), buf((2, SEQ, PROMPT), bf16), buf((SEQ, LANES), f32), buf((SEQ, LANES), f32),
            buf((SEQ, LANES), bf16), buf((SEQ, LANES), bf16), buf((LANES, SEQ), f32), buf((LANES, SEQ), f32),
            buf((LANES, SEQ), bf16), buf((LANES, SEQ), bf16), buf((LANES, SEQ), bf16),
            dma((5,)), dma((5,)), dma((5, 9)), dma((3,)), dma((3,)), dma((3,)), dma((2,)), dma((16,)), dma((16,)),
            dma((3,)), dma((3,)), dma((8,)),
        ] + [dma] * 7,
        compiler_params=pltpu.CompilerParams(collective_id=0, has_side_effects=True, vmem_limit_bytes=54 * 1024 * 1024),
        name="window",
    )(lengths, timesteps, ref_errors, prompt, gain_in, gain_out, target, gate, up, down, ctx, out, q, k, v)


def on_device(prompt, lengths, timesteps, ref_errors, gain_ffn, w_in_gate, w_in_up, w_in_down, gain_final, w_context,
              image_q, image_k, image_v, w_out, target):
    loss, grad_q, grad_k, grad_v, _ = call_window(
        lengths, timesteps, ref_errors, prompt[0], gain_ffn[None], gain_final[None], target[0].reshape(LANES, CH),
        w_in_gate, w_in_up, w_in_down, w_context, w_out.reshape(2, 128, CH), image_q[0], image_k[0], image_v[0])
    return (loss[0, :1],) + tuple(jnp.transpose(grads, (0, 2, 1))[None] for grads in (grad_q, grad_k, grad_v))


def solution(mesh):
    return jax.shard_map(
        on_device,
        mesh=mesh,
        in_specs=(
            P("fsdp", None, None),
            P("fsdp"),
            P("fsdp"),
            P("fsdp", None),
            P(),
            P("fsdp", "seq"),
            P("fsdp", "seq"),
            P("seq", "fsdp"),
            P(),
            P("fsdp", "seq"),
            P("fsdp", None, "seq", None),
            P("fsdp", None, "seq", None),
            P("fsdp", None, "seq", None),
            P("fsdp", None),
            P("fsdp", None, "seq", None),
        ),
        out_specs=(
            P("fsdp"),
            P("fsdp", None, None, "seq"),
            P("fsdp", None, None, "seq"),
            P("fsdp", None, None, "seq"),
        ),
        check_vma=False,
    )
```

```python
import math

import jax
import jax.numpy as jnp
from jax import lax
from jax.experimental import pallas as pl
from jax.experimental.pallas import tpu as pltpu
from jax.sharding import PartitionSpec as P

PROMPT = 256
HEAD = 64
CH = 1280
SEQ = 2048
LANES = 128
ROWS = 256

dpo_beta = 20.0
norm_eps = 1e-06

NT = (((1,), (1,)), ((), ()))
NN = (((1,), (0,)), ((), ()))


def dot(a, b, dims=NN):
    return lax.dot_general(a, b, dims, preferred_element_type=jnp.float32)


def noise_level(step_index):
    fraction = (step_index.astype(jnp.float32) + 1.0) / 1000.0
    return 3.0 * fraction / (1.0 + 2.0 * fraction)


def head_lanes(j):
    lane = lax.broadcasted_iota(jnp.int32, (1, LANES), 1)
    return (lane >= j * HEAD) & (lane < (j + 1) * HEAD)


def with_ones(values):
    return jnp.concatenate([values, jnp.ones_like(values)], axis=1)


def by_head(first, second):
    return jnp.where(head_lanes(0), first, second)


def image_rows(q, k, v_aug, e_ref):
    q = q * jnp.asarray(1.0 / math.sqrt(HEAD), jnp.bfloat16)
    outs, tops = [], []
    for j in range(2):
        qj = jnp.where(head_lanes(j), q, jnp.zeros_like(q))
        s = dot(qj, k, NT)
        top = jnp.max(s, axis=-1, keepdims=True)
        e = jnp.exp(s - top).astype(jnp.bfloat16)
        e_ref[j] = e
        outs.append(dot(e, v_aug))
        tops.append(top)
    return (
        by_head(outs[0][:, :LANES], outs[1][:, :LANES]),
        by_head(outs[0][:, LANES:], outs[1][:, LANES:]),
        by_head(tops[0], tops[1]),
    )


def place():
    seat, pair = lax.axis_index("seq"), lax.axis_index("fsdp")
    chip = seat // 2
    return seat, lax.rem(seat, 2), lax.rem(chip, 4), chip // 4, pair, lax.rem(pair, 4), pair // 4


def remote(src, dst, send_sem, recv_sem, seat, pair):
    return pltpu.make_async_remote_copy(
        src_ref=src, dst_ref=dst, send_sem=send_sem, recv_sem=recv_sem,
        device_id=(seat, pair), device_id_type=pl.DeviceIdType.MESH,
    )


def arrived(ref, sem):
    pltpu.make_async_copy(ref, ref, sem).wait()


ALTERNATE = (1, 3, 2, 0)


def window(
    len_ref, step_ref, error_ref, prompt_ref, gain_in_ref, gain_out_ref, target_ref, gate_in, up_in, down_in, ctx_in, out_in, q_in, k_in, v_in,
    loss_ref, gq_ref, gk_ref, gv_ref, ei_ref,
    gate_buf, up_buf, down_buf, ctx_buf, out_buf, normed, gate_acc, up_acc, part, sib, half, from_x, sum_x, from_z, state,
    ctx_pair, e_tile, o_all, z_all, m_all, tok, resid, grad, err_all,
    q_ref, k_ref, v_ref, kt_ref, vt_ref, et_ref, si_ref, st_ref, att_ref, g_ref, k_acc, v_acc, give_q, give_k, give_v,
    w_local, w_send, w_recv, qkv_local, qkv_send, qkv_recv, e_sem, stage_send, stage_recv, swap_send, swap_recv, g_recv,
    tok_local, tok_send, tok_recv, g_local, g_send, err_send, err_recv,
):
    seat, core, x, zh, pair, y, zl = place()
    other = seat + 1 - 2 * core
    low = lax.rem(seat, 8)
    up_y, down_y = lax.rem(y + 1, 4), lax.rem(y + 3, 4)
    far = lax.rem(y + 2, 4)
    base, base_p = zl * 4, (1 - zl) * 4
    partner = base_p + y

    barrier = pltpu.get_barrier_semaphore()

    @pl.loop(1, 32)
    def _(d):
        pl.semaphore_signal(barrier, inc=1, device_id=(lax.rem(seat + d, 32), pair), device_id_type=pl.DeviceIdType.MESH)

    for peer in (partner, base + up_y, base + down_y):
        pl.semaphore_signal(barrier, inc=1, device_id=(seat, peer), device_id_type=pl.DeviceIdType.MESH)
    pl.semaphore_wait(barrier, 34)

    def plain(buf):
        return lambda slot, rows=None: buf.at[slot] if rows is None else buf.at[slot, rows]

    def own_half(slot, rows=None):
        return out_buf.at[slot, core] if rows is None else out_buf.at[slot, core, rows]

    weights = (
        (gate_in, plain(gate_buf), 512), (up_in, plain(up_buf), 512), (down_in, plain(down_buf), 256),
        (ctx_in, plain(ctx_buf), 512), (out_in.at[core], own_half, 128),
    )
    early, late = (0, 1, 2), (3, 4)

    def send_weight(w, src, dst, sem, peer):
        remote(src, dst, w_send.at[w], w_recv.at[w, sem], seat, peer).start()

    def upper(w, slot):
        return weights[w][1](slot, pl.ds(0, weights[w][2] // 2))

    def lower(w, slot):
        return weights[w][1](slot, pl.ds(weights[w][2] // 2, weights[w][2] // 2))

    def send_own(w):
        src, at, _ = weights[w]
        send_weight(w, src, at(pair), 0, partner)
        send_weight(w, src, at(pair), 1, base + up_y)
        send_weight(w, src, at(pair), 2, base + down_y)
        pltpu.make_async_copy(src, at(pair), w_local.at[w]).start()

    def forward_near(w):
        at = weights[w][1]
        arrived(at(partner), w_recv.at[w, 0])
        send_weight(w, at(partner), at(partner), 3, base + up_y)
        send_weight(w, at(partner), at(partner), 4, base + down_y)
        arrived(at(base + down_y), w_recv.at[w, 1])
        send_weight(w, upper(w, base + down_y), upper(w, base + down_y), 5, base + up_y)
        arrived(at(base + up_y), w_recv.at[w, 2])
        send_weight(w, lower(w, base + up_y), lower(w, base + up_y), 6, base + down_y)

    def forward_partner(w):
        at = weights[w][1]
        arrived(at(base_p + down_y), w_recv.at[w, 3])
        send_weight(w, upper(w, base_p + down_y), upper(w, base_p + down_y), 7, base + up_y)
        arrived(at(base_p + up_y), w_recv.at[w, 4])
        send_weight(w, lower(w, base_p + up_y), lower(w, base_p + up_y), 8, base + down_y)

    def weight_ready(w):
        arrived(upper(w, base + far), w_recv.at[w, 5])
        arrived(lower(w, base + far), w_recv.at[w, 6])
        arrived(upper(w, base_p + far), w_recv.at[w, 7])
        arrived(lower(w, base_p + far), w_recv.at[w, 8])
        pltpu.make_async_copy(weights[w][0], weights[w][1](pair), w_local.at[w]).wait()

    for w in early:
        send_own(w)

    def token_rows(to):
        return pl.ds(pl.multiple_of(to * 64, 64), 64)

    def lanes_of(to):
        return pl.ds(pl.multiple_of((to // 2) * LANES, LANES), LANES)

    def stream_rows(to):
        return pl.ds(pl.multiple_of(lax.rem(to, 2) * 64, 64), 64)

    images = ((q_in, q_ref), (k_in, k_ref), (v_in, v_ref))

    def send_image(i):
        src, dst = images[i]

        @pl.loop(0, 8)
        def _(j):
            for dz in ALTERNATE:
                to = lax.rem(zh + dz, 4) * 8 + lax.rem(low + j, 8)

                def start(to=to):
                    remote(src.at[lax.rem(to, 2), :, lanes_of(to)], dst.at[token_rows(seat), :],
                           qkv_send.at[i], qkv_recv.at[i], to, pair).start()

                if dz:
                    start()
                else:
                    pl.when(j > 0)(start)

        pltpu.make_async_copy(src.at[core, :, lanes_of(seat)], dst.at[token_rows(seat), :], qkv_local.at[i]).start()

    total = jnp.zeros((PROMPT, 1), jnp.float32)
    for f in range(8):
        rows = prompt_ref[:, 512 * f:512 * (f + 1)].astype(jnp.float32)
        total = total + jnp.sum(rows * rows, axis=-1, keepdims=True)
    inv = lax.rsqrt(total * (1.0 / 4096) + norm_eps)
    for f in range(8):
        cols = slice(512 * f, 512 * (f + 1))
        normed[f] = (prompt_ref[:, cols].astype(jnp.float32) * inv * gain_in_ref[:, cols]).astype(jnp.bfloat16)

    for w in early:
        forward_near(w)
    for i in range(3):
        send_image(i)
        forward_partner(i)

    def images_ready():
        for i, (_, dst) in enumerate(images):
            arrived(dst.at[pl.ds(0, 31 * 64), :], qkv_recv.at[i])
            arrived(dst.at[pl.ds(0, 64), :], qkv_local.at[i])

    blocks = SEQ // ROWS

    def out_copy(b):
        slot = lax.rem(b, 2)
        return pltpu.make_async_copy(e_tile.at[slot], ei_ref.at[:, pl.ds(pl.multiple_of(b * ROWS, ROWS), ROWS), :], e_sem.at[slot])

    def image_blocks(start, stop):
        @pl.loop(start, stop)
        def _(b):
            @pl.when(b >= 2)
            def _():
                out_copy(b - 2).wait()

            rows = pl.ds(pl.multiple_of(b * ROWS, ROWS), ROWS)
            o, z, m = image_rows(q_ref[rows, :], k_ref[...], with_ones(v_ref[...]), e_tile.at[lax.rem(b, 2)])
            o_all[rows, :], z_all[rows, :], m_all[rows, :] = o, z, m
            out_copy(b).start()

    weight_ready(0)
    weight_ready(1)
    gate_acc[...] = jnp.zeros_like(gate_acc)
    up_acc[...] = jnp.zeros_like(up_acc)

    @pl.loop(0, 8)
    def _(f):
        gate_acc[...] += dot(normed[f], gate_buf[f])
        up_acc[...] += dot(normed[f], up_buf[f])

    hidden = (jax.nn.gelu(gate_acc[...], approximate=True) * up_acc[...]).astype(jnp.bfloat16)
    weight_ready(2)

    def part_block(f):
        part[f] = dot(hidden, down_buf[f]).astype(jnp.bfloat16)

    def two(c, start=0):
        return pl.ds(start + 2 * c, 2)

    def sems(c, stage):
        return stage_send.at[16 * c + stage], stage_recv.at[16 * c + stage]

    to_other = []
    for c in range(2):
        for i in range(2):
            part_block((1 - core) * 4 + 2 * c + i)
        to_other.append(remote(part.at[two(c, (1 - core) * 4)], sib.at[two(c)], *sems(c, 0), other, pair))
        to_other[c].start()
    for w in late:
        send_own(w)

    @pl.loop(0, 4)
    def _(i):
        part_block(core * 4 + i)

    def seat_of(zh_to, x_to):
        return (zh_to * 4 + x_to) * 2 + core

    def rows_x(at):
        return pl.ds(pl.multiple_of(at * 64, 64), 64)

    def rows_z(at):
        return pl.ds(pl.multiple_of(at * 16, 16), 16)

    def begin(make):
        copies = [make(d) for d in (1, 3, 2)]
        for copy in copies:
            copy.start()
        return copies

    def finish(copies):
        for copy in copies:
            copy.wait()

    mine = rows_z(x * 4 + zh)

    def reduce_x(c):
        to_other[c].wait()
        for i in (2 * c, 2 * c + 1):
            half[i] = (part[core * 4 + i].astype(jnp.float32) + sib[i].astype(jnp.float32)).astype(jnp.bfloat16)
        return begin(lambda d: remote(
            half.at[two(c), rows_x(lax.rem(x + d, 4)), :], from_x.at[d, two(c)], *sems(c, d), seat_of(zh, lax.rem(x + d, 4)), pair))

    def reduce_z(c, copies):
        finish(copies)
        for i in (2 * c, 2 * c + 1):
            acc = half[i, rows_x(x), :].astype(jnp.float32)
            for d in (1, 2, 3):
                acc = acc + from_x[d, i].astype(jnp.float32)
            sum_x[i] = acc.astype(jnp.bfloat16)
        return begin(lambda d: remote(
            sum_x.at[two(c), rows_z(lax.rem(zh + d, 4)), :], from_z.at[d, two(c)], *sems(c, 3 + d),
            seat_of(lax.rem(zh + d, 4), x), pair))

    def gather_z(c, copies):
        finish(copies)
        for i in (2 * c, 2 * c + 1):
            columns = pl.ds(pl.multiple_of(core * 2048 + i * 512, 512), 512)
            acc = prompt_ref[mine, columns].astype(jnp.float32) + sum_x[i, rows_z(zh), :].astype(jnp.float32)
            for d in (1, 2, 3):
                acc = acc + from_z[d, i].astype(jnp.float32)
            state[core * 4 + i, mine, :] = acc.astype(jnp.bfloat16)
        spot = state.at[two(c, core * 4), mine, :]
        return begin(lambda d: remote(spot, spot, *sems(c, 6 + d), seat_of(lax.rem(zh + d, 4), x), pair))

    def gather_x(c, copies):
        finish(copies)
        spot = state.at[two(c, core * 4), rows_x(x), :]
        return begin(lambda d: remote(spot, spot, *sems(c, 9 + d), seat_of(zh, lax.rem(x + d, 4)), pair))

    def gather_core(c, copies):
        finish(copies)
        spot = state.at[two(c, core * 4)]
        copy = remote(spot, spot, *sems(c, 13), other, pair)
        copy.start()
        return copy

    first = reduce_x(0)
    second = reduce_x(1)
    first = reduce_z(0, first)
    images_ready()
    image_blocks(0, 2)
    second = reduce_z(1, second)
    first = gather_z(0, first)
    for w in late:
        forward_near(w)
    image_blocks(2, 4)
    second = gather_z(1, second)
    first = gather_x(0, first)
    image_blocks(4, 5)
    second = gather_x(1, second)
    for w in late:
        forward_partner(w)
    image_blocks(5, 8)
    first = gather_core(0, first)
    second = gather_core(1, second)
    weight_ready(3)
    first.wait()
    second.wait()

    total = jnp.zeros((PROMPT, 1), jnp.float32)
    for f in range(8):
        rows = state[f].astype(jnp.float32)
        total = total + jnp.sum(rows * rows, axis=-1, keepdims=True)
    inv = lax.rsqrt(total * (1.0 / 4096) + norm_eps)
    context = jnp.zeros((PROMPT, LANES), jnp.float32)
    for f in range(8):
        encoded = (state[f].astype(jnp.float32) * inv * gain_out_ref[:, 512 * f:512 * (f + 1)]).astype(jnp.bfloat16)
        context = context + dot(encoded, ctx_buf[f])
    ctx_pair[core] = context.astype(jnp.bfloat16)
    text_swap = remote(ctx_pair.at[core], ctx_pair.at[core], stage_send.at[14], stage_recv.at[14], other, pair)
    text_swap.start()
    weight_ready(4)
    share = remote(out_buf.at[:, core], out_buf.at[:, core], stage_send.at[15], stage_recv.at[15], other, pair)
    share.start()
    text_swap.wait()
    first, second = ctx_pair[0].astype(jnp.float32), ctx_pair[1].astype(jnp.float32)
    kt_ref[...] = by_head(first, pltpu.roll(second, HEAD, 1)).astype(jnp.bfloat16)
    vt_ref[...] = by_head(pltpu.roll(first, HEAD, 1), second).astype(jnp.bfloat16)

    spot = tok.at[stream_rows(seat), lanes_of(seat)]
    kept = lax.broadcasted_iota(jnp.int32, (1, PROMPT), 1) < len_ref[0]

    @pl.loop(0, 2)
    def _(part_of):
        for dz in ALTERNATE:
            b = lax.rem(zh + dz, 4) * 2 + part_of
            rows = pl.ds(pl.multiple_of(b * ROWS, ROWS), ROWS)
            att, scale_i, scale_t = text_rows(
                q_ref[rows, :], kt_ref[...], with_ones(vt_ref[...]), kept, o_all[rows, :], z_all[rows, :], m_all[rows, :],
                et_ref.at[:, rows, :])
            att_ref[rows, :], si_ref[rows, :], st_ref[rows, :] = att, scale_i, scale_t
            for t in range(4):
                to = b * 4 + t

                def start(to=to):
                    remote(att_ref.at[token_rows(to), :], spot, tok_send, tok_recv, to, pair).start()

                def keep(to=to):
                    pltpu.make_async_copy(att_ref.at[token_rows(to), :], spot, tok_local).start()

                if dz:
                    start()
                else:
                    pl.when(to != seat)(start)
                    pl.when(to == seat)(keep)

    share.wait()
    arrived(spot, tok_local)
    arrived(att_ref.at[pl.ds(0, 31 * 64), :], tok_recv)

    acc = -target_ref[...].astype(jnp.float32)
    resid[...] = acc

    @pl.loop(0, 8)
    def _(f):
        columns = pl.ds(pl.multiple_of(f * 256, 256), 256)
        resid[...] += dot(tok[:, columns], out_buf[f].reshape(256, CH))

    halves = []
    for stream in range(2):
        rows = resid[64 * stream:64 * (stream + 1), :]
        halves.append(jnp.sum(jnp.sum(rows * rows, axis=1, keepdims=True), axis=0, keepdims=True))
    row = lax.broadcasted_iota(jnp.int32, (8, LANES), 0)
    err_all[seat] = jnp.where(row == 0, halves[0], jnp.where(row == 1, halves[1], 0.0))
    rounded = resid[...].astype(jnp.bfloat16)

    @pl.loop(0, 2)
    def _(part_of):
        for dz in ALTERNATE:
            n = lax.rem(zh + dz, 4) * 2 + lax.rem(low // 4 + part_of, 2)
            columns = pl.ds(pl.multiple_of(n * 256, 256), 256)
            grad[:, columns] = dot(rounded, out_buf[n].reshape(256, CH), NT).astype(jnp.bfloat16)
            for t in range(4):
                to = n * 4 + t

                def start(to=to):
                    remote(grad.at[stream_rows(to), lanes_of(to)], g_ref.at[token_rows(seat), :], g_send, g_recv.at[seat // 4], to, pair).start()
                    remote(err_all.at[seat], err_all.at[seat], err_send, err_recv, to, pair).start()

                def keep(to=to):
                    pltpu.make_async_copy(grad.at[stream_rows(to), lanes_of(to)], g_ref.at[token_rows(seat), :], g_local).start()

                if dz:
                    start()
                else:
                    pl.when(to != seat)(start)
                    pl.when(to == seat)(keep)

    def order(i):
        r = lax.rem(i, 4)
        return lax.rem(zh + lax.rem(1 + 2 * r + r // 2, 4), 4) * 2 + lax.rem(low // 4 + i // 4, 2)

    def in_copy(i):
        slot = lax.rem(i, 2)
        rows = pl.ds(pl.multiple_of(order(i) * ROWS, ROWS), ROWS)
        return pltpu.make_async_copy(ei_ref.at[:, rows, :], e_tile.at[slot], e_sem.at[slot])

    out_copy(blocks - 2).wait()
    out_copy(blocks - 1).wait()
    in_copy(0).start()
    in_copy(1).start()
    k_acc[...] = jnp.zeros_like(k_acc)
    v_acc[...] = jnp.zeros_like(v_acc)

    arrived(err_all.at[pl.ds(0, 31)], err_recv)
    mean_errors = jnp.sum(err_all[...], axis=0) * (1.0 / (SEQ * CH))
    error_gap = (mean_errors[0:1] - error_ref[:, 0:1]) - (mean_errors[1:2] - error_ref[:, 1:2])
    sigma = noise_level(jnp.full((1, LANES), step_ref[0], jnp.int32))
    logit = dpo_beta * sigma * error_gap
    loss_ref[...] = jnp.maximum(logit, 0.0) + jnp.log1p(jnp.exp(-jnp.abs(logit)))
    coef = sigma / (1.0 + jnp.exp(-logit)) * (1 - 2 * core).astype(jnp.float32)
    factor = coef * (1.0 / math.sqrt(HEAD))
    head_rows = pl.ds(pl.multiple_of(core * HEAD, HEAD), HEAD)
    other_rows = pl.ds(pl.multiple_of((1 - core) * HEAD, HEAD), HEAD)
    arrived(g_ref.at[pl.ds(0, 64), :], g_local)

    def give(i, staged, out, cols):
        return remote(staged.at[other_rows, cols], out.at[core, :, cols], swap_send.at[i], swap_recv.at[i], other, pair)

    every = pl.ds(0, SEQ)

    @pl.loop(0, blocks)
    def _(i):
        b = order(i)
        rows = pl.ds(pl.multiple_of(b * ROWS, ROWS), ROWS)

        @pl.when(b == seat // 4)
        def _():
            arrived(g_ref.at[pl.ds(0, 192), :], g_recv.at[b])

        @pl.when(b != seat // 4)
        def _():
            arrived(g_ref.at[pl.ds(0, 256), :], g_recv.at[b])

        in_copy(i).wait()
        grad_q = backward_rows(
            q_ref[rows, :], g_ref[rows, :], att_ref[rows, :], e_tile.at[lax.rem(i, 2)], et_ref.at[:, rows, :],
            si_ref[rows, :], st_ref[rows, :], k_ref[...], with_ones(v_ref[...]), kt_ref[...], with_ones(vt_ref[...]), k_acc, v_acc)

        @pl.when(i + 2 < blocks)
        def _():
            in_copy(i + 2).start()

        give_q[:, rows] = (grad_q * factor).T.astype(jnp.bfloat16)
        gq_ref[core, :, rows] = give_q[head_rows, rows]
        give(0, give_q, gq_ref, rows).start()

    give_k[...] = (k_acc[...] * factor[:, :1]).astype(jnp.bfloat16)
    give(1, give_k, gk_ref, every).start()
    give_v[...] = (v_acc[...] * coef[:, :1]).astype(jnp.bfloat16)
    give(2, give_v, gv_ref, every).start()
    gk_ref[core] = give_k[head_rows, :]
    gv_ref[core] = give_v[head_rows, :]
    for w, buf in enumerate((gate_buf, up_buf, down_buf, ctx_buf)):
        arrived(buf.at[pl.ds(0, 7)], w_send.at[w])
    arrived(out_buf.at[pl.ds(0, 7), 0], w_send.at[4])
    for i, (_, dst) in enumerate(images):
        arrived(dst.at[pl.ds(0, 31 * 64), :], qkv_send.at[i])
    arrived(g_ref.at[pl.ds(0, 31 * 64), :], g_send)
    arrived(att_ref.at[pl.ds(0, 31 * 64), :], tok_send)
    arrived(err_all.at[pl.ds(0, 31)], err_send)
    for i, (staged, out) in enumerate(((give_q, gq_ref), (give_k, gk_ref), (give_v, gv_ref))):
        give(i, staged, out, every).wait()


def text_rows(q, k, v_aug, kept, o, z, m, e_ref):
    q = q * jnp.asarray(1.0 / math.sqrt(HEAD), jnp.bfloat16)
    outs, tops = [], []
    for j in range(2):
        qj = jnp.where(head_lanes(j), q, jnp.zeros_like(q))
        s = jnp.where(kept, dot(qj, k, NT), -jnp.inf)
        top = jnp.maximum(m[:, j * HEAD:j * HEAD + 1], jnp.max(s, axis=-1, keepdims=True))
        e = jnp.exp(s - top).astype(jnp.bfloat16)
        e_ref[j] = e
        outs.append(dot(e, v_aug))
        tops.append(top)
    alpha = jnp.exp(m - by_head(tops[0], tops[1]))
    inv = 1.0 / (alpha * z + by_head(outs[0][:, LANES:], outs[1][:, LANES:]))
    o = alpha * o + by_head(outs[0][:, :LANES], outs[1][:, :LANES])
    return (o * inv).astype(jnp.bfloat16), alpha * inv, inv


def backward_rows(q, g, att, ei_ref, et_ref, si, st, k, v_aug, kt, vt_aug, k_acc, v_acc):
    g = g.astype(jnp.float32)
    prod = g * att.astype(jnp.float32)
    q_t = q.T
    lane = lax.broadcasted_iota(jnp.int32, (1, LANES), 1)
    grads = []
    for j in range(2):
        mine = head_lanes(j)
        gj = jnp.where(mine, g, 0.0)
        delta = jnp.sum(jnp.where(mine, prod, 0.0), axis=-1, keepdims=True)

        def scaled(scale):
            gs = (gj * scale).astype(jnp.bfloat16)
            d = -delta * scale
            hi = d.astype(jnp.bfloat16)
            low = (d - hi.astype(jnp.float32)).astype(jnp.bfloat16)
            extra = jnp.where(lane == 0, hi, jnp.where(lane == 1, low, jnp.zeros_like(hi)))
            return gs, jnp.concatenate([gs, extra], axis=1)

        gi, lhs_i = scaled(si[:, j * HEAD:j * HEAD + 1])
        _, lhs_t = scaled(st[:, j * HEAD:j * HEAD + 1])
        ei = ei_ref[j]
        ds = (ei.astype(jnp.float32) * dot(lhs_i, v_aug, NT)).astype(jnp.bfloat16)
        ds_t = (et_ref[j].astype(jnp.float32) * dot(lhs_t, vt_aug, NT)).astype(jnp.bfloat16)
        grads.append(dot(ds, k) + dot(ds_t, kt))
        rows = slice(j * HEAD, (j + 1) * HEAD)
        k_acc[rows, :] += dot(q_t[rows, :], ds)
        v_acc[rows, :] += dot(gi.T[rows, :], ei)
    return by_head(grads[0], grads[1])


def copy_out(q_in, k_in, v_in, q_ref, k_ref, v_ref, sem):
    copies = [
        pltpu.make_async_copy(src.at[stream], dst.at[stream], sem.at[2 * i + stream])
        for i, (src, dst) in enumerate(((q_in, q_ref), (k_in, k_ref), (v_in, v_ref)))
        for stream in range(2)
    ]
    for copy in copies:
        copy.start()
    for copy in copies:
        copy.wait()


def call_copy_out(*grads):
    anywhere = pl.BlockSpec(memory_space=pl.ANY)
    return pl.pallas_call(
        copy_out,
        in_specs=[anywhere] * 3,
        out_specs=[anywhere] * 3,
        out_shape=[jax.ShapeDtypeStruct((2, HEAD, SEQ), jnp.bfloat16)] * 3,
        scratch_shapes=[pltpu.SemaphoreType.DMA((6,))],
        name="copy_out",
    )(*grads)


def call_window(lengths, timesteps, ref_errors, prompt, gain_in, gain_out, target, gate, up, down, ctx, out, q, k, v):
    bf16, f32 = jnp.bfloat16, jnp.float32
    anywhere, vmem = pl.BlockSpec(memory_space=pl.ANY), pl.BlockSpec(memory_space=pltpu.VMEM)
    shape = jax.ShapeDtypeStruct
    dma, buf = pltpu.SemaphoreType.DMA, pltpu.VMEM
    grads = shape((2, HEAD, SEQ), bf16)
    return pl.pallas_call(
        window,
        in_specs=[pl.BlockSpec(memory_space=pltpu.SMEM)] * 2 + [vmem] * 5 + [anywhere] * 8,
        out_specs=[vmem] * 4 + [anywhere],
        out_shape=[shape((1, LANES), f32)] + [grads] * 3 + [shape((2, SEQ, SEQ), bf16)],
        scratch_shapes=[
            buf((8, 512, 256), bf16), buf((8, 512, 256), bf16), buf((8, 256, 512), bf16), buf((8, 512, 128), bf16),
            buf((8, 2, 128, CH), bf16),
            buf((8, PROMPT, 512), bf16), buf((PROMPT, 256), f32), buf((PROMPT, 256), f32),
            buf((8, PROMPT, 512), bf16), buf((4, PROMPT, 512), bf16), buf((4, PROMPT, 512), bf16),
            buf((4, 4, 64, 512), bf16), buf((4, 64, 512), bf16), buf((4, 4, 16, 512), bf16),
            buf((8, PROMPT, 512), bf16), buf((2, PROMPT, LANES), bf16), buf((2, 2, ROWS, SEQ), bf16),
            buf((SEQ, LANES), f32), buf((SEQ, LANES), f32), buf((SEQ, LANES), f32),
            buf((LANES, 2048), bf16), buf((LANES, CH), f32), buf((LANES, 2048), bf16), buf((32, 8, LANES), f32),
            buf((SEQ, LANES), bf16), buf((SEQ, LANES), bf16), buf((SEQ, LANES), bf16), buf((PROMPT, LANES), bf16),
            buf((PROMPT, LANES), bf16), buf((2, SEQ, PROMPT), bf16), buf((SEQ, LANES), f32), buf((SEQ, LANES), f32),
            buf((SEQ, LANES), bf16), buf((SEQ, LANES), bf16), buf((LANES, SEQ), f32), buf((LANES, SEQ), f32),
            buf((LANES, SEQ), bf16), buf((LANES, SEQ), bf16), buf((LANES, SEQ), bf16),
            dma((5,)), dma((5,)), dma((5, 9)), dma((3,)), dma((3,)), dma((3,)), dma((2,)), dma((32,)), dma((32,)),
            dma((3,)), dma((3,)), dma((8,)),
        ] + [dma] * 7,
        compiler_params=pltpu.CompilerParams(collective_id=0, has_side_effects=True, vmem_limit_bytes=54 * 1024 * 1024),
        name="window",
    )(lengths, timesteps, ref_errors, prompt, gain_in, gain_out, target, gate, up, down, ctx, out, q, k, v)


def on_device(prompt, lengths, timesteps, ref_errors, gain_ffn, w_in_gate, w_in_up, w_in_down, gain_final, w_context,
              image_q, image_k, image_v, w_out, target):
    loss, grad_q, grad_k, grad_v, _ = call_window(
        lengths, timesteps, ref_errors, prompt[0], gain_ffn[None], gain_final[None], target[0].reshape(LANES, CH),
        w_in_gate, w_in_up, w_in_down, w_context, w_out.reshape(2, 128, CH), image_q[0], image_k[0], image_v[0])
    return (loss[0, :1],) + tuple(jnp.transpose(grads, (0, 2, 1))[None] for grads in call_copy_out(grad_q, grad_k, grad_v))


def solution(mesh):
    return jax.shard_map(
        on_device,
        mesh=mesh,
        in_specs=(
            P("fsdp", None, None),
            P("fsdp"),
            P("fsdp"),
            P("fsdp", None),
            P(),
            P("fsdp", "seq"),
            P("fsdp", "seq"),
            P("seq", "fsdp"),
            P(),
            P("fsdp", "seq"),
            P("fsdp", None, "seq", None),
            P("fsdp", None, "seq", None),
            P("fsdp", None, "seq", None),
            P("fsdp", None),
            P("fsdp", None, "seq", None),
        ),
        out_specs=(
            P("fsdp"),
            P("fsdp", None, None, "seq"),
            P("fsdp", None, None, "seq"),
            P("fsdp", None, None, "seq"),
        ),
        check_vma=False,
    )
```

```python
import math

import jax
import jax.numpy as jnp
from jax import lax
from jax.experimental import pallas as pl
from jax.experimental.pallas import tpu as pltpu
from jax.sharding import PartitionSpec as P

PROMPT = 256
HEAD = 64
CH = 1280
SEQ = 2048
LANES = 128
ROWS = 256

dpo_beta = 20.0
norm_eps = 1e-06

NT = (((1,), (1,)), ((), ()))
NN = (((1,), (0,)), ((), ()))


def dot(a, b, dims=NN):
    return lax.dot_general(a, b, dims, preferred_element_type=jnp.float32)


def noise_level(step_index):
    fraction = (step_index.astype(jnp.float32) + 1.0) / 1000.0
    return 3.0 * fraction / (1.0 + 2.0 * fraction)


def head_lanes(j):
    lane = lax.broadcasted_iota(jnp.int32, (1, LANES), 1)
    return (lane >= j * HEAD) & (lane < (j + 1) * HEAD)


def with_ones(values):
    return jnp.concatenate([values, jnp.ones_like(values)], axis=1)


def by_head(first, second):
    return jnp.where(head_lanes(0), first, second)


def image_rows(q, k, v_aug, e_ref):
    q = q * jnp.asarray(1.0 / math.sqrt(HEAD), jnp.bfloat16)
    outs, tops = [], []
    for j in range(2):
        qj = jnp.where(head_lanes(j), q, jnp.zeros_like(q))
        s = dot(qj, k, NT)
        top = jnp.max(s, axis=-1, keepdims=True)
        e = jnp.exp(s - top).astype(jnp.bfloat16)
        e_ref[j] = e
        outs.append(dot(e, v_aug))
        tops.append(top)
    return (
        by_head(outs[0][:, :LANES], outs[1][:, :LANES]),
        by_head(outs[0][:, LANES:], outs[1][:, LANES:]),
        by_head(tops[0], tops[1]),
    )


def place():
    seat, pair = lax.axis_index("seq"), lax.axis_index("fsdp")
    chip = seat // 2
    return seat, lax.rem(seat, 2), lax.rem(chip, 4), chip // 4, pair, lax.rem(pair, 4), pair // 4


def remote(src, dst, send_sem, recv_sem, seat, pair):
    return pltpu.make_async_remote_copy(
        src_ref=src, dst_ref=dst, send_sem=send_sem, recv_sem=recv_sem,
        device_id=(seat, pair), device_id_type=pl.DeviceIdType.MESH,
    )


def arrived(ref, sem):
    pltpu.make_async_copy(ref, ref, sem).wait()


ALTERNATE = (1, 3, 2, 0)


def window(
    len_ref, step_ref, error_ref, prompt_ref, gain_in_ref, gain_out_ref, target_ref, gate_in, up_in, down_in, ctx_in, out_in, q_in, k_in, v_in,
    loss_ref, gq_ref, gk_ref, gv_ref, ei_ref,
    gate_buf, up_buf, down_buf, ctx_buf, out_buf, normed, gate_acc, up_acc, part, sib, half, from_x, sum_x, from_z, state,
    ctx_pair, e_tile, o_all, z_all, m_all, tok, resid, grad, err_all,
    q_ref, k_ref, v_ref, kt_ref, vt_ref, et_ref, si_ref, st_ref, att_ref, g_ref, k_acc, v_acc, give_q, give_k, give_v,
    w_local, w_send, w_recv, qkv_local, qkv_send, qkv_recv, e_sem, stage_send, stage_recv, swap_send, swap_recv, g_recv,
    tok_local, tok_send, tok_recv, g_local, g_send, err_send, err_recv,
):
    seat, core, x, zh, pair, y, zl = place()
    other = seat + 1 - 2 * core
    low = lax.rem(seat, 8)
    up_y, down_y = lax.rem(y + 1, 4), lax.rem(y + 3, 4)
    far = lax.rem(y + 2, 4)
    base, base_p = zl * 4, (1 - zl) * 4
    partner = base_p + y

    barrier = pltpu.get_barrier_semaphore()

    @pl.loop(1, 32)
    def _(d):
        pl.semaphore_signal(barrier, inc=1, device_id=(lax.rem(seat + d, 32), pair), device_id_type=pl.DeviceIdType.MESH)

    for peer in (partner, base + up_y, base + down_y):
        pl.semaphore_signal(barrier, inc=1, device_id=(seat, peer), device_id_type=pl.DeviceIdType.MESH)
    pl.semaphore_wait(barrier, 34)

    def plain(buf):
        return lambda slot, rows=None: buf.at[slot] if rows is None else buf.at[slot, rows]

    def own_half(slot, rows=None):
        return out_buf.at[slot, core] if rows is None else out_buf.at[slot, core, rows]

    weights = (
        (gate_in, plain(gate_buf), 512), (up_in, plain(up_buf), 512), (down_in, plain(down_buf), 256),
        (ctx_in, plain(ctx_buf), 512), (out_in.at[core], own_half, 128),
    )
    early, late = (0, 1, 2), (3, 4)

    def send_weight(w, src, dst, sem, peer):
        remote(src, dst, w_send.at[w], w_recv.at[w, sem], seat, peer).start()

    def upper(w, slot):
        return weights[w][1](slot, pl.ds(0, weights[w][2] // 2))

    def lower(w, slot):
        return weights[w][1](slot, pl.ds(weights[w][2] // 2, weights[w][2] // 2))

    def send_own(w):
        src, at, _ = weights[w]
        send_weight(w, src, at(pair), 0, partner)
        send_weight(w, src, at(pair), 1, base + up_y)
        send_weight(w, src, at(pair), 2, base + down_y)
        pltpu.make_async_copy(src, at(pair), w_local.at[w]).start()

    def forward_near(w):
        at = weights[w][1]
        arrived(at(partner), w_recv.at[w, 0])
        send_weight(w, at(partner), at(partner), 3, base + up_y)
        send_weight(w, at(partner), at(partner), 4, base + down_y)
        arrived(at(base + down_y), w_recv.at[w, 1])
        send_weight(w, upper(w, base + down_y), upper(w, base + down_y), 5, base + up_y)
        arrived(at(base + up_y), w_recv.at[w, 2])
        send_weight(w, lower(w, base + up_y), lower(w, base + up_y), 6, base + down_y)

    def forward_partner(w):
        at = weights[w][1]
        arrived(at(base_p + down_y), w_recv.at[w, 3])
        send_weight(w, upper(w, base_p + down_y), upper(w, base_p + down_y), 7, base + up_y)
        arrived(at(base_p + up_y), w_recv.at[w, 4])
        send_weight(w, lower(w, base_p + up_y), lower(w, base_p + up_y), 8, base + down_y)

    def weight_ready(w):
        arrived(upper(w, base + far), w_recv.at[w, 5])
        arrived(lower(w, base + far), w_recv.at[w, 6])
        arrived(upper(w, base_p + far), w_recv.at[w, 7])
        arrived(lower(w, base_p + far), w_recv.at[w, 8])
        pltpu.make_async_copy(weights[w][0], weights[w][1](pair), w_local.at[w]).wait()

    for w in early:
        send_own(w)

    def token_rows(to):
        return pl.ds(pl.multiple_of(to * 64, 64), 64)

    def lanes_of(to):
        return pl.ds(pl.multiple_of((to // 2) * LANES, LANES), LANES)

    def stream_rows(to):
        return pl.ds(pl.multiple_of(lax.rem(to, 2) * 64, 64), 64)

    images = ((q_in, q_ref), (k_in, k_ref), (v_in, v_ref))

    def send_image(i):
        src, dst = images[i]

        @pl.loop(0, 8)
        def _(j):
            for dz in ALTERNATE:
                to = lax.rem(zh + dz, 4) * 8 + lax.rem(low + j, 8)

                def start(to=to):
                    remote(src.at[lax.rem(to, 2), :, lanes_of(to)], dst.at[token_rows(seat), :],
                           qkv_send.at[i], qkv_recv.at[i], to, pair).start()

                if dz:
                    start()
                else:
                    pl.when(j > 0)(start)

        pltpu.make_async_copy(src.at[core, :, lanes_of(seat)], dst.at[token_rows(seat), :], qkv_local.at[i]).start()

    total = jnp.zeros((PROMPT, 1), jnp.float32)
    for f in range(8):
        rows = prompt_ref[:, 512 * f:512 * (f + 1)].astype(jnp.float32)
        total = total + jnp.sum(rows * rows, axis=-1, keepdims=True)
    inv = lax.rsqrt(total * (1.0 / 4096) + norm_eps)
    for f in range(8):
        cols = slice(512 * f, 512 * (f + 1))
        normed[f] = (prompt_ref[:, cols].astype(jnp.float32) * inv * gain_in_ref[:, cols]).astype(jnp.bfloat16)

    for w in early:
        forward_near(w)
    for i in range(3):
        send_image(i)
        forward_partner(i)

    def images_ready():
        for i, (_, dst) in enumerate(images):
            arrived(dst.at[pl.ds(0, 31 * 64), :], qkv_recv.at[i])
            arrived(dst.at[pl.ds(0, 64), :], qkv_local.at[i])

    blocks = SEQ // ROWS

    def out_copy(b):
        slot = lax.rem(b, 2)
        return pltpu.make_async_copy(e_tile.at[slot], ei_ref.at[:, pl.ds(pl.multiple_of(b * ROWS, ROWS), ROWS), :], e_sem.at[slot])

    def image_blocks(start, stop):
        @pl.loop(start, stop)
        def _(b):
            @pl.when(b >= 2)
            def _():
                out_copy(b - 2).wait()

            rows = pl.ds(pl.multiple_of(b * ROWS, ROWS), ROWS)
            o, z, m = image_rows(q_ref[rows, :], k_ref[...], with_ones(v_ref[...]), e_tile.at[lax.rem(b, 2)])
            o_all[rows, :], z_all[rows, :], m_all[rows, :] = o, z, m
            out_copy(b).start()

    weight_ready(0)
    weight_ready(1)
    gate_acc[...] = jnp.zeros_like(gate_acc)
    up_acc[...] = jnp.zeros_like(up_acc)

    @pl.loop(0, 8)
    def _(f):
        gate_acc[...] += dot(normed[f], gate_buf[f])
        up_acc[...] += dot(normed[f], up_buf[f])

    hidden = (jax.nn.gelu(gate_acc[...], approximate=True) * up_acc[...]).astype(jnp.bfloat16)
    weight_ready(2)

    def part_block(f):
        part[f] = dot(hidden, down_buf[f]).astype(jnp.bfloat16)

    def two(c, start=0):
        return pl.ds(start + 2 * c, 2)

    def sems(c, stage):
        return stage_send.at[16 * c + stage], stage_recv.at[16 * c + stage]

    to_other = []
    for c in range(2):
        for i in range(2):
            part_block((1 - core) * 4 + 2 * c + i)
        to_other.append(remote(part.at[two(c, (1 - core) * 4)], sib.at[two(c)], *sems(c, 0), other, pair))
        to_other[c].start()
    for w in late:
        send_own(w)

    @pl.loop(0, 4)
    def _(i):
        part_block(core * 4 + i)

    def seat_of(zh_to, x_to):
        return (zh_to * 4 + x_to) * 2 + core

    def rows_x(at):
        return pl.ds(pl.multiple_of(at * 64, 64), 64)

    def rows_z(at):
        return pl.ds(pl.multiple_of(at * 16, 16), 16)

    def begin(make):
        copies = [make(d) for d in (1, 3, 2)]
        for copy in copies:
            copy.start()
        return copies

    def finish(copies):
        for copy in copies:
            copy.wait()

    mine = rows_z(x * 4 + zh)

    def reduce_x(c):
        to_other[c].wait()
        for i in (2 * c, 2 * c + 1):
            half[i] = (part[core * 4 + i].astype(jnp.float32) + sib[i].astype(jnp.float32)).astype(jnp.bfloat16)
        return begin(lambda d: remote(
            half.at[two(c), rows_x(lax.rem(x + d, 4)), :], from_x.at[d, two(c)], *sems(c, d), seat_of(zh, lax.rem(x + d, 4)), pair))

    def reduce_z(c, copies):
        finish(copies)
        for i in (2 * c, 2 * c + 1):
            acc = half[i, rows_x(x), :].astype(jnp.float32)
            for d in (1, 2, 3):
                acc = acc + from_x[d, i].astype(jnp.float32)
            sum_x[i] = acc.astype(jnp.bfloat16)
        return begin(lambda d: remote(
            sum_x.at[two(c), rows_z(lax.rem(zh + d, 4)), :], from_z.at[d, two(c)], *sems(c, 3 + d),
            seat_of(lax.rem(zh + d, 4), x), pair))

    def gather_z(c, copies):
        finish(copies)
        for i in (2 * c, 2 * c + 1):
            columns = pl.ds(pl.multiple_of(core * 2048 + i * 512, 512), 512)
            acc = prompt_ref[mine, columns].astype(jnp.float32) + sum_x[i, rows_z(zh), :].astype(jnp.float32)
            for d in (1, 2, 3):
                acc = acc + from_z[d, i].astype(jnp.float32)
            state[core * 4 + i, mine, :] = acc.astype(jnp.bfloat16)
        spot = state.at[two(c, core * 4), mine, :]
        return begin(lambda d: remote(spot, spot, *sems(c, 6 + d), seat_of(lax.rem(zh + d, 4), x), pair))

    def gather_x(c, copies):
        finish(copies)
        spot = state.at[two(c, core * 4), rows_x(x), :]
        return begin(lambda d: remote(spot, spot, *sems(c, 9 + d), seat_of(zh, lax.rem(x + d, 4)), pair))

    def gather_core(c, copies):
        finish(copies)
        spot = state.at[two(c, core * 4)]
        copy = remote(spot, spot, *sems(c, 13), other, pair)
        copy.start()
        return copy

    first = reduce_x(0)
    second = reduce_x(1)
    first = reduce_z(0, first)
    images_ready()
    image_blocks(0, 2)
    second = reduce_z(1, second)
    first = gather_z(0, first)
    for w in late:
        forward_near(w)
    image_blocks(2, 4)
    second = gather_z(1, second)
    first = gather_x(0, first)
    image_blocks(4, 5)
    second = gather_x(1, second)
    for w in late:
        forward_partner(w)
    image_blocks(5, 8)
    first = gather_core(0, first)
    second = gather_core(1, second)
    weight_ready(3)
    first.wait()
    second.wait()

    total = jnp.zeros((PROMPT, 1), jnp.float32)
    for f in range(8):
        rows = state[f].astype(jnp.float32)
        total = total + jnp.sum(rows * rows, axis=-1, keepdims=True)
    inv = lax.rsqrt(total * (1.0 / 4096) + norm_eps)
    context = jnp.zeros((PROMPT, LANES), jnp.float32)
    for f in range(8):
        encoded = (state[f].astype(jnp.float32) * inv * gain_out_ref[:, 512 * f:512 * (f + 1)]).astype(jnp.bfloat16)
        context = context + dot(encoded, ctx_buf[f])
    ctx_pair[core] = context.astype(jnp.bfloat16)
    text_swap = remote(ctx_pair.at[core], ctx_pair.at[core], stage_send.at[14], stage_recv.at[14], other, pair)
    text_swap.start()
    weight_ready(4)
    share = remote(out_buf.at[:, core], out_buf.at[:, core], stage_send.at[15], stage_recv.at[15], other, pair)
    share.start()
    text_swap.wait()
    first, second = ctx_pair[0].astype(jnp.float32), ctx_pair[1].astype(jnp.float32)
    kt_ref[...] = by_head(first, pltpu.roll(second, HEAD, 1)).astype(jnp.bfloat16)
    vt_ref[...] = by_head(pltpu.roll(first, HEAD, 1), second).astype(jnp.bfloat16)

    spot = tok.at[stream_rows(seat), lanes_of(seat)]
    kept = lax.broadcasted_iota(jnp.int32, (1, PROMPT), 1) < len_ref[0]

    @pl.loop(0, 2)
    def _(part_of):
        for dz in ALTERNATE:
            b = lax.rem(zh + dz, 4) * 2 + part_of
            rows = pl.ds(pl.multiple_of(b * ROWS, ROWS), ROWS)
            att, scale_i, scale_t = text_rows(
                q_ref[rows, :], kt_ref[...], with_ones(vt_ref[...]), kept, o_all[rows, :], z_all[rows, :], m_all[rows, :],
                et_ref.at[:, rows, :])
            att_ref[rows, :], si_ref[rows, :], st_ref[rows, :] = att, scale_i, scale_t
            for t in range(4):
                to = b * 4 + t

                def start(to=to):
                    remote(att_ref.at[token_rows(to), :], spot, tok_send, tok_recv, to, pair).start()

                def keep(to=to):
                    pltpu.make_async_copy(att_ref.at[token_rows(to), :], spot, tok_local).start()

                if dz:
                    start()
                else:
                    pl.when(to != seat)(start)
                    pl.when(to == seat)(keep)

    share.wait()
    arrived(spot, tok_local)
    arrived(att_ref.at[pl.ds(0, 31 * 64), :], tok_recv)

    acc = -target_ref[...].astype(jnp.float32)
    resid[...] = acc

    @pl.loop(0, 8)
    def _(f):
        columns = pl.ds(pl.multiple_of(f * 256, 256), 256)
        resid[...] += dot(tok[:, columns], out_buf[f].reshape(256, CH))

    halves = []
    for stream in range(2):
        rows = resid[64 * stream:64 * (stream + 1), :]
        halves.append(jnp.sum(jnp.sum(rows * rows, axis=1, keepdims=True), axis=0, keepdims=True))
    row = lax.broadcasted_iota(jnp.int32, (8, LANES), 0)
    err_all[seat] = jnp.where(row == 0, halves[0], jnp.where(row == 1, halves[1], 0.0))
    rounded = resid[...].astype(jnp.bfloat16)

    @pl.loop(0, 2)
    def _(part_of):
        for dz in ALTERNATE:
            n = lax.rem(zh + dz, 4) * 2 + lax.rem(low // 4 + part_of, 2)
            columns = pl.ds(pl.multiple_of(n * 256, 256), 256)
            grad[:, columns] = dot(rounded, out_buf[n].reshape(256, CH), NT).astype(jnp.bfloat16)
            for t in range(4):
                to = n * 4 + t

                def start(to=to):
                    remote(grad.at[stream_rows(to), lanes_of(to)], g_ref.at[token_rows(seat), :], g_send, g_recv.at[seat // 4], to, pair).start()
                    remote(err_all.at[seat], err_all.at[seat], err_send, err_recv, to, pair).start()

                def keep(to=to):
                    pltpu.make_async_copy(grad.at[stream_rows(to), lanes_of(to)], g_ref.at[token_rows(seat), :], g_local).start()

                if dz:
                    start()
                else:
                    pl.when(to != seat)(start)
                    pl.when(to == seat)(keep)

    def order(i):
        r = lax.rem(i, 4)
        return lax.rem(zh + lax.rem(1 + 2 * r + r // 2, 4), 4) * 2 + lax.rem(low // 4 + i // 4, 2)

    def in_copy(i):
        slot = lax.rem(i, 2)
        rows = pl.ds(pl.multiple_of(order(i) * ROWS, ROWS), ROWS)
        return pltpu.make_async_copy(ei_ref.at[:, rows, :], e_tile.at[slot], e_sem.at[slot])

    out_copy(blocks - 2).wait()
    out_copy(blocks - 1).wait()
    in_copy(0).start()
    in_copy(1).start()
    k_acc[...] = jnp.zeros_like(k_acc)
    v_acc[...] = jnp.zeros_like(v_acc)

    arrived(err_all.at[pl.ds(0, 31)], err_recv)
    mean_errors = jnp.sum(err_all[...], axis=0) * (1.0 / (SEQ * CH))
    error_gap = (mean_errors[0:1] - error_ref[:, 0:1]) - (mean_errors[1:2] - error_ref[:, 1:2])
    sigma = noise_level(jnp.full((1, LANES), step_ref[0], jnp.int32))
    logit = dpo_beta * sigma * error_gap
    loss_ref[...] = jnp.maximum(logit, 0.0) + jnp.log1p(jnp.exp(-jnp.abs(logit)))
    coef = sigma / (1.0 + jnp.exp(-logit)) * (1 - 2 * core).astype(jnp.float32)
    factor = coef * (1.0 / math.sqrt(HEAD))
    head_rows = pl.ds(pl.multiple_of(core * HEAD, HEAD), HEAD)
    other_rows = pl.ds(pl.multiple_of((1 - core) * HEAD, HEAD), HEAD)
    arrived(g_ref.at[pl.ds(0, 64), :], g_local)

    def give(i, staged, out, cols):
        return remote(staged.at[other_rows, cols], out.at[core, :, cols], swap_send.at[i], swap_recv.at[i], other, pair)

    every = pl.ds(0, SEQ)

    @pl.loop(0, blocks)
    def _(i):
        b = order(i)
        rows = pl.ds(pl.multiple_of(b * ROWS, ROWS), ROWS)

        @pl.when(b == seat // 4)
        def _():
            arrived(g_ref.at[pl.ds(0, 192), :], g_recv.at[b])

        @pl.when(b != seat // 4)
        def _():
            arrived(g_ref.at[pl.ds(0, 256), :], g_recv.at[b])

        in_copy(i).wait()
        grad_q = backward_rows(
            q_ref[rows, :], g_ref[rows, :], att_ref[rows, :], e_tile.at[lax.rem(i, 2)], et_ref.at[:, rows, :],
            si_ref[rows, :], st_ref[rows, :], k_ref[...], with_ones(v_ref[...]), kt_ref[...], with_ones(vt_ref[...]), k_acc, v_acc)

        @pl.when(i + 2 < blocks)
        def _():
            in_copy(i + 2).start()

        give_q[:, rows] = (grad_q * factor).T.astype(jnp.bfloat16)
        gq_ref[core, :, rows] = give_q[head_rows, rows]
        give(0, give_q, gq_ref, rows).start()

    give_k[...] = (k_acc[...] * factor[:, :1]).astype(jnp.bfloat16)
    give(1, give_k, gk_ref, every).start()
    give_v[...] = (v_acc[...] * coef[:, :1]).astype(jnp.bfloat16)
    give(2, give_v, gv_ref, every).start()
    gk_ref[core] = give_k[head_rows, :]
    gv_ref[core] = give_v[head_rows, :]
    for w, buf in enumerate((gate_buf, up_buf, down_buf, ctx_buf)):
        arrived(buf.at[pl.ds(0, 7)], w_send.at[w])
    arrived(out_buf.at[pl.ds(0, 7), 0], w_send.at[4])
    for i, (_, dst) in enumerate(images):
        arrived(dst.at[pl.ds(0, 31 * 64), :], qkv_send.at[i])
    arrived(g_ref.at[pl.ds(0, 31 * 64), :], g_send)
    arrived(att_ref.at[pl.ds(0, 31 * 64), :], tok_send)
    arrived(err_all.at[pl.ds(0, 31)], err_send)
    for i, (staged, out) in enumerate(((give_q, gq_ref), (give_k, gk_ref), (give_v, gv_ref))):
        give(i, staged, out, every).wait()


def text_rows(q, k, v_aug, kept, o, z, m, e_ref):
    q = q * jnp.asarray(1.0 / math.sqrt(HEAD), jnp.bfloat16)
    outs, tops = [], []
    for j in range(2):
        qj = jnp.where(head_lanes(j), q, jnp.zeros_like(q))
        s = jnp.where(kept, dot(qj, k, NT), -jnp.inf)
        top = jnp.maximum(m[:, j * HEAD:j * HEAD + 1], jnp.max(s, axis=-1, keepdims=True))
        e = jnp.exp(s - top).astype(jnp.bfloat16)
        e_ref[j] = e
        outs.append(dot(e, v_aug))
        tops.append(top)
    alpha = jnp.exp(m - by_head(tops[0], tops[1]))
    inv = 1.0 / (alpha * z + by_head(outs[0][:, LANES:], outs[1][:, LANES:]))
    o = alpha * o + by_head(outs[0][:, :LANES], outs[1][:, :LANES])
    return (o * inv).astype(jnp.bfloat16), alpha * inv, inv


def backward_rows(q, g, att, ei_ref, et_ref, si, st, k, v_aug, kt, vt_aug, k_acc, v_acc):
    g = g.astype(jnp.float32)
    prod = g * att.astype(jnp.float32)
    q_t = q.T
    lane = lax.broadcasted_iota(jnp.int32, (1, LANES), 1)
    grads = []
    for j in range(2):
        mine = head_lanes(j)
        gj = jnp.where(mine, g, 0.0)
        delta = jnp.sum(jnp.where(mine, prod, 0.0), axis=-1, keepdims=True)

        def scaled(scale):
            gs = (gj * scale).astype(jnp.bfloat16)
            d = -delta * scale
            hi = d.astype(jnp.bfloat16)
            low = (d - hi.astype(jnp.float32)).astype(jnp.bfloat16)
            extra = jnp.where(lane == 0, hi, jnp.where(lane == 1, low, jnp.zeros_like(hi)))
            return gs, jnp.concatenate([gs, extra], axis=1)

        gi, lhs_i = scaled(si[:, j * HEAD:j * HEAD + 1])
        _, lhs_t = scaled(st[:, j * HEAD:j * HEAD + 1])
        ei = ei_ref[j]
        ds = (ei.astype(jnp.float32) * dot(lhs_i, v_aug, NT)).astype(jnp.bfloat16)
        ds_t = (et_ref[j].astype(jnp.float32) * dot(lhs_t, vt_aug, NT)).astype(jnp.bfloat16)
        grads.append(dot(ds, k) + dot(ds_t, kt))
        rows = slice(j * HEAD, (j + 1) * HEAD)
        k_acc[rows, :] += dot(q_t[rows, :], ds)
        v_acc[rows, :] += dot(gi.T[rows, :], ei)
    return by_head(grads[0], grads[1])


def copy_out(q_in, k_in, v_in, q_ref, k_ref, v_ref):
    q_ref[...], k_ref[...], v_ref[...] = q_in[...], k_in[...], v_in[...]


def call_copy_out(*grads):
    vmem = pl.BlockSpec(memory_space=pltpu.VMEM)
    return pl.pallas_call(
        copy_out,
        in_specs=[vmem] * 3,
        out_specs=[vmem] * 3,
        out_shape=[jax.ShapeDtypeStruct((2, HEAD, SEQ), jnp.bfloat16)] * 3,
        name="copy_out",
    )(*grads)


def call_window(lengths, timesteps, ref_errors, prompt, gain_in, gain_out, target, gate, up, down, ctx, out, q, k, v):
    bf16, f32 = jnp.bfloat16, jnp.float32
    anywhere, vmem = pl.BlockSpec(memory_space=pl.ANY), pl.BlockSpec(memory_space=pltpu.VMEM)
    shape = jax.ShapeDtypeStruct
    dma, buf = pltpu.SemaphoreType.DMA, pltpu.VMEM
    grads = shape((2, HEAD, SEQ), bf16)
    return pl.pallas_call(
        window,
        in_specs=[pl.BlockSpec(memory_space=pltpu.SMEM)] * 2 + [vmem] * 5 + [anywhere] * 8,
        out_specs=[vmem] * 4 + [anywhere],
        out_shape=[shape((1, LANES), f32)] + [grads] * 3 + [shape((2, SEQ, SEQ), bf16)],
        scratch_shapes=[
            buf((8, 512, 256), bf16), buf((8, 512, 256), bf16), buf((8, 256, 512), bf16), buf((8, 512, 128), bf16),
            buf((8, 2, 128, CH), bf16),
            buf((8, PROMPT, 512), bf16), buf((PROMPT, 256), f32), buf((PROMPT, 256), f32),
            buf((8, PROMPT, 512), bf16), buf((4, PROMPT, 512), bf16), buf((4, PROMPT, 512), bf16),
            buf((4, 4, 64, 512), bf16), buf((4, 64, 512), bf16), buf((4, 4, 16, 512), bf16),
            buf((8, PROMPT, 512), bf16), buf((2, PROMPT, LANES), bf16), buf((2, 2, ROWS, SEQ), bf16),
            buf((SEQ, LANES), f32), buf((SEQ, LANES), f32), buf((SEQ, LANES), f32),
            buf((LANES, 2048), bf16), buf((LANES, CH), f32), buf((LANES, 2048), bf16), buf((32, 8, LANES), f32),
            buf((SEQ, LANES), bf16), buf((SEQ, LANES), bf16), buf((SEQ, LANES), bf16), buf((PROMPT, LANES), bf16),
            buf((PROMPT, LANES), bf16), buf((2, SEQ, PROMPT), bf16), buf((SEQ, LANES), f32), buf((SEQ, LANES), f32),
            buf((SEQ, LANES), bf16), buf((SEQ, LANES), bf16), buf((LANES, SEQ), f32), buf((LANES, SEQ), f32),
            buf((LANES, SEQ), bf16), buf((LANES, SEQ), bf16), buf((LANES, SEQ), bf16),
            dma((5,)), dma((5,)), dma((5, 9)), dma((3,)), dma((3,)), dma((3,)), dma((2,)), dma((32,)), dma((32,)),
            dma((3,)), dma((3,)), dma((8,)),
        ] + [dma] * 7,
        compiler_params=pltpu.CompilerParams(collective_id=0, has_side_effects=True, vmem_limit_bytes=54 * 1024 * 1024),
        name="window",
    )(lengths, timesteps, ref_errors, prompt, gain_in, gain_out, target, gate, up, down, ctx, out, q, k, v)


def on_device(prompt, lengths, timesteps, ref_errors, gain_ffn, w_in_gate, w_in_up, w_in_down, gain_final, w_context,
              image_q, image_k, image_v, w_out, target):
    loss, grad_q, grad_k, grad_v, _ = call_window(
        lengths, timesteps, ref_errors, prompt[0], gain_ffn[None], gain_final[None], target[0].reshape(LANES, CH),
        w_in_gate, w_in_up, w_in_down, w_context, w_out.reshape(2, 128, CH), image_q[0], image_k[0], image_v[0])
    return (loss[0, :1],) + tuple(jnp.transpose(grads, (0, 2, 1))[None] for grads in call_copy_out(grad_q, grad_k, grad_v))


def solution(mesh):
    return jax.shard_map(
        on_device,
        mesh=mesh,
        in_specs=(
            P("fsdp", None, None),
            P("fsdp"),
            P("fsdp"),
            P("fsdp", None),
            P(),
            P("fsdp", "seq"),
            P("fsdp", "seq"),
            P("seq", "fsdp"),
            P(),
            P("fsdp", "seq"),
            P("fsdp", None, "seq", None),
            P("fsdp", None, "seq", None),
            P("fsdp", None, "seq", None),
            P("fsdp", None),
            P("fsdp", None, "seq", None),
        ),
        out_specs=(
            P("fsdp"),
            P("fsdp", None, None, "seq"),
            P("fsdp", None, None, "seq"),
            P("fsdp", None, None, "seq"),
        ),
        check_vma=False,
    )
```

```python
import math

import jax
import jax.numpy as jnp
from jax import lax
from jax.experimental import pallas as pl
from jax.experimental.pallas import tpu as pltpu
from jax.sharding import PartitionSpec as P

PROMPT = 256
HEAD = 64
CH = 1280
SEQ = 2048
LANES = 128
ROWS = 256

dpo_beta = 20.0
norm_eps = 1e-06

NT = (((1,), (1,)), ((), ()))
NN = (((1,), (0,)), ((), ()))


def dot(a, b, dims=NN):
    return lax.dot_general(a, b, dims, preferred_element_type=jnp.float32)


def noise_level(step_index):
    fraction = (step_index.astype(jnp.float32) + 1.0) / 1000.0
    return 3.0 * fraction / (1.0 + 2.0 * fraction)


def head_lanes(j):
    lane = lax.broadcasted_iota(jnp.int32, (1, LANES), 1)
    return (lane >= j * HEAD) & (lane < (j + 1) * HEAD)


def with_ones(values):
    return jnp.concatenate([values, jnp.ones_like(values)], axis=1)


def by_head(first, second):
    return jnp.where(head_lanes(0), first, second)


def image_rows(q, k, v_aug, e_ref):
    q = q * jnp.asarray(1.0 / math.sqrt(HEAD), jnp.bfloat16)
    outs, tops = [], []
    for j in range(2):
        qj = jnp.where(head_lanes(j), q, jnp.zeros_like(q))
        s = dot(qj, k, NT)
        top = jnp.max(s, axis=-1, keepdims=True)
        e = jnp.exp(s - top).astype(jnp.bfloat16)
        e_ref[j] = e
        outs.append(dot(e, v_aug))
        tops.append(top)
    return (
        by_head(outs[0][:, :LANES], outs[1][:, :LANES]),
        by_head(outs[0][:, LANES:], outs[1][:, LANES:]),
        by_head(tops[0], tops[1]),
    )


def place():
    seat, pair = lax.axis_index("seq"), lax.axis_index("fsdp")
    chip = seat // 2
    return seat, lax.rem(seat, 2), lax.rem(chip, 4), chip // 4, pair, lax.rem(pair, 4), pair // 4


def remote(src, dst, send_sem, recv_sem, seat, pair):
    return pltpu.make_async_remote_copy(
        src_ref=src, dst_ref=dst, send_sem=send_sem, recv_sem=recv_sem,
        device_id=(seat, pair), device_id_type=pl.DeviceIdType.MESH,
    )


def arrived(ref, sem):
    pltpu.make_async_copy(ref, ref, sem).wait()


ALTERNATE = (1, 3, 2, 0)


def window(
    len_ref, step_ref, error_ref, prompt_ref, gain_in_ref, gain_out_ref, target_ref, gate_in, up_in, down_in, ctx_in, out_in, q_in, k_in, v_in,
    loss_ref, gq_ref, gk_ref, gv_ref, ei_ref,
    gate_buf, up_buf, down_buf, ctx_buf, out_buf, normed, gate_acc, up_acc, part, sib, from_x, sum_x, from_z, state,
    ctx_pair, e_tile, o_all, z_all, m_all, tok, resid, grad, err_all,
    q_ref, k_ref, v_aug, kt_ref, vt_ref, et_ref, si_ref, st_ref, att_ref, g_ref, k_acc, v_acc, give_q, give_k, give_v,
    w_local, w_send, w_recv, qkv_local, qkv_send, qkv_recv, e_sem, stage_send, stage_recv, swap_send, swap_recv, g_recv,
    tok_local, tok_send, tok_recv, g_local, g_send, err_send, err_recv,
):
    seat, core, x, zh, pair, y, zl = place()
    other = seat + 1 - 2 * core
    low = lax.rem(seat, 8)
    up_y, down_y = lax.rem(y + 1, 4), lax.rem(y + 3, 4)
    far = lax.rem(y + 2, 4)
    base, base_p = zl * 4, (1 - zl) * 4
    partner = base_p + y

    v_aug[:, LANES:] = jnp.ones((SEQ, LANES), jnp.bfloat16)
    v_ref = v_aug.at[:, pl.ds(0, LANES)]
    barrier = pltpu.get_barrier_semaphore()

    @pl.loop(1, 32)
    def _(d):
        pl.semaphore_signal(barrier, inc=1, device_id=(lax.rem(seat + d, 32), pair), device_id_type=pl.DeviceIdType.MESH)

    for peer in (partner, base + up_y, base + down_y):
        pl.semaphore_signal(barrier, inc=1, device_id=(seat, peer), device_id_type=pl.DeviceIdType.MESH)
    pl.semaphore_wait(barrier, 34)

    def plain(buf):
        return lambda slot, rows=None: buf.at[slot] if rows is None else buf.at[slot, rows]

    def own_half(slot, rows=None):
        return out_buf.at[slot, core] if rows is None else out_buf.at[slot, core, rows]

    weights = (
        (gate_in, plain(gate_buf), 512), (up_in, plain(up_buf), 512), (down_in, plain(down_buf), 256),
        (ctx_in, plain(ctx_buf), 512), (out_in.at[core], own_half, 128),
    )
    early, late = (0, 1, 2), (3, 4)

    def send_weight(w, src, dst, sem, peer):
        remote(src, dst, w_send.at[w], w_recv.at[w, sem], seat, peer).start()

    def upper(w, slot):
        return weights[w][1](slot, pl.ds(0, weights[w][2] // 2))

    def lower(w, slot):
        return weights[w][1](slot, pl.ds(weights[w][2] // 2, weights[w][2] // 2))

    def send_own(w):
        src, at, _ = weights[w]
        send_weight(w, src, at(pair), 0, partner)
        send_weight(w, src, at(pair), 1, base + up_y)
        send_weight(w, src, at(pair), 2, base + down_y)
        pltpu.make_async_copy(src, at(pair), w_local.at[w]).start()

    def forward_near(w):
        at = weights[w][1]
        arrived(at(partner), w_recv.at[w, 0])
        send_weight(w, at(partner), at(partner), 3, base + up_y)
        send_weight(w, at(partner), at(partner), 4, base + down_y)
        arrived(at(base + down_y), w_recv.at[w, 1])
        send_weight(w, upper(w, base + down_y), upper(w, base + down_y), 5, base + up_y)
        arrived(at(base + up_y), w_recv.at[w, 2])
        send_weight(w, lower(w, base + up_y), lower(w, base + up_y), 6, base + down_y)

    def forward_partner(w):
        at = weights[w][1]
        arrived(at(base_p + down_y), w_recv.at[w, 3])
        send_weight(w, upper(w, base_p + down_y), upper(w, base_p + down_y), 7, base + up_y)
        arrived(at(base_p + up_y), w_recv.at[w, 4])
        send_weight(w, lower(w, base_p + up_y), lower(w, base_p + up_y), 8, base + down_y)

    def weight_ready(w):
        arrived(upper(w, base + far), w_recv.at[w, 5])
        arrived(lower(w, base + far), w_recv.at[w, 6])
        arrived(upper(w, base_p + far), w_recv.at[w, 7])
        arrived(lower(w, base_p + far), w_recv.at[w, 8])
        pltpu.make_async_copy(weights[w][0], weights[w][1](pair), w_local.at[w]).wait()

    for w in early:
        send_own(w)

    def token_rows(to):
        return pl.ds(pl.multiple_of(to * 64, 64), 64)

    def lanes_of(to):
        return pl.ds(pl.multiple_of((to // 2) * LANES, LANES), LANES)

    def stream_rows(to):
        return pl.ds(pl.multiple_of(lax.rem(to, 2) * 64, 64), 64)

    images = ((q_in, q_ref), (k_in, k_ref), (v_in, v_ref))

    def send_image(i):
        src, dst = images[i]

        @pl.loop(0, 8)
        def _(j):
            for dz in ALTERNATE:
                to = lax.rem(zh + dz, 4) * 8 + lax.rem(low + j, 8)

                def start(to=to):
                    remote(src.at[lax.rem(to, 2), :, lanes_of(to)], dst.at[token_rows(seat), :],
                           qkv_send.at[i], qkv_recv.at[i], to, pair).start()

                if dz:
                    start()
                else:
                    pl.when(j > 0)(start)

        pltpu.make_async_copy(src.at[core, :, lanes_of(seat)], dst.at[token_rows(seat), :], qkv_local.at[i]).start()

    total = jnp.zeros((PROMPT, 1), jnp.float32)
    for f in range(8):
        rows = prompt_ref[:, 512 * f:512 * (f + 1)].astype(jnp.float32)
        total = total + jnp.sum(rows * rows, axis=-1, keepdims=True)
    inv = lax.rsqrt(total * (1.0 / 4096) + norm_eps)
    for f in range(8):
        cols = slice(512 * f, 512 * (f + 1))
        normed[f] = (prompt_ref[:, cols].astype(jnp.float32) * inv * gain_in_ref[:, cols]).astype(jnp.bfloat16)

    for w in early:
        forward_near(w)
    for i in range(3):
        send_image(i)
        forward_partner(i)

    def images_ready():
        for i, (_, dst) in enumerate(images):
            arrived(dst.at[pl.ds(0, 31 * 64), :], qkv_recv.at[i])
            arrived(dst.at[pl.ds(0, 64), :], qkv_local.at[i])

    blocks = SEQ // ROWS

    def out_copy(b):
        slot = lax.rem(b, 2)
        return pltpu.make_async_copy(e_tile.at[slot], ei_ref.at[:, pl.ds(pl.multiple_of(b * ROWS, ROWS), ROWS), :], e_sem.at[slot])

    def image_blocks(start, stop):
        @pl.loop(start, stop)
        def _(b):
            @pl.when(b >= 2)
            def _():
                out_copy(b - 2).wait()

            rows = pl.ds(pl.multiple_of(b * ROWS, ROWS), ROWS)
            o, z, m = image_rows(q_ref[rows, :], k_ref[...], v_aug[...], e_tile.at[lax.rem(b, 2)])
            o_all[rows, :], z_all[rows, :], m_all[rows, :] = o, z, m
            out_copy(b).start()

    weight_ready(0)
    weight_ready(1)
    gate_acc[...] = jnp.zeros_like(gate_acc)
    up_acc[...] = jnp.zeros_like(up_acc)

    @pl.loop(0, 8)
    def _(f):
        gate_acc[...] += dot(normed[f], gate_buf[f])
        up_acc[...] += dot(normed[f], up_buf[f])

    hidden = (jax.nn.gelu(gate_acc[...], approximate=True) * up_acc[...]).astype(jnp.bfloat16)
    weight_ready(2)

    def part_block(f):
        part[f] = dot(hidden, down_buf[f]).astype(jnp.bfloat16)

    def two(c, start=0):
        return pl.ds(start + 2 * c, 2)

    def sems(c, stage):
        return stage_send.at[16 * c + stage], stage_recv.at[16 * c + stage]

    to_other = []
    for c in range(2):
        for i in range(2):
            part_block((1 - core) * 4 + 2 * c + i)
        to_other.append(remote(part.at[two(c, (1 - core) * 4)], sib.at[two(c)], *sems(c, 0), other, pair))
        to_other[c].start()
    for w in late:
        send_own(w)

    @pl.loop(0, 4)
    def _(i):
        part_block(core * 4 + i)

    def seat_of(zh_to, x_to):
        return (zh_to * 4 + x_to) * 2 + core

    def rows_x(at):
        return pl.ds(pl.multiple_of(at * 64, 64), 64)

    def rows_z(at):
        return pl.ds(pl.multiple_of(at * 16, 16), 16)

    def begin(make):
        copies = [make(d) for d in (1, 3, 2)]
        for copy in copies:
            copy.start()
        return copies

    def finish(copies):
        for copy in copies:
            copy.wait()

    mine = rows_z(x * 4 + zh)

    def reduce_x(c):
        to_other[c].wait()
        for i in (2 * c, 2 * c + 1):
            sib[i] = (part[core * 4 + i].astype(jnp.float32) + sib[i].astype(jnp.float32)).astype(jnp.bfloat16)
        return begin(lambda d: remote(
            sib.at[two(c), rows_x(lax.rem(x + d, 4)), :], from_x.at[d, two(c)], *sems(c, d), seat_of(zh, lax.rem(x + d, 4)), pair))

    def reduce_z(c, copies):
        finish(copies)
        for i in (2 * c, 2 * c + 1):
            acc = sib[i, rows_x(x), :].astype(jnp.float32)
            for d in (1, 2, 3):
                acc = acc + from_x[d, i].astype(jnp.float32)
            sum_x[i] = acc.astype(jnp.bfloat16)
        return begin(lambda d: remote(
            sum_x.at[two(c), rows_z(lax.rem(zh + d, 4)), :], from_z.at[d, two(c)], *sems(c, 3 + d),
            seat_of(lax.rem(zh + d, 4), x), pair))

    def gather_z(c, copies):
        finish(copies)
        for i in (2 * c, 2 * c + 1):
            columns = pl.ds(pl.multiple_of(core * 2048 + i * 512, 512), 512)
            acc = prompt_ref[mine, columns].astype(jnp.float32) + sum_x[i, rows_z(zh), :].astype(jnp.float32)
            for d in (1, 2, 3):
                acc = acc + from_z[d, i].astype(jnp.float32)
            state[core * 4 + i, mine, :] = acc.astype(jnp.bfloat16)
        spot = state.at[two(c, core * 4), mine, :]
        return begin(lambda d: remote(spot, spot, *sems(c, 6 + d), seat_of(lax.rem(zh + d, 4), x), pair))

    def gather_x(c, copies):
        finish(copies)
        spot = state.at[two(c, core * 4), rows_x(x), :]
        return begin(lambda d: remote(spot, spot, *sems(c, 9 + d), seat_of(zh, lax.rem(x + d, 4)), pair))

    def gather_core(c, copies):
        finish(copies)
        spot = state.at[two(c, core * 4)]
        copy = remote(spot, spot, *sems(c, 13), other, pair)
        copy.start()
        return copy

    first = reduce_x(0)
    second = reduce_x(1)
    first = reduce_z(0, first)
    images_ready()
    image_blocks(0, 2)
    second = reduce_z(1, second)
    first = gather_z(0, first)
    for w in late:
        forward_near(w)
    image_blocks(2, 4)
    second = gather_z(1, second)
    first = gather_x(0, first)
    image_blocks(4, 5)
    second = gather_x(1, second)
    for w in late:
        forward_partner(w)
    image_blocks(5, 8)
    first = gather_core(0, first)
    second = gather_core(1, second)
    weight_ready(3)
    first.wait()
    second.wait()

    total = jnp.zeros((PROMPT, 1), jnp.float32)
    for f in range(8):
        rows = state[f].astype(jnp.float32)
        total = total + jnp.sum(rows * rows, axis=-1, keepdims=True)
    inv = lax.rsqrt(total * (1.0 / 4096) + norm_eps)
    context = jnp.zeros((PROMPT, LANES), jnp.float32)
    for f in range(8):
        encoded = (state[f].astype(jnp.float32) * inv * gain_out_ref[:, 512 * f:512 * (f + 1)]).astype(jnp.bfloat16)
        context = context + dot(encoded, ctx_buf[f])
    ctx_pair[core] = context.astype(jnp.bfloat16)
    text_swap = remote(ctx_pair.at[core], ctx_pair.at[core], stage_send.at[14], stage_recv.at[14], other, pair)
    text_swap.start()
    weight_ready(4)
    share = remote(out_buf.at[:, core], out_buf.at[:, core], stage_send.at[15], stage_recv.at[15], other, pair)
    share.start()
    text_swap.wait()
    first, second = ctx_pair[0].astype(jnp.float32), ctx_pair[1].astype(jnp.float32)
    kt_ref[...] = by_head(first, pltpu.roll(second, HEAD, 1)).astype(jnp.bfloat16)
    vt_ref[...] = by_head(pltpu.roll(first, HEAD, 1), second).astype(jnp.bfloat16)

    def order(i):
        r = lax.rem(i, 4)
        return lax.rem(zh + lax.rem(1 + 2 * r + r // 2, 4), 4) * 2 + lax.rem(low // 4 + i // 4, 2)

    spot = tok.at[stream_rows(seat), lanes_of(seat)]
    kept = lax.broadcasted_iota(jnp.int32, (1, PROMPT), 1) < len_ref[0]

    @pl.loop(0, 2)
    def _(part_of):
        for dz in ALTERNATE:
            b = lax.rem(zh + dz, 4) * 2 + lax.rem(low // 4 + part_of, 2)
            rows = pl.ds(pl.multiple_of(b * ROWS, ROWS), ROWS)
            att, scale_i, scale_t = text_rows(
                q_ref[rows, :], kt_ref[...], with_ones(vt_ref[...]), kept, o_all[rows, :], z_all[rows, :], m_all[rows, :],
                et_ref.at[:, rows, :])
            att_ref[rows, :], si_ref[rows, :], st_ref[rows, :] = att, scale_i, scale_t
            for t in range(4):
                to = b * 4 + t

                def start(to=to):
                    remote(att_ref.at[token_rows(to), :], spot, tok_send, tok_recv.at[seat // 4], to, pair).start()

                def keep(to=to):
                    pltpu.make_async_copy(att_ref.at[token_rows(to), :], spot, tok_local).start()

                if dz:
                    start()
                else:
                    pl.when(to != seat)(start)
                    pl.when(to == seat)(keep)

    def block_arrived(ref, sem, b):
        @pl.when(b == seat // 4)
        def _():
            arrived(ref.at[pl.ds(0, 192), :], sem.at[b])

        @pl.when(b != seat // 4)
        def _():
            arrived(ref.at[pl.ds(0, 256), :], sem.at[b])

    resid[...] = -target_ref[...].astype(jnp.float32)
    share.wait()
    arrived(spot, tok_local)

    @pl.loop(0, 8)
    def _(i):
        b = order(i)
        block_arrived(att_ref, tok_recv, b)
        resid[...] += dot(tok[:, pl.ds(pl.multiple_of(b * 256, 256), 256)], out_buf[b].reshape(256, CH))

    halves = []
    for stream in range(2):
        rows = resid[64 * stream:64 * (stream + 1), :]
        halves.append(jnp.sum(jnp.sum(rows * rows, axis=1, keepdims=True), axis=0, keepdims=True))
    row = lax.broadcasted_iota(jnp.int32, (8, LANES), 0)
    err_all[seat] = jnp.where(row == 0, halves[0], jnp.where(row == 1, halves[1], 0.0))
    rounded = resid[...].astype(jnp.bfloat16)

    @pl.loop(0, 2)
    def _(part_of):
        for dz in ALTERNATE:
            n = lax.rem(zh + dz, 4) * 2 + lax.rem(low // 4 + part_of, 2)
            columns = pl.ds(pl.multiple_of(n * 256, 256), 256)
            grad[:, columns] = dot(rounded, out_buf[n].reshape(256, CH), NT).astype(jnp.bfloat16)
            for t in range(4):
                to = n * 4 + t

                def start(to=to):
                    remote(grad.at[stream_rows(to), lanes_of(to)], g_ref.at[token_rows(seat), :], g_send, g_recv.at[seat // 4], to, pair).start()
                    remote(err_all.at[seat], err_all.at[seat], err_send, err_recv, to, pair).start()

                def keep(to=to):
                    pltpu.make_async_copy(grad.at[stream_rows(to), lanes_of(to)], g_ref.at[token_rows(seat), :], g_local).start()

                if dz:
                    start()
                else:
                    pl.when(to != seat)(start)
                    pl.when(to == seat)(keep)

    def in_copy(i):
        slot = lax.rem(i, 2)
        rows = pl.ds(pl.multiple_of(order(i) * ROWS, ROWS), ROWS)
        return pltpu.make_async_copy(ei_ref.at[:, rows, :], e_tile.at[slot], e_sem.at[slot])

    out_copy(blocks - 2).wait()
    out_copy(blocks - 1).wait()
    in_copy(0).start()
    in_copy(1).start()
    k_acc[...] = jnp.zeros_like(k_acc)
    v_acc[...] = jnp.zeros_like(v_acc)

    arrived(err_all.at[pl.ds(0, 31)], err_recv)
    mean_errors = jnp.sum(err_all[...], axis=0) * (1.0 / (SEQ * CH))
    error_gap = (mean_errors[0:1] - error_ref[:, 0:1]) - (mean_errors[1:2] - error_ref[:, 1:2])
    sigma = noise_level(jnp.full((1, LANES), step_ref[0], jnp.int32))
    logit = dpo_beta * sigma * error_gap
    loss_ref[...] = jnp.maximum(logit, 0.0) + jnp.log1p(jnp.exp(-jnp.abs(logit)))
    coef = sigma / (1.0 + jnp.exp(-logit)) * (1 - 2 * core).astype(jnp.float32)
    factor = coef * (1.0 / math.sqrt(HEAD))
    head_rows = pl.ds(pl.multiple_of(core * HEAD, HEAD), HEAD)
    other_rows = pl.ds(pl.multiple_of((1 - core) * HEAD, HEAD), HEAD)
    arrived(g_ref.at[pl.ds(0, 64), :], g_local)

    def give(i, staged, out, cols):
        return remote(staged.at[other_rows, cols], out.at[core, :, cols], swap_send.at[i], swap_recv.at[i], other, pair)

    every = pl.ds(0, SEQ)

    @pl.loop(0, blocks)
    def _(i):
        b = order(i)
        rows = pl.ds(pl.multiple_of(b * ROWS, ROWS), ROWS)

        block_arrived(g_ref, g_recv, b)
        in_copy(i).wait()
        grad_q = backward_rows(
            q_ref[rows, :], g_ref[rows, :], att_ref[rows, :], e_tile.at[lax.rem(i, 2)], et_ref.at[:, rows, :],
            si_ref[rows, :], st_ref[rows, :], k_ref[...], v_aug[...], kt_ref[...], with_ones(vt_ref[...]), k_acc, v_acc)

        @pl.when(i + 2 < blocks)
        def _():
            in_copy(i + 2).start()

        give_q[:, rows] = (grad_q * factor).T.astype(jnp.bfloat16)
        gq_ref[core, :, rows] = give_q[head_rows, rows]
        give(0, give_q, gq_ref, rows).start()

    give_k[...] = (k_acc[...] * factor[:, :1]).astype(jnp.bfloat16)
    give(1, give_k, gk_ref, every).start()
    give_v[...] = (v_acc[...] * coef[:, :1]).astype(jnp.bfloat16)
    give(2, give_v, gv_ref, every).start()
    gk_ref[core] = give_k[head_rows, :]
    gv_ref[core] = give_v[head_rows, :]
    for w, buf in enumerate((gate_buf, up_buf, down_buf, ctx_buf)):
        arrived(buf.at[pl.ds(0, 7)], w_send.at[w])
    arrived(out_buf.at[pl.ds(0, 7), 0], w_send.at[4])
    for i, (_, dst) in enumerate(images):
        arrived(dst.at[pl.ds(0, 31 * 64), :], qkv_send.at[i])
    arrived(g_ref.at[pl.ds(0, 31 * 64), :], g_send)
    arrived(att_ref.at[pl.ds(0, 31 * 64), :], tok_send)
    arrived(err_all.at[pl.ds(0, 31)], err_send)
    for i, (staged, out) in enumerate(((give_q, gq_ref), (give_k, gk_ref), (give_v, gv_ref))):
        give(i, staged, out, every).wait()


def text_rows(q, k, v_aug, kept, o, z, m, e_ref):
    q = q * jnp.asarray(1.0 / math.sqrt(HEAD), jnp.bfloat16)
    outs, tops = [], []
    for j in range(2):
        qj = jnp.where(head_lanes(j), q, jnp.zeros_like(q))
        s = jnp.where(kept, dot(qj, k, NT), -jnp.inf)
        top = jnp.maximum(m[:, j * HEAD:j * HEAD + 1], jnp.max(s, axis=-1, keepdims=True))
        e = jnp.exp(s - top).astype(jnp.bfloat16)
        e_ref[j] = e
        outs.append(dot(e, v_aug))
        tops.append(top)
    alpha = jnp.exp(m - by_head(tops[0], tops[1]))
    inv = 1.0 / (alpha * z + by_head(outs[0][:, LANES:], outs[1][:, LANES:]))
    o = alpha * o + by_head(outs[0][:, :LANES], outs[1][:, :LANES])
    return (o * inv).astype(jnp.bfloat16), alpha * inv, inv


def backward_rows(q, g, att, ei_ref, et_ref, si, st, k, v_aug, kt, vt_aug, k_acc, v_acc):
    g = g.astype(jnp.float32)
    prod = g * att.astype(jnp.float32)
    q_t = q.T
    lane = lax.broadcasted_iota(jnp.int32, (1, LANES), 1)
    grads = []
    for j in range(2):
        mine = head_lanes(j)
        gj = jnp.where(mine, g, 0.0)
        delta = jnp.sum(jnp.where(mine, prod, 0.0), axis=-1, keepdims=True)

        def scaled(scale):
            gs = (gj * scale).astype(jnp.bfloat16)
            d = -delta * scale
            hi = d.astype(jnp.bfloat16)
            low = (d - hi.astype(jnp.float32)).astype(jnp.bfloat16)
            extra = jnp.where(lane == 0, hi, jnp.where(lane == 1, low, jnp.zeros_like(hi)))
            return gs, jnp.concatenate([gs, extra], axis=1)

        gi, lhs_i = scaled(si[:, j * HEAD:j * HEAD + 1])
        _, lhs_t = scaled(st[:, j * HEAD:j * HEAD + 1])
        ei = ei_ref[j]
        ds = ei * dot(lhs_i, v_aug, NT).astype(jnp.bfloat16)
        ds_t = et_ref[j] * dot(lhs_t, vt_aug, NT).astype(jnp.bfloat16)
        grads.append(dot(ds, k) + dot(ds_t, kt))
        rows = slice(j * HEAD, (j + 1) * HEAD)
        k_acc[rows, :] += dot(q_t[rows, :], ds)
        v_acc[rows, :] += dot(gi.T[rows, :], ei)
    return by_head(grads[0], grads[1])


def copy_out(q_in, k_in, v_in, q_ref, k_ref, v_ref):
    q_ref[...], k_ref[...], v_ref[...] = q_in[...], k_in[...], v_in[...]


def call_copy_out(*grads):
    vmem = pl.BlockSpec(memory_space=pltpu.VMEM)
    return pl.pallas_call(
        copy_out,
        in_specs=[vmem] * 3,
        out_specs=[vmem] * 3,
        out_shape=[jax.ShapeDtypeStruct((2, HEAD, SEQ), jnp.bfloat16)] * 3,
        name="copy_out",
    )(*grads)


def call_window(lengths, timesteps, ref_errors, prompt, gain_in, gain_out, target, gate, up, down, ctx, out, q, k, v):
    bf16, f32 = jnp.bfloat16, jnp.float32
    anywhere, vmem = pl.BlockSpec(memory_space=pl.ANY), pl.BlockSpec(memory_space=pltpu.VMEM)
    shape = jax.ShapeDtypeStruct
    dma, buf = pltpu.SemaphoreType.DMA, pltpu.VMEM
    grads = shape((2, HEAD, SEQ), bf16)
    return pl.pallas_call(
        window,
        in_specs=[pl.BlockSpec(memory_space=pltpu.SMEM)] * 2 + [vmem] * 5 + [anywhere] * 8,
        out_specs=[vmem] * 4 + [anywhere],
        out_shape=[shape((1, LANES), f32)] + [grads] * 3 + [shape((2, SEQ, SEQ), bf16)],
        scratch_shapes=[
            buf((8, 512, 256), bf16), buf((8, 512, 256), bf16), buf((8, 256, 512), bf16), buf((8, 512, 128), bf16),
            buf((8, 2, 128, CH), bf16),
            buf((8, PROMPT, 512), bf16), buf((PROMPT, 256), f32), buf((PROMPT, 256), f32),
            buf((8, PROMPT, 512), bf16), buf((4, PROMPT, 512), bf16),
            buf((4, 4, 64, 512), bf16), buf((4, 64, 512), bf16), buf((4, 4, 16, 512), bf16),
            buf((8, PROMPT, 512), bf16), buf((2, PROMPT, LANES), bf16), buf((2, 2, ROWS, SEQ), bf16),
            buf((SEQ, LANES), f32), buf((SEQ, LANES), f32), buf((SEQ, LANES), f32),
            buf((LANES, 2048), bf16), buf((LANES, CH), f32), buf((LANES, 2048), bf16), buf((32, 8, LANES), f32),
            buf((SEQ, LANES), bf16), buf((SEQ, LANES), bf16), buf((SEQ, 2 * LANES), bf16), buf((PROMPT, LANES), bf16),
            buf((PROMPT, LANES), bf16), buf((2, SEQ, PROMPT), bf16), buf((SEQ, LANES), f32), buf((SEQ, LANES), f32),
            buf((SEQ, LANES), bf16), buf((SEQ, LANES), bf16), buf((LANES, SEQ), f32), buf((LANES, SEQ), f32),
            buf((LANES, SEQ), bf16), buf((LANES, SEQ), bf16), buf((LANES, SEQ), bf16),
            dma((5,)), dma((5,)), dma((5, 9)), dma((3,)), dma((3,)), dma((3,)), dma((2,)), dma((32,)), dma((32,)),
            dma((3,)), dma((3,)), dma((8,)), dma, dma, dma((8,)),
        ] + [dma] * 4,
        compiler_params=pltpu.CompilerParams(collective_id=0, has_side_effects=True, vmem_limit_bytes=61 * 1024 * 1024),
        name="window",
    )(lengths, timesteps, ref_errors, prompt, gain_in, gain_out, target, gate, up, down, ctx, out, q, k, v)


def on_device(prompt, lengths, timesteps, ref_errors, gain_ffn, w_in_gate, w_in_up, w_in_down, gain_final, w_context,
              image_q, image_k, image_v, w_out, target):
    loss, grad_q, grad_k, grad_v, _ = call_window(
        lengths, timesteps, ref_errors, prompt[0], gain_ffn[None], gain_final[None], target[0].reshape(LANES, CH),
        w_in_gate, w_in_up, w_in_down, w_context, w_out.reshape(2, 128, CH), image_q[0], image_k[0], image_v[0])
    return (loss[0, :1],) + tuple(jnp.transpose(grads, (0, 2, 1))[None] for grads in call_copy_out(grad_q, grad_k, grad_v))


def solution(mesh):
    return jax.shard_map(
        on_device,
        mesh=mesh,
        in_specs=(
            P("fsdp", None, None),
            P("fsdp"),
            P("fsdp"),
            P("fsdp", None),
            P(),
            P("fsdp", "seq"),
            P("fsdp", "seq"),
            P("seq", "fsdp"),
            P(),
            P("fsdp", "seq"),
            P("fsdp", None, "seq", None),
            P("fsdp", None, "seq", None),
            P("fsdp", None, "seq", None),
            P("fsdp", None),
            P("fsdp", None, "seq", None),
        ),
        out_specs=(
            P("fsdp"),
            P("fsdp", None, None, "seq"),
            P("fsdp", None, None, "seq"),
            P("fsdp", None, None, "seq"),
        ),
        check_vma=False,
    )
```
